512 devices in a mesh: stream: 64 (over x, z, core), azi: 8 (over y).
Axes of the slice: x: 4, y: 8, z: 8, core: 2. Of those that a mesh axis runs over, the one named last changes fastest.
Arguments:
- right_sides: float32 [1024, 320, 128], P(('stream', 'azi')), may hold values from -2.5 to 2.5
- inverse_blocks: float32 [1024, 320, 320], P(('stream', 'azi')), may hold values from -1 to 2
- lower_faces: float32 [1024, 80, 240], P(('stream', 'azi')), may hold values from -2 to 1
- upper_faces: float32 [1024, 80, 240], P(('stream', 'azi')), may hold values from -2 to 1
- upwind_index: int32 [1024, 3], P(('stream', 'azi')), may hold values from 0 to 2, as said below
- wake_rows: float32 [32768, 320], P(('stream', 'azi')), may hold values from -2 to 2
- wake_target: int32 [32768], P(('stream', 'azi')), may hold values from 0 to 15
Outputs:
- solution: float32 [1024, 320, 128], P(('stream', 'azi'))
The draws below stay inside these ranges and needn't reach their ends.
Inputs may be any that keep to these rules, and one draw needn't show every extreme that they name: `upwind_index`: row n = (k * 8 + a) * 2 + e: every entry is an element place below e, or exactly 2, which names the last element of the previous slab in the same sector; the three entries of every row with e = 0 are 2.
All inputs are finite; a program needn't handle non-finite values.
Results may differ from the reference program's by a relative error of at most 0.0003.
Values sent between devices are 32-bit elements; how exact they have to be, the bound alone decides.
No kernel may reach another device: no remote copies, remote signals or barrier semaphores. Data moves between devices by JAX's collectives and lax.ppermute only.
A program may use at most 64 MiB of HBM per device.

```python
import math
import jax
import jax.numpy as jnp
from jax import lax

FIELDS = 5
POINTS = 4
COLUMNS = 128
SECTOR_ELEMENTS = 2
PARTICLES = 64
BLOCK = 320
TRACE = 80
ELEMENTS = 1024
WAKE_ROWS = 32768
N_STREAM = 64
N_AZI = 8
DEVICES = 512


def channel_rates(key, lowest, highest):
    spread = jax.random.uniform(key, (TRACE,), jnp.float32)
    return jnp.exp(math.log(lowest) + spread * (math.log(highest) - math.log(lowest)))


def coupling_draw(key, damping_rates, main_scale, side_scale):
    multiplier_key, gust_key, layer_depth_key, jitter_key = jax.random.split(key, 4)
    device_factor = jnp.exp(jax.random.uniform(multiplier_key, (DEVICES, TRACE), jnp.float32, math.log(0.5), math.log(2.0)))
    element_multiplier = jnp.repeat(device_factor, SECTOR_ELEMENTS, axis=0)
    gust_strike = jax.random.bernoulli(gust_key, 0.0625, (DEVICES,))
    gust_depth = jax.random.uniform(layer_depth_key, (DEVICES,), jnp.float32, 0.5, 0.8)
    final_position = jnp.arange(ELEMENTS, dtype=jnp.int32) % SECTOR_ELEMENTS == SECTOR_ELEMENTS - 1
    gust_factor = jnp.where(final_position & jnp.repeat(gust_strike, SECTOR_ELEMENTS), jnp.repeat(gust_depth, SECTOR_ELEMENTS), 1.0)
    channel_amplitude = jnp.exp(-damping_rates[None, :] * element_multiplier) * gust_factor[:, None]
    noise_part = jnp.clip(jax.random.normal(jitter_key, (ELEMENTS, TRACE, 3 * TRACE), jnp.float32), -4.0, 4.0)
    row_index = jnp.arange(TRACE, dtype=jnp.int32)[:, None]
    column = jnp.arange(3 * TRACE, dtype=jnp.int32)[None, :]
    scales = jnp.where(column < TRACE, main_scale, side_scale) / math.sqrt(TRACE)
    diagonal = (row_index == column).astype(jnp.float32)
    return noise_part * scales[None, :, :] - diagonal[None, :, :] * channel_amplitude[:, :, None]


def draw_lower_faces(key, part):
    damping_rates = channel_rates(key, 0.0005, 0.1)
    key = jax.random.fold_in(key, 5)
    return coupling_draw(key, damping_rates, 0.1, 0.15)


def draw_upper_faces(key, part):
    damping_rates = channel_rates(key, 0.0005, 0.1)
    key = jax.random.fold_in(key, 6)
    return coupling_draw(key, damping_rates, 0.1, 0.15)


def draw_inverse_blocks(key, part):
    key = jax.random.fold_in(key, 21)
    diag_key, ahead_key, behind_key, jitter_key = jax.random.split(key, 4)
    row_index = jnp.arange(BLOCK, dtype=jnp.int32)[:, None]
    column = jnp.arange(BLOCK, dtype=jnp.int32)[None, :]
    cube_size = POINTS * POINTS * POINTS
    plane_size = POINTS * POINTS
    same_line = (row_index // cube_size == column // cube_size) & (row_index % plane_size == column % plane_size)
    row_level = row_index // plane_size % POINTS
    column_level = column // plane_size % POINTS
    ahead_mask = same_line & (row_level == POINTS - 1) & (column_level == 0)
    behind_mask = same_line & (row_level == 0) & (column_level == POINTS - 1)
    diagonal = row_index == column
    self_gain = jax.random.uniform(diag_key, (ELEMENTS, BLOCK, 1), jnp.float32, 0.5, 1.0)
    ahead_gain = jax.random.uniform(ahead_key, (ELEMENTS, BLOCK, 1), jnp.float32, 0.99, 1.0)
    behind_gain = jax.random.uniform(behind_key, (ELEMENTS, BLOCK, 1), jnp.float32, 0.99, 1.0)
    noise_part = jnp.clip(jax.random.normal(jitter_key, (ELEMENTS, BLOCK, BLOCK), jnp.float32), -4.0, 4.0) * (0.12 / math.sqrt(BLOCK))
    structure = jnp.where(diagonal[None], self_gain, 0.0) + jnp.where(ahead_mask[None], ahead_gain, 0.0) + jnp.where(behind_mask[None], behind_gain, 0.0)
    return noise_part + structure


def draw_upwind_index(key, part):
    key = jax.random.fold_in(key, 11)
    first_key, second_key = jax.random.split(key)
    position = (jnp.arange(ELEMENTS, dtype=jnp.int32) % SECTOR_ELEMENTS)[:, None]
    randoms = jax.random.randint(first_key, (ELEMENTS, 3), 0, 1 << 20)
    crossing = jax.random.randint(second_key, (ELEMENTS, 3), 0, 4)
    earlier = randoms % jnp.maximum(position, 1)
    return jnp.where((crossing == 0) | (position == 0), SECTOR_ELEMENTS, earlier).astype(jnp.int32)


def set_ends(drawn, stream_key, least, largest):
    extent = drawn.shape
    spot = [jax.random.randint(jax.random.fold_in(stream_key, axis), (), 0, extent[axis]) for axis in range(len(extent))]
    drawn = drawn.at[tuple(spot)].set(least)
    longest = extent.index(max(extent))
    spot[longest] = (spot[longest] + 1) % extent[longest]
    return drawn.at[tuple(spot)].set(largest)


def block_levels(stream_key, extent, cuts, least, top_value):
    factor_of, own = 1.0, jax.random.fold_in(stream_key, 6)
    for dim, blocks in cuts:
        steps = jnp.exp(jax.random.uniform(jax.random.fold_in(own, dim), (blocks,), jnp.float32, least / len(cuts), top_value / len(cuts)))
        factor_of = factor_of * jnp.repeat(steps, extent[dim] // blocks).reshape([-1 if axis == dim else 1 for axis in range(len(extent))])
    return factor_of


def gaussian(stream_key, dims, width, bound, shards=(), held_as=jnp.bfloat16):
    entries = jax.random.normal(stream_key, dims, jnp.float32) * width
    if len(shards) > 0:
        entries = block_levels(stream_key, dims, shards, -0.22, 0.18) * entries
    return jnp.clip(entries, min=-bound, max=bound).astype(held_as)


def setup_inputs(seed: int = 0) -> dict:
    key_list = jax.random.split(jax.random.key(seed), 8)
    right_sides = gaussian(key_list[0], (ELEMENTS, BLOCK, COLUMNS), 0.4, 2.5, ((0, 512),), jnp.float32)
    inverse_blocks = draw_inverse_blocks(jax.random.fold_in(key_list[7], 71), 0)
    lower_faces = draw_lower_faces(jax.random.fold_in(key_list[7], 71), 0)
    upper_faces = draw_upper_faces(jax.random.fold_in(key_list[7], 71), 0)
    upwind_index = draw_upwind_index(jax.random.fold_in(key_list[7], 71), 0)
    wake_rows = gaussian(key_list[5], (WAKE_ROWS, BLOCK), 0.15, 2.0, ((0, 512),), jnp.float32)
    wake_target = set_ends(jax.random.randint(key_list[6], (WAKE_ROWS,), 0, N_AZI * SECTOR_ELEMENTS), jax.random.fold_in(key_list[6], 1), 0, (N_AZI * SECTOR_ELEMENTS) - 1).astype(jnp.int32)
    return {"right_sides": right_sides, "inverse_blocks": inverse_blocks, "lower_faces": lower_faces, "upper_faces": upper_faces, "upwind_index": upwind_index, "wake_rows": wake_rows, "wake_target": wake_target}


PRECISE = lax.Precision.HIGHEST


def matmul(operand_a, operand_b):
    return jnp.dot(operand_a, operand_b, precision=PRECISE, preferred_element_type=jnp.float32)


def take_face(values, face_slot):
    cubed = values.reshape(FIELDS, POINTS, POINTS, POINTS, values.shape[-1])
    side_index = 0 if face_slot % 2 == 0 else POINTS - 1
    face_plane = lax.index_in_dim(cubed, side_index, face_slot // 2 + 1, keepdims=False)
    return face_plane.reshape(FIELDS * POINTS * POINTS, values.shape[-1])


def put_face(values, face_rows, face_slot):
    cubed = values.reshape(FIELDS, POINTS, POINTS, POINTS, values.shape[-1])
    side_index = 0 if face_slot % 2 == 0 else POINTS - 1
    position = [slice(None)] * 5
    position[face_slot // 2 + 1] = side_index
    face_plane = face_rows.reshape(FIELDS, POINTS, POINTS, values.shape[-1])
    return cubed.at[tuple(position)].add(face_plane).reshape(values.shape)


def lower_sweep(source, inverse, lower, upwind, inflow):
    local_count = source.shape[0]
    trace_rows = inflow.shape[0]
    solved = []
    for element in range(local_count):
        summed = source[element]
        for face_no in range(3):
            options = [take_face(solved[earlier], 2 * face_no + 1) for earlier in range(element)]
            stacked = jnp.stack(options + [inflow])
            chosen = jnp.minimum(upwind[element, face_no], element)
            traced = lax.dynamic_index_in_dim(stacked, chosen, 0, keepdims=False)
            coupling = lower[element, :, face_no * trace_rows:(face_no + 1) * trace_rows]
            summed = put_face(summed, -matmul(coupling, traced), 2 * face_no)
        solved.append(matmul(inverse[element], summed))
    return jnp.stack(solved), take_face(solved[-1], 1)


def upper_sweep(base, inverse, upper, upwind, incoming):
    local_count = base.shape[0]
    trace_rows = incoming.shape[0]
    results = [None] * local_count
    pending = []
    outgoing = jnp.zeros_like(incoming)
    for element in reversed(range(local_count)):
        summed = jnp.zeros_like(base[element])
        for later_elem, face_no, coupled in pending:
            matches = (upwind[later_elem, face_no] == element).astype(jnp.float32)
            summed = put_face(summed, matches * coupled, 2 * face_no + 1)
        if element == local_count - 1:
            summed = put_face(summed, incoming, 1)
        solved = base[element] - matmul(inverse[element], summed)
        results[element] = solved
        for face_no in range(3):
            coupling = upper[element, :, face_no * trace_rows:(face_no + 1) * trace_rows]
            coupled = matmul(coupling, take_face(solved, 2 * face_no))
            pending.append((element, face_no, coupled))
            crossing = (upwind[element, face_no] == local_count).astype(jnp.float32)
            outgoing = outgoing + crossing * coupled
    return jnp.stack(results), outgoing


def by_slab(values):
    return values.reshape((N_STREAM, N_AZI, SECTOR_ELEMENTS) + values.shape[1:])


def reference(right_sides, inverse_blocks, lower_faces, upper_faces, upwind_index, wake_rows, wake_target):
    owners = jnp.arange(WAKE_ROWS, dtype=jnp.int32) // (PARTICLES * N_AZI)
    targets = (owners * (N_AZI * SECTOR_ELEMENTS) + wake_target).astype(jnp.int32)
    wake = jax.ops.segment_sum(wake_rows, targets, num_segments=ELEMENTS)
    source = right_sides + wake[:, :, None]
    forward_map = jax.vmap(lower_sweep)
    backward_map = jax.vmap(upper_sweep)

    def forward_step(inflow, pieces):
        solved, outflow = forward_map(pieces[0], pieces[1], pieces[2], pieces[3], inflow)
        return outflow, solved

    def backward_step(incoming, pieces):
        solved, outflow = backward_map(pieces[0], pieces[1], pieces[2], pieces[3], incoming)
        return outflow, solved

    initial = jnp.zeros((N_AZI, TRACE, COLUMNS), jnp.float32)
    slab_inverse = by_slab(inverse_blocks)
    slab_upwind = by_slab(upwind_index)
    _, lowered = lax.scan(forward_step, initial, (by_slab(source), slab_inverse, by_slab(lower_faces), slab_upwind))
    _, solution = lax.scan(backward_step, initial, (lowered, slab_inverse, by_slab(upper_faces), slab_upwind), reverse=True)
    return solution.reshape(right_sides.shape)
```

```python
import functools

import jax
import jax.numpy as jnp
from jax import lax
from jax.experimental import pallas as pl
from jax.experimental.pallas import tpu as pltpu
from jax.sharding import PartitionSpec as P

TRACE = 80
BLOCK = 320
COLUMNS = 128
PLANE = 16
CUBE = 64
HALF = 128
F32 = jnp.float32
BF16 = jnp.bfloat16
VMEM = pl.BlockSpec(memory_space=pltpu.VMEM)
SMEM = pl.BlockSpec(memory_space=pltpu.SMEM)


def split(value):
    high = value.astype(BF16)
    return high, (value - high.astype(F32)).astype(BF16)


def dot(left, right):
    return jnp.dot(left, right, preferred_element_type=F32)


def product(left, right):
    return dot(left[0], right[0]) + (dot(left[0], right[1]) + dot(left[1], right[0]))


def select_rows(onehot, value):
    return dot(onehot, value[0]), dot(onehot, value[1])


def wake_kernel(target_ref, rows_ref, out_ref):
    ids = lax.broadcasted_iota(jnp.int32, (out_ref.shape[0], target_ref.shape[1]), 0)
    onehot = jnp.where(ids == target_ref[...], 1.0, 0.0).astype(BF16)
    high, low = split(rows_ref[...])
    out_ref[...] = dot(onehot, high) + dot(onehot, low)


def face_block(ref, element, face):
    return ref[element, :, face * TRACE : (face + 1) * TRACE]


def rows_of(slots, transposed):
    shape = (1, 3 * TRACE) if transposed else (3 * TRACE, 1)
    place = lax.broadcasted_iota(jnp.int32, shape, 1 if transposed else 0)
    which = jnp.where(place >= 2 * TRACE, 2, jnp.where(place >= TRACE, 1, 0))
    trace = place - which * TRACE
    field, upper, lower = trace >> 4, (trace >> 2) & 3, trace & 3
    side = 3 * (slots[0] % 2)
    row = jnp.where(
        which == 0,
        side * 16 + upper * 4 + lower,
        jnp.where(which == 1, upper * 16 + side * 4 + lower, upper * 16 + lower * 4 + side),
    )
    row = field * CUBE + row
    whole = (BLOCK, 3 * TRACE) if transposed else (3 * TRACE, BLOCK)
    rows = lax.broadcasted_iota(jnp.int32, whole, 0 if transposed else 1)
    return jnp.where(rows == row, 1.0, 0.0).astype(BF16)


def last_plane(value):
    return jnp.concatenate(
        [value[at + CUBE - PLANE : at + CUBE] for at in range(0, BLOCK, CUBE)], axis=0
    )


def pack(first, second, third, fourth):
    lead = TRACE
    spare = HALF - lead
    mid = third[:, :HALF]
    return jnp.concatenate(
        [
            first[:, :lead],
            mid[:, :spare],
            first[:, HALF:],
            fourth[:, :lead],
            mid[:, spare:lead],
            jnp.zeros((TRACE, 2 * spare - lead), F32),
            third[:, HALF:],
        ],
        axis=1,
    )


def unpack(value):
    lead = TRACE
    spare = HALF - lead
    zeros = jnp.zeros((TRACE, spare), F32)
    forward = value[:, : 2 * HALF]
    mixed = jnp.concatenate(
        [
            value[:, lead:HALF],
            value[:, 2 * HALF + lead : 2 * HALF + lead + (lead - spare)],
            zeros,
            value[:, 3 * HALF :],
        ],
        axis=1,
    )
    return forward, mixed, value[:, 2 * HALF : 2 * HALF + lead]


def local_kernel(upwind_ref, rhs_ref, inv_ref, low_ref, up_ref, wake_ref, total_ref, keep_ref):
    put_even = rows_of((0, 2, 4), True)
    take_even = rows_of((0, 2, 4), False)
    put_odd = rows_of((1, 3, 5), True)
    take_odd = rows_of((1, 3, 5), False)
    ones = jnp.ones((wake_ref.shape[1], COLUMNS), BF16)

    def source(element):
        high, low = split(wake_ref[element])
        dims = (((0,), (0,)), ((), ()))
        wake = lax.dot_general(high, ones, dims, preferred_element_type=F32)
        wake += lax.dot_general(low, ones, dims, preferred_element_type=F32)
        return rhs_ref[element] + wake

    inverse = [split(inv_ref[0]), split(inv_ref[1])]
    crosses = [upwind_ref[1, face] == 2 for face in range(3)]
    zeros_low = jnp.zeros((TRACE, HALF - TRACE), F32)
    eye = jnp.where(
        lax.broadcasted_iota(jnp.int32, (TRACE, 2 * HALF), 0)
        == lax.broadcasted_iota(jnp.int32, (TRACE, 2 * HALF), 1),
        1.0,
        0.0,
    )

    stacked = jnp.concatenate([face_block(low_ref, 0, face) for face in range(3)], axis=0)
    stacked = jnp.concatenate([stacked, jnp.zeros((3 * TRACE, HALF - TRACE), F32)], axis=1)
    spread = sum(select_rows(put_even, split(stacked)))
    first = product(inverse[0], split(jnp.concatenate([-spread, source(0)], axis=1)))

    traced = select_rows(take_odd, split(first))
    coupled = []
    for face in range(3):
        at = slice(face * TRACE, (face + 1) * TRACE)
        high = jnp.where(crosses[face], eye, traced[0][at]).astype(BF16)
        lows = jnp.where(crosses[face], 0.0, traced[1][at]).astype(BF16)
        coupled.append(product(split(face_block(low_ref, 1, face)), (high, lows)))
    spread = sum(select_rows(put_even, split(jnp.concatenate(coupled, axis=0))))
    base = jnp.concatenate([jnp.zeros((BLOCK, HALF), F32), source(1)], axis=1)
    second = product(inverse[1], split(base - spread))
    forward = last_plane(second)

    side = put_odd[:, :HALF]
    returned = -(dot(inverse[1][0], side) + dot(inverse[1][1], side))
    lane = lax.broadcasted_iota(jnp.int32, (BLOCK, HALF), 1)
    returned = jnp.where(lane < TRACE, returned, 0.0)
    second = jnp.concatenate([second, returned], axis=1)
    keep_ref[1] = second
    traced = select_rows(take_even, split(second))
    outgoing = jnp.zeros((TRACE, 3 * HALF), F32)
    coupled = []
    for face in range(3):
        at = slice(face * TRACE, (face + 1) * TRACE)
        pair = (traced[0][at].astype(BF16), traced[1][at].astype(BF16))
        value = product(split(face_block(up_ref, 1, face)), pair)
        outgoing += jnp.where(crosses[face], value, 0.0)
        coupled.append(jnp.where(crosses[face], 0.0, value))
    spread = sum(select_rows(put_odd, split(jnp.concatenate(coupled, axis=0))))
    first = jnp.concatenate([first, jnp.zeros((BLOCK, HALF), F32)], axis=1)
    first = first - product(inverse[0], split(spread))
    keep_ref[0] = first
    traced = select_rows(take_even, split(first))
    pair = (traced[0].astype(BF16), traced[1].astype(BF16))
    outgoing += product(split(up_ref[0]), pair)
    total_ref[...] = pack(forward, None, outgoing[:, : 2 * HALF], outgoing[:, 2 * HALF :])


def is_upper(level):
    return (lax.axis_index("stream") >> level) & 1


def ordered(level, mine_ref, other_ref):
    upper = is_upper(level) == 1
    mine, other = mine_ref[...], other_ref[...]
    return unpack(jnp.where(upper, other, mine)), unpack(jnp.where(upper, mine, other))


def combine_kernel(level, mine_ref, other_ref, total_ref, cross_ref):
    (forward1, mixed1, back1), (forward2, mixed2, back2) = ordered(level, mine_ref, other_ref)
    lane = lax.broadcasted_iota(jnp.int32, (TRACE, 2 * HALF), 1)
    columns = lane >= HALF
    clean = columns | (lane < TRACE)
    forward_pair = split(jnp.where(clean, forward1, 0.0))
    cross = product(split(mixed2[:, :TRACE]), forward_pair) + jnp.where(columns, mixed2, 0.0)
    forward = product(split(forward2[:, :TRACE]), forward_pair)
    forward = forward + jnp.where(columns, forward2, 0.0)
    back_pair = split(back1)
    mixed = mixed1 + product(back_pair, split(cross))
    back = product(back_pair, split(back2))
    total_ref[...] = pack(forward, None, mixed, back)
    cross_ref[...] = cross


def track_first_kernel(level, mine_ref, other_ref, cross_ref, state_ref):
    (forward1, _, _), (_, _, back2) = ordered(level, mine_ref, other_ref)
    upper = is_upper(level) == 1
    lane = lax.broadcasted_iota(jnp.int32, (TRACE, 2 * HALF), 1)
    row = lax.broadcasted_iota(jnp.int32, (TRACE, 2 * HALF), 0)
    eye = jnp.where(lane == row, 1.0, 0.0)
    clean = (lane >= HALF) | (lane < TRACE)
    state_ref[:, : 2 * HALF] = jnp.where(upper, jnp.where(clean, forward1, 0.0), eye)
    state_ref[:, 2 * HALF : 4 * HALF] = jnp.where(upper, 0.0, cross_ref[...])
    back2 = jnp.concatenate([back2, jnp.zeros((TRACE, HALF - TRACE), F32)], axis=1)
    state_ref[:, 4 * HALF :] = jnp.where(upper, eye[:, :HALF], back2)


def track_kernel(level, mine_ref, other_ref, cross_ref, old_ref, state_ref):
    lane = lax.broadcasted_iota(jnp.int32, (TRACE, 2 * HALF), 1)
    columns = lane >= HALF

    @pl.when(is_upper(level) == 1)
    def _():
        forward1 = jnp.where(columns | (lane < TRACE), other_ref[:, : 2 * HALF], 0.0)
        pair = split(forward1)
        here = old_ref[:, : 2 * HALF]
        back = old_ref[:, 2 * HALF : 4 * HALF]
        state_ref[:, : 2 * HALF] = product(split(here[:, :TRACE]), pair) + jnp.where(columns, here, 0.0)
        state_ref[:, 2 * HALF : 4 * HALF] = product(split(back[:, :TRACE]), pair) + jnp.where(columns, back, 0.0)
        state_ref[:, 4 * HALF :] = old_ref[:, 4 * HALF :]

    @pl.when(is_upper(level) == 0)
    def _():
        gain = split(old_ref[:, 4 * HALF : 4 * HALF + TRACE])
        back2 = jnp.where(lane[:, :HALF] < TRACE, other_ref[:, 2 * HALF : 3 * HALF], 0.0)
        state_ref[:, : 2 * HALF] = old_ref[:, : 2 * HALF]
        state_ref[:, 2 * HALF : 4 * HALF] = old_ref[:, 2 * HALF : 4 * HALF] + product(gain, split(cross_ref[...]))
        state_ref[:, 4 * HALF :] = product(gain, split(back2))


def last_kernel(level, mine_ref, other_ref, old_ref, keep_ref, out_ref, ends_ref):
    @pl.when(is_upper(level) == 1)
    def _():
        inflow = split(other_ref[:, HALF : 2 * HALF])
        ends_ref[0] = old_ref[:, HALF : 2 * HALF] + product(split(old_ref[:, :TRACE]), inflow)
        ends_ref[1] = old_ref[:, 3 * HALF : 4 * HALF] + product(split(old_ref[:, 2 * HALF : 2 * HALF + TRACE]), inflow)

    @pl.when(is_upper(level) == 0)
    def _():
        outflow = split(mine_ref[:, HALF : 2 * HALF])
        value = other_ref[:, HALF : 2 * HALF] + product(split(other_ref[:, :TRACE]), outflow)
        gain = split(old_ref[:, 4 * HALF : 4 * HALF + TRACE])
        ends_ref[0] = old_ref[:, HALF : 2 * HALF]
        ends_ref[1] = old_ref[:, 3 * HALF : 4 * HALF] + product(gain, split(value))

    inflow = split(ends_ref[0])
    incoming = split(ends_ref[1])
    for element in range(2):
        known = keep_ref[element]
        out_ref[element] = (
            known[:, HALF : 2 * HALF]
            + product(split(known[:, :TRACE]), inflow)
            + product(split(known[:, 2 * HALF : 2 * HALF + TRACE]), incoming)
        )


def call(kernel, shapes, operands, flops, scalars=0, scratch=()):
    moved = 4 * sum(v.size for v in operands) + 4 * sum(s.size for s in shapes)
    single = len(shapes) == 1
    return pl.pallas_call(
        kernel,
        out_shape=shapes[0] if single else shapes,
        in_specs=[SMEM] * scalars + [VMEM] * (len(operands) - scalars),
        out_specs=VMEM if single else [VMEM] * len(shapes),
        scratch_shapes=list(scratch),
        compiler_params=pltpu.CompilerParams(vmem_limit_bytes=40 * 1024 * 1024),
        cost_estimate=pl.CostEstimate(flops=flops, bytes_accessed=moved, transcendentals=0),
    )(*operands)


def shape(*dims):
    return jax.ShapeDtypeStruct(dims, F32)


PARTNERS = ((0, 0, 1), (0, 1, 0), (0, 2, 0), (0, 6, 0), (1, 0, 0), (3, 0, 0))


def exchange(value, level):
    across, along, core = PARTNERS[level]
    mask = (across * 8 + along) * 2 + core
    count = lax.axis_size("stream")
    return lax.ppermute(value, "stream", [(k, k ^ mask) for k in range(count)])


def shards(rhs, inverse, lower, upper, upwind, rows, target):
    groups = lax.axis_size("azi")
    local = rhs.shape[0]
    partial = call(wake_kernel, [shape(groups * local, BLOCK)], [target.reshape(1, -1), rows], 10**6)
    parts = lax.all_to_all(partial.reshape(groups, local, BLOCK), "azi", 0, 0)
    parts = jnp.swapaxes(parts, 0, 1)
    total, keep = call(
        local_kernel,
        [shape(TRACE, 4 * HALF), shape(local, BLOCK, 3 * HALF)],
        [upwind, rhs, inverse, lower, upper, parts],
        2 * 10**9,
        scalars=1,
    )
    state = None
    for level in range(5):
        other = exchange(total, level)
        merged, cross = call(
            functools.partial(combine_kernel, level),
            [shape(TRACE, 4 * HALF), shape(TRACE, 2 * HALF)],
            [total, other],
            2 * 10**7,
        )
        if level == 0:
            state = call(
                functools.partial(track_first_kernel, level),
                [shape(TRACE, 5 * HALF)],
                [total, other, cross],
                10**6,
            )
        else:
            state = call(
                functools.partial(track_kernel, level),
                [shape(TRACE, 5 * HALF)],
                [total, other, cross, state],
                10**7,
            )
        total = merged
    top = (lax.axis_index("stream") >> 5) & 1
    forward, mixed, _ = unpack(total)
    other = exchange(jnp.where(top == 1, mixed, forward), 5)
    return call(
        functools.partial(last_kernel, 5),
        [shape(local, BLOCK, COLUMNS)],
        [total, other, state, keep],
        10**8,
        scratch=[pltpu.VMEM((2, TRACE, COLUMNS), F32)],
    )


def solution(mesh):
    both = ("stream", "azi")
    return jax.shard_map(
        shards,
        mesh=mesh,
        in_specs=(
            P(both, None, None),
            P(both, None, None),
            P(both, None, None),
            P(both, None, None),
            P(both, None),
            P(both, None),
            P(both),
        ),
        out_specs=P(both, None, None),
        check_vma=False,
    )
```

```python
import functools

import jax
import jax.numpy as jnp
from jax import lax
from jax.experimental import pallas as pl
from jax.experimental.pallas import tpu as pltpu
from jax.sharding import PartitionSpec as P

TRACE = 80
BLOCK = 320
COLUMNS = 128
PLANE = 16
CUBE = 64
HALF = 128
F32 = jnp.float32
BF16 = jnp.bfloat16
VMEM = pl.BlockSpec(memory_space=pltpu.VMEM)
SMEM = pl.BlockSpec(memory_space=pltpu.SMEM)
HBM = pl.BlockSpec(memory_space=pltpu.HBM)


def split(value):
    high = value.astype(BF16)
    return high, (value - high.astype(F32)).astype(BF16)


def dot(left, right):
    return jnp.dot(left, right, preferred_element_type=F32)


def product(left, right):
    return dot(left[0], right[0]) + (dot(left[0], right[1]) + dot(left[1], right[0]))


def select_rows(onehot, value):
    return dot(onehot, value[0]), dot(onehot, value[1])


def fetch(sources, buffers, sems):
    copies = [pltpu.make_async_copy(a, b, sems.at[i]) for i, (a, b) in enumerate(zip(sources, buffers))]
    for copy in copies:
        copy.start()
    return copies


def wake_kernel(target_hbm, rows_hbm, out_ref, target_ref, rows_ref, sems):
    for copy in fetch((target_hbm, rows_hbm), (target_ref, rows_ref), sems):
        copy.wait()
    ids = lax.broadcasted_iota(jnp.int32, (out_ref.shape[0], target_ref.shape[1]), 0)
    onehot = jnp.where(ids == target_ref[...], 1.0, 0.0).astype(BF16)
    high, low = split(rows_ref[...])
    out_ref[...] = dot(onehot, high) + dot(onehot, low)


def face_block(ref, element, face):
    return ref[element, :, face * TRACE : (face + 1) * TRACE]


def rows_of(slots, transposed):
    shape = (1, 3 * TRACE) if transposed else (3 * TRACE, 1)
    place = lax.broadcasted_iota(jnp.int32, shape, 1 if transposed else 0)
    which = jnp.where(place >= 2 * TRACE, 2, jnp.where(place >= TRACE, 1, 0))
    trace = place - which * TRACE
    field, upper, lower = trace >> 4, (trace >> 2) & 3, trace & 3
    side = 3 * (slots[0] % 2)
    row = jnp.where(
        which == 0,
        side * 16 + upper * 4 + lower,
        jnp.where(which == 1, upper * 16 + side * 4 + lower, upper * 16 + lower * 4 + side),
    )
    row = field * CUBE + row
    whole = (BLOCK, 3 * TRACE) if transposed else (3 * TRACE, BLOCK)
    rows = lax.broadcasted_iota(jnp.int32, whole, 0 if transposed else 1)
    return jnp.where(rows == row, 1.0, 0.0).astype(BF16)


def last_plane(value):
    return jnp.concatenate(
        [value[at + CUBE - PLANE : at + CUBE] for at in range(0, BLOCK, CUBE)], axis=0
    )


def pack(first, second, third, fourth):
    lead = TRACE
    spare = HALF - lead
    mid = third[:, :HALF]
    return jnp.concatenate(
        [
            first[:, :lead],
            mid[:, :spare],
            first[:, HALF:],
            fourth[:, :lead],
            mid[:, spare:lead],
            jnp.zeros((TRACE, 2 * spare - lead), F32),
            third[:, HALF:],
        ],
        axis=1,
    )


def unpack(value):
    lead = TRACE
    spare = HALF - lead
    zeros = jnp.zeros((TRACE, spare), F32)
    forward = value[:, : 2 * HALF]
    mixed = jnp.concatenate(
        [
            value[:, lead:HALF],
            value[:, 2 * HALF + lead : 2 * HALF + lead + (lead - spare)],
            zeros,
            value[:, 3 * HALF :],
        ],
        axis=1,
    )
    return forward, mixed, value[:, 2 * HALF : 2 * HALF + lead]


def local_kernel(
    upwind_ref,
    wake_ref,
    low_hbm,
    inv_hbm,
    rhs_hbm,
    up_hbm,
    total_ref,
    keep_ref,
    low_ref,
    first_inv_ref,
    second_inv_ref,
    rhs_ref,
    up_ref,
    sems,
):
    copies = fetch(
        (low_hbm, rhs_hbm, inv_hbm.at[0], inv_hbm.at[1], up_hbm),
        (low_ref, rhs_ref, first_inv_ref, second_inv_ref, up_ref),
        sems,
    )
    put_even = rows_of((0, 2, 4), True)
    take_even = rows_of((0, 2, 4), False)
    put_odd = rows_of((1, 3, 5), True)
    take_odd = rows_of((1, 3, 5), False)
    ones = jnp.ones((wake_ref.shape[1], COLUMNS), BF16)

    def source(element):
        high, low = split(wake_ref[element])
        dims = (((0,), (0,)), ((), ()))
        wake = lax.dot_general(high, ones, dims, preferred_element_type=F32)
        wake += lax.dot_general(low, ones, dims, preferred_element_type=F32)
        return rhs_ref[element] + wake

    crosses = [upwind_ref[1, face] == 2 for face in range(3)]
    zeros_low = jnp.zeros((TRACE, HALF - TRACE), F32)
    eye = jnp.where(
        lax.broadcasted_iota(jnp.int32, (TRACE, 2 * HALF), 0)
        == lax.broadcasted_iota(jnp.int32, (TRACE, 2 * HALF), 1),
        1.0,
        0.0,
    )

    copies[0].wait()
    stacked = jnp.concatenate([face_block(low_ref, 0, face) for face in range(3)], axis=0)
    stacked = jnp.concatenate([stacked, jnp.zeros((3 * TRACE, HALF - TRACE), F32)], axis=1)
    spread = sum(select_rows(put_even, split(stacked)))
    copies[1].wait()
    copies[2].wait()
    inverse = split(first_inv_ref[...])
    first = product(inverse, split(jnp.concatenate([-spread, source(0)], axis=1)))

    traced = select_rows(take_odd, split(first))
    coupled = []
    for face in range(3):
        at = slice(face * TRACE, (face + 1) * TRACE)
        high = jnp.where(crosses[face], eye, traced[0][at]).astype(BF16)
        lows = jnp.where(crosses[face], 0.0, traced[1][at]).astype(BF16)
        coupled.append(product(split(face_block(low_ref, 1, face)), (high, lows)))
    spread = sum(select_rows(put_even, split(jnp.concatenate(coupled, axis=0))))
    base = jnp.concatenate([jnp.zeros((BLOCK, HALF), F32), source(1)], axis=1)
    copies[3].wait()
    later_inverse = split(second_inv_ref[...])
    second = product(later_inverse, split(base - spread))
    forward = last_plane(second)

    side = put_odd[:, :HALF]
    returned = -(dot(later_inverse[0], side) + dot(later_inverse[1], side))
    lane = lax.broadcasted_iota(jnp.int32, (BLOCK, HALF), 1)
    returned = jnp.where(lane < TRACE, returned, 0.0)
    second = jnp.concatenate([second, returned], axis=1)
    keep_ref[1] = second
    traced = select_rows(take_even, split(second))
    copies[4].wait()
    outgoing = jnp.zeros((TRACE, 3 * HALF), F32)
    coupled = []
    for face in range(3):
        at = slice(face * TRACE, (face + 1) * TRACE)
        pair = (traced[0][at].astype(BF16), traced[1][at].astype(BF16))
        value = product(split(face_block(up_ref, 1, face)), pair)
        outgoing += jnp.where(crosses[face], value, 0.0)
        coupled.append(jnp.where(crosses[face], 0.0, value))
    spread = sum(select_rows(put_odd, split(jnp.concatenate(coupled, axis=0))))
    first = jnp.concatenate([first, jnp.zeros((BLOCK, HALF), F32)], axis=1)
    first = first - product(inverse, split(spread))
    keep_ref[0] = first
    traced = select_rows(take_even, split(first))
    pair = (traced[0].astype(BF16), traced[1].astype(BF16))
    outgoing += product(split(up_ref[0]), pair)
    total_ref[...] = pack(forward, None, outgoing[:, : 2 * HALF], outgoing[:, 2 * HALF :])


def is_upper(level):
    return (lax.axis_index("stream") >> level) & 1


def combine_kernel(last, pair_ref, total_ref, cross_ref):
    forward1, mixed1, back1 = unpack(pair_ref[0])
    forward2, mixed2, back2 = unpack(pair_ref[1])
    lane = lax.broadcasted_iota(jnp.int32, (TRACE, 2 * HALF), 1)
    columns = lane >= HALF
    clean = columns | (lane < TRACE)
    forward_pair = split(jnp.where(clean, forward1, 0.0))
    cross = product(split(mixed2[:, :TRACE]), forward_pair) + jnp.where(columns, mixed2, 0.0)
    forward = product(split(forward2[:, :TRACE]), forward_pair)
    forward = forward + jnp.where(columns, forward2, 0.0)
    back_pair = split(back1)
    mixed = mixed1 + product(back_pair, split(cross))
    if last:
        total_ref[...] = jnp.where(is_upper(last) == 1, mixed, forward)
    else:
        total_ref[...] = pack(forward, None, mixed, product(back_pair, split(back2)))
    cross_ref[...] = cross


def track_first_kernel(level, pair_ref, cross_ref, state_ref):
    upper = is_upper(level) == 1
    lane = lax.broadcasted_iota(jnp.int32, (TRACE, 2 * HALF), 1)
    row = lax.broadcasted_iota(jnp.int32, (TRACE, 2 * HALF), 0)
    eye = jnp.where(lane == row, 1.0, 0.0)
    forward1 = jnp.where((lane >= HALF) | (lane < TRACE), pair_ref[0, :, : 2 * HALF], 0.0)
    back2 = jnp.where(lane[:, :HALF] < TRACE, pair_ref[1, :, 2 * HALF : 3 * HALF], 0.0)
    state_ref[:, : 2 * HALF] = jnp.where(upper, forward1, eye)
    state_ref[:, 2 * HALF : 4 * HALF] = jnp.where(upper, 0.0, cross_ref[...])
    state_ref[:, 4 * HALF :] = jnp.where(upper, eye[:, :HALF], back2)


def track_kernel(level, pair_ref, cross_ref, old_ref, state_ref):
    lane = lax.broadcasted_iota(jnp.int32, (TRACE, 2 * HALF), 1)
    columns = lane >= HALF

    @pl.when(is_upper(level) == 1)
    def _():
        forward1 = jnp.where(columns | (lane < TRACE), pair_ref[0, :, : 2 * HALF], 0.0)
        pair = split(forward1)
        here = old_ref[:, : 2 * HALF]
        back = old_ref[:, 2 * HALF : 4 * HALF]
        state_ref[:, : 2 * HALF] = product(split(here[:, :TRACE]), pair) + jnp.where(columns, here, 0.0)
        state_ref[:, 2 * HALF : 4 * HALF] = product(split(back[:, :TRACE]), pair) + jnp.where(columns, back, 0.0)
        state_ref[:, 4 * HALF :] = old_ref[:, 4 * HALF :]

    @pl.when(is_upper(level) == 0)
    def _():
        gain = split(old_ref[:, 4 * HALF : 4 * HALF + TRACE])
        back2 = jnp.where(lane[:, :HALF] < TRACE, pair_ref[1, :, 2 * HALF : 3 * HALF], 0.0)
        state_ref[:, : 2 * HALF] = old_ref[:, : 2 * HALF]
        state_ref[:, 2 * HALF : 4 * HALF] = old_ref[:, 2 * HALF : 4 * HALF] + product(gain, split(cross_ref[...]))
        state_ref[:, 4 * HALF :] = product(gain, split(back2))


def last_kernel(level, pair_ref, old_ref, keep_ref, out_ref, ends_ref):
    @pl.when(is_upper(level) == 1)
    def _():
        inflow = split(pair_ref[0, :, HALF:])
        ends_ref[0] = old_ref[:, HALF : 2 * HALF] + product(split(old_ref[:, :TRACE]), inflow)
        ends_ref[1] = old_ref[:, 3 * HALF : 4 * HALF] + product(split(old_ref[:, 2 * HALF : 2 * HALF + TRACE]), inflow)

    @pl.when(is_upper(level) == 0)
    def _():
        outflow = split(pair_ref[0, :, HALF:])
        value = pair_ref[1, :, HALF:] + product(split(pair_ref[1, :, :TRACE]), outflow)
        gain = split(old_ref[:, 4 * HALF : 4 * HALF + TRACE])
        ends_ref[0] = old_ref[:, HALF : 2 * HALF]
        ends_ref[1] = old_ref[:, 3 * HALF : 4 * HALF] + product(gain, split(value))

    inflow = split(ends_ref[0])
    incoming = split(ends_ref[1])
    for element in range(2):
        known = keep_ref[element]
        out_ref[element] = (
            known[:, HALF : 2 * HALF]
            + product(split(known[:, :TRACE]), inflow)
            + product(split(known[:, 2 * HALF : 2 * HALF + TRACE]), incoming)
        )


def call(kernel, shapes, operands, flops, specs=None, scratch=(), limit=8 * 1024):
    moved = 4 * sum(v.size for v in operands) + 4 * sum(s.size for s in shapes)
    single = len(shapes) == 1
    return pl.pallas_call(
        kernel,
        out_shape=shapes[0] if single else shapes,
        in_specs=specs or [VMEM] * len(operands),
        out_specs=VMEM if single else [VMEM] * len(shapes),
        scratch_shapes=list(scratch),
        compiler_params=pltpu.CompilerParams(vmem_limit_bytes=limit * 1024),
        cost_estimate=pl.CostEstimate(flops=flops, bytes_accessed=moved, transcendentals=0),
    )(*operands)


def shape(*dims):
    return jax.ShapeDtypeStruct(dims, F32)


PARTNERS = ((0, 0, 1), (0, 1, 0), (0, 2, 0), (0, 7, 0), (1, 0, 0), (3, 0, 0))


def exchange(value, level):
    across, along, core = PARTNERS[level]
    mask = (across * 8 + along) * 2 + core
    count = lax.axis_size("stream")
    pairs = [[k, k ^ mask] for k in range(count) if k < k ^ mask]
    return lax.all_gather(value, "stream", axis_index_groups=pairs)


def shards(rhs, inverse, lower, upper, upwind, rows, target):
    groups = lax.axis_size("azi")
    local = rhs.shape[0]
    top = len(PARTNERS) - 1
    target = target.reshape(1, -1)
    partial = call(
        wake_kernel,
        [shape(groups * local, BLOCK)],
        [target, rows],
        10**6,
        specs=[HBM, HBM],
        scratch=[
            pltpu.VMEM(target.shape, jnp.int32),
            pltpu.VMEM(rows.shape, F32),
            pltpu.SemaphoreType.DMA((2,)),
        ],
        limit=56 * 1024,
    )
    parts = lax.all_to_all(partial.reshape(groups, local, BLOCK), "azi", 0, 0)
    parts = jnp.swapaxes(parts, 0, 1)
    total, keep = call(
        local_kernel,
        [shape(TRACE, 4 * HALF), shape(local, BLOCK, 3 * HALF)],
        [upwind, parts, lower, inverse, rhs, upper],
        2 * 10**9,
        specs=[SMEM, VMEM, HBM, HBM, HBM, HBM],
        scratch=[
            pltpu.VMEM(lower.shape, F32),
            pltpu.VMEM(inverse.shape[1:], F32),
            pltpu.VMEM(inverse.shape[1:], F32),
            pltpu.VMEM(rhs.shape, F32),
            pltpu.VMEM(upper.shape, F32),
            pltpu.SemaphoreType.DMA((5,)),
        ],
        limit=56 * 1024,
    )
    state = None
    for level in range(top):
        pair = exchange(total, level)
        last = top if level == top - 1 else 0
        total, cross = call(
            functools.partial(combine_kernel, last),
            [shape(TRACE, (2 if last else 4) * HALF), shape(TRACE, 2 * HALF)],
            [pair],
            2 * 10**7,
        )
        track = functools.partial(track_kernel if level else track_first_kernel, level)
        operands = [pair, cross, state] if level else [pair, cross]
        state = call(track, [shape(TRACE, 5 * HALF)], operands, 10**7)
    return call(
        functools.partial(last_kernel, top),
        [shape(local, BLOCK, COLUMNS)],
        [exchange(total, top), state, keep],
        10**8,
        scratch=[pltpu.VMEM((2, TRACE, COLUMNS), F32)],
    )


def solution(mesh):
    both = ("stream", "azi")
    return jax.shard_map(
        shards,
        mesh=mesh,
        in_specs=(
            P(both, None, None),
            P(both, None, None),
            P(both, None, None),
            P(both, None, None),
            P(both, None),
            P(both, None),
            P(both),
        ),
        out_specs=P(both, None, None),
        check_vma=False,
    )
```

```python
import functools

import jax
import jax.numpy as jnp
from jax import lax
from jax.experimental import pallas as pl
from jax.experimental.pallas import tpu as pltpu
from jax.sharding import PartitionSpec as P

TRACE = 80
BLOCK = 320
COLUMNS = 128
PLANE = 16
CUBE = 64
HALF = 128
F32 = jnp.float32
BF16 = jnp.bfloat16
VMEM = pl.BlockSpec(memory_space=pltpu.VMEM)
SMEM = pl.BlockSpec(memory_space=pltpu.SMEM)
HBM = pl.BlockSpec(memory_space=pltpu.HBM)


def split(value):
    high = value.astype(BF16)
    return high, (value - high.astype(F32)).astype(BF16)


def dot(left, right):
    return jnp.dot(left, right, preferred_element_type=F32)


def product(left, right):
    return dot(left[0], right[0]) + (dot(left[0], right[1]) + dot(left[1], right[0]))


def select_rows(onehot, value):
    return dot(onehot, value[0]), dot(onehot, value[1])


def fetch(sources, buffers, sems):
    copies = [pltpu.make_async_copy(a, b, sems.at[i]) for i, (a, b) in enumerate(zip(sources, buffers))]
    for copy in copies:
        copy.start()
    return copies


def wake_kernel(target_hbm, rows_hbm, out_ref, target_ref, rows_ref, sems):
    for copy in fetch((target_hbm, rows_hbm), (target_ref, rows_ref), sems):
        copy.wait()
    ids = lax.broadcasted_iota(jnp.int32, (out_ref.shape[0], target_ref.shape[1]), 0)
    onehot = jnp.where(ids == target_ref[...], 1.0, 0.0).astype(BF16)
    high, low = split(rows_ref[...])
    out_ref[...] = dot(onehot, high) + dot(onehot, low)


def face_block(ref, element, face):
    return ref[element, :, face * TRACE : (face + 1) * TRACE]


def rows_of(slots, transposed):
    shape = (1, 3 * TRACE) if transposed else (3 * TRACE, 1)
    place = lax.broadcasted_iota(jnp.int32, shape, 1 if transposed else 0)
    which = jnp.where(place >= 2 * TRACE, 2, jnp.where(place >= TRACE, 1, 0))
    trace = place - which * TRACE
    field, upper, lower = trace >> 4, (trace >> 2) & 3, trace & 3
    side = 3 * (slots[0] % 2)
    row = jnp.where(
        which == 0,
        side * 16 + upper * 4 + lower,
        jnp.where(which == 1, upper * 16 + side * 4 + lower, upper * 16 + lower * 4 + side),
    )
    row = field * CUBE + row
    whole = (BLOCK, 3 * TRACE) if transposed else (3 * TRACE, BLOCK)
    rows = lax.broadcasted_iota(jnp.int32, whole, 0 if transposed else 1)
    return jnp.where(rows == row, 1.0, 0.0).astype(BF16)


def last_plane(value):
    return jnp.concatenate(
        [value[at + CUBE - PLANE : at + CUBE] for at in range(0, BLOCK, CUBE)], axis=0
    )


def pack(first, second, third, fourth):
    lead = TRACE
    spare = HALF - lead
    mid = third[:, :HALF]
    return jnp.concatenate(
        [
            first[:, :lead],
            mid[:, :spare],
            first[:, HALF:],
            fourth[:, :lead],
            mid[:, spare:lead],
            jnp.zeros((TRACE, 2 * spare - lead), F32),
            third[:, HALF:],
        ],
        axis=1,
    )


def unpack(value):
    lead = TRACE
    spare = HALF - lead
    zeros = jnp.zeros((TRACE, spare), F32)
    forward = value[:, : 2 * HALF]
    mixed = jnp.concatenate(
        [
            value[:, lead:HALF],
            value[:, 2 * HALF + lead : 2 * HALF + lead + (lead - spare)],
            zeros,
            value[:, 3 * HALF :],
        ],
        axis=1,
    )
    return forward, mixed, value[:, 2 * HALF : 2 * HALF + lead]


def expand(block, take):
    high, low = split(block)
    return dot(high, take) + dot(low, take)


def local_kernel(
    wake_ref,
    upwind_hbm,
    low_hbm,
    up_hbm,
    inv_hbm,
    rhs_hbm,
    total_ref,
    keep_ref,
    upwind_ref,
    low_ref,
    up_ref,
    first_inv_ref,
    second_inv_ref,
    rhs_ref,
    sems,
):
    copies = fetch(
        (upwind_hbm, low_hbm, up_hbm, inv_hbm.at[0], rhs_hbm, inv_hbm.at[1]),
        (upwind_ref, low_ref, up_ref, first_inv_ref, rhs_ref, second_inv_ref),
        sems,
    )
    put_even = rows_of((0, 2, 4), True)
    take_even = rows_of((0, 2, 4), False)
    put_odd = rows_of((1, 3, 5), True)
    take_odd = rows_of((1, 3, 5), False)
    ones = jnp.ones((wake_ref.shape[1], COLUMNS), BF16)
    spare = jnp.zeros((3 * TRACE, HALF - TRACE), F32)
    at = [slice(face * TRACE, (face + 1) * TRACE) for face in range(3)]

    def source(element):
        high, low = split(wake_ref[element])
        dims = (((0,), (0,)), ((), ()))
        wake = lax.dot_general(high, ones, dims, preferred_element_type=F32)
        wake += lax.dot_general(low, ones, dims, preferred_element_type=F32)
        return rhs_ref[element] + wake

    def put(onehot, rows):
        return sum(select_rows(onehot, split(rows)))

    for copy in copies[:3]:
        copy.wait()
    crosses = [upwind_ref[1, face] == 2 for face in range(3)]

    def kept(values, crossing):
        return [jnp.where(cross == crossing, v, 0.0) for cross, v in zip(crosses, values)]

    def wide(values):
        return jnp.concatenate([jnp.concatenate(values, axis=0), spare], axis=1)

    from_first = put(put_even, wide([face_block(low_ref, 0, face) for face in range(3)]))
    blocks = [face_block(low_ref, 1, face) for face in range(3)]
    from_second = put(put_even, wide(kept(blocks, True)))
    inside = [expand(blocks[face], take_odd[at[face]]) for face in range(3)]
    down = split(put(put_even, jnp.concatenate(kept(inside, False), axis=0)))
    inside = [expand(face_block(up_ref, 1, face), take_even[at[face]]) for face in range(3)]
    up = split(put(put_odd, jnp.concatenate(kept(inside, False), axis=0)))
    leave_second = split(sum(kept(inside, True)))
    leave_first = split(expand(up_ref[0], take_even))

    for copy in copies[3:]:
        copy.wait()
    inverse = split(first_inv_ref[...])
    later_inverse = split(second_inv_ref[...])
    first = product(inverse, split(jnp.concatenate([-from_first, source(0)], axis=1)))

    side = put_odd[:, :HALF]
    lane = lax.broadcasted_iota(jnp.int32, (BLOCK, HALF), 1)
    returned = -(dot(later_inverse[0], side) + dot(later_inverse[1], side))
    returned = jnp.where(lane < TRACE, returned, 0.0)
    returned_pair = split(returned)
    keep_ref[1, :, 2 * HALF :] = returned

    inner = product(down, split(first))
    earlier = -product(inverse, split(product(up, returned_pair)))
    keep_ref[0, :, 2 * HALF :] = earlier

    base = jnp.concatenate([-from_second, source(1)], axis=1)
    second = product(later_inverse, split(base - inner))
    keep_ref[1, :, : 2 * HALF] = second
    second_pair = split(second)
    back = product(leave_second, returned_pair) + product(leave_first, split(earlier))
    inner = product(up, second_pair)
    first = first - product(inverse, split(inner))
    keep_ref[0, :, : 2 * HALF] = first
    mixed = product(leave_second, second_pair) + product(leave_first, split(first))
    total_ref[...] = pack(last_plane(second), None, mixed, back)


def is_upper(level):
    return (lax.axis_index("stream") >> level) & 1


def combine_kernel(level, sends, pair_ref, *refs):
    total_ref, state_ref = refs[-2:]
    forward1, mixed1, back1 = unpack(pair_ref[0])
    forward2, mixed2, back2 = unpack(pair_ref[1])
    lane = lax.broadcasted_iota(jnp.int32, (TRACE, 2 * HALF), 1)
    columns = lane >= HALF
    forward1 = jnp.where(columns | (lane < TRACE), forward1, 0.0)
    forward_pair = split(forward1)
    cross = product(split(mixed2[:, :TRACE]), forward_pair) + jnp.where(columns, mixed2, 0.0)
    forward = product(split(forward2[:, :TRACE]), forward_pair)
    forward = forward + jnp.where(columns, forward2, 0.0)
    back_pair = split(back1)
    mixed = mixed1 + product(back_pair, split(cross))
    if sends == "top":
        total_ref[...] = jnp.where(is_upper(level + 1) == 1, mixed, forward)
    else:
        total = pack(forward, None, mixed, product(back_pair, split(back2)))
        if sends == "half":
            half = TRACE // 2
            total = jnp.where(is_upper(0) == 1, total[half:], total[:half])
        total_ref[...] = total

    upper = is_upper(level) == 1
    back2 = jnp.concatenate([back2, jnp.zeros((TRACE, HALF - TRACE), F32)], axis=1)
    if level == 0:
        row = lax.broadcasted_iota(jnp.int32, (TRACE, 2 * HALF), 0)
        eye = jnp.where(lane == row, 1.0, 0.0)
        state_ref[:, : 2 * HALF] = jnp.where(upper, forward1, eye)
        state_ref[:, 2 * HALF : 4 * HALF] = jnp.where(upper, 0.0, cross)
        state_ref[:, 4 * HALF :] = jnp.where(upper, eye[:, :HALF], back2)
        return
    old_ref = refs[0]

    @pl.when(upper)
    def _():
        here = old_ref[:, : 2 * HALF]
        back = old_ref[:, 2 * HALF : 4 * HALF]
        state_ref[:, : 2 * HALF] = product(split(here[:, :TRACE]), forward_pair) + jnp.where(columns, here, 0.0)
        state_ref[:, 2 * HALF : 4 * HALF] = product(split(back[:, :TRACE]), forward_pair) + jnp.where(columns, back, 0.0)
        state_ref[:, 4 * HALF :] = old_ref[:, 4 * HALF :]

    @pl.when(jnp.logical_not(upper))
    def _():
        gain = split(old_ref[:, 4 * HALF : 4 * HALF + TRACE])
        state_ref[:, : 2 * HALF] = old_ref[:, : 2 * HALF]
        state_ref[:, 2 * HALF : 4 * HALF] = old_ref[:, 2 * HALF : 4 * HALF] + product(gain, split(cross))
        state_ref[:, 4 * HALF :] = product(gain, split(back2))


def last_kernel(level, pair_ref, old_ref, keep_ref, out_ref, ends_ref):
    @pl.when(is_upper(level) == 1)
    def _():
        inflow = split(pair_ref[0, :, HALF:])
        ends_ref[0] = old_ref[:, HALF : 2 * HALF] + product(split(old_ref[:, :TRACE]), inflow)
        ends_ref[1] = old_ref[:, 3 * HALF : 4 * HALF] + product(split(old_ref[:, 2 * HALF : 2 * HALF + TRACE]), inflow)

    @pl.when(is_upper(level) == 0)
    def _():
        outflow = split(pair_ref[0, :, HALF:])
        value = pair_ref[1, :, HALF:] + product(split(pair_ref[1, :, :TRACE]), outflow)
        gain = split(old_ref[:, 4 * HALF : 4 * HALF + TRACE])
        ends_ref[0] = old_ref[:, HALF : 2 * HALF]
        ends_ref[1] = old_ref[:, 3 * HALF : 4 * HALF] + product(gain, split(value))

    inflow = split(ends_ref[0])
    incoming = split(ends_ref[1])
    for element in range(2):
        known = keep_ref[element]
        out_ref[element] = (
            known[:, HALF : 2 * HALF]
            + product(split(known[:, :TRACE]), inflow)
            + product(split(known[:, 2 * HALF : 2 * HALF + TRACE]), incoming)
        )


def call(kernel, shapes, operands, flops, specs=None, scratch=(), limit=8 * 1024):
    moved = 4 * sum(v.size for v in operands) + 4 * sum(s.size for s in shapes)
    single = len(shapes) == 1
    return pl.pallas_call(
        kernel,
        out_shape=shapes[0] if single else shapes,
        in_specs=specs or [VMEM] * len(operands),
        out_specs=VMEM if single else [VMEM] * len(shapes),
        scratch_shapes=list(scratch),
        compiler_params=pltpu.CompilerParams(vmem_limit_bytes=limit * 1024),
        cost_estimate=pl.CostEstimate(flops=flops, bytes_accessed=moved, transcendentals=0),
    )(*operands)


def shape(*dims):
    return jax.ShapeDtypeStruct(dims, F32)


LEVELS = (
    ((0, 0, 1), "whole"),
    ((0, 1, 0), "whole"),
    ((0, 2, 0), "half"),
    ((0, 6, 0), "half"),
    ((1, 0, 0), "whole"),
    ((3, 0, 0), "top"),
)


def exchange(value, level):
    (across, along, core), sends = LEVELS[level]
    mask = (across * 8 + along) * 2 + core
    count = lax.axis_size("stream")
    if sends == "half":
        groups = [[k, k + 1, k ^ mask, (k ^ mask) + 1] for k in range(0, count, 2) if k < k ^ mask]
    else:
        groups = [[k, k ^ mask] for k in range(count) if k < k ^ mask]
    gathered = lax.all_gather(value, "stream", axis_index_groups=groups)
    return gathered.reshape(2, TRACE, value.shape[-1])


def shards(rhs, inverse, lower, upper, upwind, rows, target):
    groups = lax.axis_size("azi")
    local = rhs.shape[0]
    top = len(LEVELS) - 1
    target = target.reshape(1, -1)
    rhs, inverse, lower, upper, upwind, rows, target = [
        pltpu.with_memory_space_constraint(v, pltpu.HBM)
        for v in (rhs, inverse, lower, upper, upwind, rows, target)
    ]
    partial = call(
        wake_kernel,
        [shape(groups * local, BLOCK)],
        [target, rows],
        10**6,
        specs=[HBM, HBM],
        scratch=[
            pltpu.VMEM(target.shape, jnp.int32),
            pltpu.VMEM(rows.shape, F32),
            pltpu.SemaphoreType.DMA((2,)),
        ],
    )
    parts = lax.all_to_all(partial.reshape(groups, local, BLOCK), "azi", 0, 0)
    parts = jnp.swapaxes(parts, 0, 1)
    total, keep = call(
        local_kernel,
        [shape(TRACE, 4 * HALF), shape(local, BLOCK, 3 * HALF)],
        [parts, upwind, lower, upper, inverse, rhs],
        2 * 10**9,
        specs=[VMEM, HBM, HBM, HBM, HBM, HBM],
        scratch=[
            pltpu.SMEM(upwind.shape, jnp.int32),
            pltpu.VMEM(lower.shape, F32),
            pltpu.VMEM(upper.shape, F32),
            pltpu.VMEM(inverse.shape[1:], F32),
            pltpu.VMEM(inverse.shape[1:], F32),
            pltpu.VMEM(rhs.shape, F32),
            pltpu.SemaphoreType.DMA((6,)),
        ],
        limit=24 * 1024,
    )
    state = []
    for level in range(top):
        sends = LEVELS[level + 1][1]
        height = TRACE // 2 if sends == "half" else TRACE
        width = 2 * HALF if sends == "top" else 4 * HALF
        total, after = call(
            functools.partial(combine_kernel, level, sends),
            [shape(height, width), shape(TRACE, 5 * HALF)],
            [exchange(total, level)] + state,
            3 * 10**7,
        )
        state = [after]
    return call(
        functools.partial(last_kernel, top),
        [shape(local, BLOCK, COLUMNS)],
        [exchange(total, top), state[0], keep],
        10**8,
        scratch=[pltpu.VMEM((2, TRACE, COLUMNS), F32)],
    )


def solution(mesh):
    both = ("stream", "azi")
    return jax.shard_map(
        shards,
        mesh=mesh,
        in_specs=(
            P(both, None, None),
            P(both, None, None),
            P(both, None, None),
            P(both, None, None),
            P(both, None),
            P(both, None),
            P(both),
        ),
        out_specs=P(both, None, None),
        check_vma=False,
    )
```

```python
import functools

import jax
import jax.numpy as jnp
import numpy as np
from jax import lax
from jax.experimental import pallas as pl
from jax.experimental.pallas import tpu as pltpu
from jax.sharding import PartitionSpec as P

TRACE = 80
BLOCK = 320
COLUMNS = 128
PLANE = 16
CUBE = 64
HALF = 128
F32 = jnp.float32
BF16 = jnp.bfloat16
VMEM = pl.BlockSpec(memory_space=pltpu.VMEM)
SMEM = pl.BlockSpec(memory_space=pltpu.SMEM)
HBM = pl.BlockSpec(memory_space=pltpu.HBM)


def split(value):
    high = value.astype(BF16)
    return high, (value - high.astype(F32)).astype(BF16)


def dot(left, right):
    return jnp.dot(left, right, preferred_element_type=F32)


def product(left, right):
    return dot(left[0], right[0]) + (dot(left[0], right[1]) + dot(left[1], right[0]))


def select_rows(onehot, value):
    return dot(onehot, value[0]), dot(onehot, value[1])


def fetch(sources, buffers, sems):
    copies = [pltpu.make_async_copy(a, b, sems.at[i]) for i, (a, b) in enumerate(zip(sources, buffers))]
    for copy in copies:
        copy.start()
    return copies


def wake_kernel(target_hbm, rows_hbm, upwind_hbm, out_ref, crosses_ref, target_ref, rows_ref, upwind_ref, sems):
    for copy in fetch((target_hbm, rows_hbm, upwind_hbm), (target_ref, rows_ref, upwind_ref), sems):
        copy.wait()
    ids = lax.broadcasted_iota(jnp.int32, (out_ref.shape[0], target_ref.shape[1]), 0)
    onehot = jnp.where(ids == target_ref[...], 1.0, 0.0).astype(BF16)
    high, low = split(rows_ref[...])
    out_ref[...] = dot(onehot, high) + dot(onehot, low)
    face = lax.broadcasted_iota(jnp.int32, crosses_ref.shape, 0)
    crosses = jnp.zeros(crosses_ref.shape, F32)
    for at in range(3):
        crosses = jnp.where((face == at) & (upwind_ref[1, at] == 2), 1.0, crosses)
    crosses_ref[...] = crosses


def face_block(ref, element, face):
    return ref[element, :, face * TRACE : (face + 1) * TRACE]


def face_rows():
    trace = np.arange(TRACE)
    field, upper, lower = trace // PLANE, trace // 4 % 4, trace % 4
    take = np.zeros((2, 3 * TRACE, BLOCK), np.float32)
    for odd in range(2):
        side = 3 * odd
        places = (side * 16 + upper * 4 + lower, upper * 16 + side * 4 + lower, upper * 16 + lower * 4 + side)
        for face, place in enumerate(places):
            take[odd, face * TRACE + trace, field * CUBE + place] = 1.0
    return jnp.asarray(take, BF16), jnp.asarray(take.transpose(0, 2, 1), BF16)


WHOLE = 256


def left_parts(value):
    high, low = split(value)
    ends = [part[:, WHOLE:].astype(F32) for part in (high, low, high)]
    return high[:, :WHOLE], low[:, :WHOLE], jnp.concatenate(ends, axis=1).astype(BF16)


def right_parts(value):
    high, low = split(value)
    ends = [part[WHOLE:] for part in (high, high, low)]
    return high[:WHOLE], low[:WHOLE], jnp.concatenate(ends, axis=0)


def long_product(left, right):
    return (dot(left[0], right[0]) + dot(left[2], right[2])) + (dot(left[0], right[1]) + dot(left[1], right[0]))


def last_plane(value):
    return jnp.concatenate(
        [value[at + CUBE - PLANE : at + CUBE] for at in range(0, BLOCK, CUBE)], axis=0
    )


def pack(first, second, third, fourth):
    lead = TRACE
    spare = HALF - lead
    mid = third[:, :HALF]
    return jnp.concatenate(
        [
            first[:, :lead],
            mid[:, :spare],
            first[:, HALF:],
            fourth[:, :lead],
            mid[:, spare:lead],
            jnp.zeros((TRACE, 2 * spare - lead), F32),
            third[:, HALF:],
        ],
        axis=1,
    )


def unpack(value):
    lead = TRACE
    spare = HALF - lead
    zeros = jnp.zeros((TRACE, spare), F32)
    forward = value[:, : 2 * HALF]
    mixed = jnp.concatenate(
        [
            value[:, lead:HALF],
            value[:, 2 * HALF + lead : 2 * HALF + lead + (lead - spare)],
            zeros,
            value[:, 3 * HALF :],
        ],
        axis=1,
    )
    return forward, mixed, value[:, 2 * HALF : 2 * HALF + lead]


def expand(block, take):
    high, low = split(block)
    return dot(high, take) + dot(low, take)


def local_kernel(take_ref, put_ref, crosses_ref, wake_ref, low_ref, up_ref, inv_ref, rhs_ref, total_ref, keep_ref):
    put_even, put_odd = put_ref[0], put_ref[1]
    take_even, take_odd = take_ref[0], take_ref[1]
    ones = jnp.ones((wake_ref.shape[1], COLUMNS), BF16)
    spare = jnp.zeros((3 * TRACE, HALF - TRACE), F32)
    at = [slice(face * TRACE, (face + 1) * TRACE) for face in range(3)]

    def source(element):
        high, low = split(wake_ref[element])
        dims = (((0,), (0,)), ((), ()))
        wake = lax.dot_general(high, ones, dims, preferred_element_type=F32)
        wake += lax.dot_general(low, ones, dims, preferred_element_type=F32)
        return rhs_ref[element] + wake

    def put(onehot, rows):
        return sum(select_rows(onehot, split(rows)))

    crosses = [crosses_ref[face : face + 1, :1] > 0.5 for face in range(3)]

    def kept(values, crossing):
        return [jnp.where(cross == crossing, v, 0.0) for cross, v in zip(crosses, values)]

    def wide(values):
        return jnp.concatenate([jnp.concatenate(values, axis=0), spare], axis=1)

    from_first = put(put_even, wide([face_block(low_ref, 0, face) for face in range(3)]))
    blocks = [face_block(low_ref, 1, face) for face in range(3)]
    from_second = put(put_even, wide(kept(blocks, True)))
    inside = [expand(blocks[face], take_odd[at[face]]) for face in range(3)]
    down = left_parts(put(put_even, jnp.concatenate(kept(inside, False), axis=0)))
    inside = [expand(face_block(up_ref, 1, face), take_even[at[face]]) for face in range(3)]
    up = left_parts(put(put_odd, jnp.concatenate(kept(inside, False), axis=0)))
    leave_second = left_parts(sum(kept(inside, True)))
    leave_first = left_parts(expand(up_ref[0], take_even))

    inverse = left_parts(inv_ref[0])
    later_inverse = left_parts(inv_ref[1])
    first = long_product(inverse, right_parts(jnp.concatenate([-from_first, source(0)], axis=1)))

    side = put_odd[:, :HALF]
    lane = lax.broadcasted_iota(jnp.int32, (BLOCK, HALF), 1)
    high, low = split(inv_ref[1])
    returned = -(dot(high, side) + dot(low, side))
    returned = jnp.where(lane < TRACE, returned, 0.0)
    returned_pair = right_parts(returned)
    keep_ref[1, :, 2 * HALF :] = returned

    inner = long_product(down, right_parts(first))
    earlier = -long_product(inverse, right_parts(long_product(up, returned_pair)))
    keep_ref[0, :, 2 * HALF :] = earlier

    base = jnp.concatenate([-from_second, source(1)], axis=1)
    second = long_product(later_inverse, right_parts(base - inner))
    keep_ref[1, :, : 2 * HALF] = second
    second_pair = right_parts(second)
    back = long_product(leave_second, returned_pair) + long_product(leave_first, right_parts(earlier))
    inner = long_product(up, second_pair)
    first = first - long_product(inverse, right_parts(inner))
    keep_ref[0, :, : 2 * HALF] = first
    mixed = long_product(leave_second, second_pair) + long_product(leave_first, right_parts(first))
    total_ref[...] = pack(last_plane(second), None, mixed, back)


def is_upper(level):
    return (lax.axis_index("stream") >> level) & 1


def combine_kernel(level, sends, pair_ref, *refs):
    total_ref, state_ref = refs[-2:]
    forward1, mixed1, back1 = unpack(pair_ref[0])
    forward2, mixed2, back2 = unpack(pair_ref[1])
    lane = lax.broadcasted_iota(jnp.int32, (TRACE, 2 * HALF), 1)
    columns = lane >= HALF
    forward1 = jnp.where(columns | (lane < TRACE), forward1, 0.0)
    forward_pair = split(forward1)
    cross = product(split(mixed2[:, :TRACE]), forward_pair) + jnp.where(columns, mixed2, 0.0)
    forward = product(split(forward2[:, :TRACE]), forward_pair)
    forward = forward + jnp.where(columns, forward2, 0.0)
    back_pair = split(back1)
    mixed = mixed1 + product(back_pair, split(cross))
    if sends == "top":
        total_ref[...] = jnp.where(is_upper(level + 1) == 1, mixed, forward)
    else:
        total = pack(forward, None, mixed, product(back_pair, split(back2)))
        if sends == "half":
            half = TRACE // 2
            total = jnp.where(is_upper(0) == 1, total[half:], total[:half])
        total_ref[...] = total

    upper = is_upper(level) == 1
    back2 = jnp.concatenate([back2, jnp.zeros((TRACE, HALF - TRACE), F32)], axis=1)
    if level == 0:
        row = lax.broadcasted_iota(jnp.int32, (TRACE, 2 * HALF), 0)
        eye = jnp.where(lane == row, 1.0, 0.0)
        state_ref[:, : 2 * HALF] = jnp.where(upper, forward1, eye)
        state_ref[:, 2 * HALF : 4 * HALF] = jnp.where(upper, 0.0, cross)
        state_ref[:, 4 * HALF :] = jnp.where(upper, eye[:, :HALF], back2)
        return
    old_ref = refs[0]

    @pl.when(upper)
    def _():
        here = old_ref[:, : 2 * HALF]
        back = old_ref[:, 2 * HALF : 4 * HALF]
        state_ref[:, : 2 * HALF] = product(split(here[:, :TRACE]), forward_pair) + jnp.where(columns, here, 0.0)
        state_ref[:, 2 * HALF : 4 * HALF] = product(split(back[:, :TRACE]), forward_pair) + jnp.where(columns, back, 0.0)
        state_ref[:, 4 * HALF :] = old_ref[:, 4 * HALF :]

    @pl.when(jnp.logical_not(upper))
    def _():
        gain = split(old_ref[:, 4 * HALF : 4 * HALF + TRACE])
        state_ref[:, : 2 * HALF] = old_ref[:, : 2 * HALF]
        state_ref[:, 2 * HALF : 4 * HALF] = old_ref[:, 2 * HALF : 4 * HALF] + product(gain, split(cross))
        state_ref[:, 4 * HALF :] = product(gain, split(back2))


def last_kernel(level, pair_ref, old_ref, keep_ref, out_ref, ends_ref):
    @pl.when(is_upper(level) == 1)
    def _():
        inflow = split(pair_ref[0, :, HALF:])
        ends_ref[0] = old_ref[:, HALF : 2 * HALF] + product(split(old_ref[:, :TRACE]), inflow)
        ends_ref[1] = old_ref[:, 3 * HALF : 4 * HALF] + product(split(old_ref[:, 2 * HALF : 2 * HALF + TRACE]), inflow)

    @pl.when(is_upper(level) == 0)
    def _():
        outflow = split(pair_ref[0, :, HALF:])
        value = pair_ref[1, :, HALF:] + product(split(pair_ref[1, :, :TRACE]), outflow)
        gain = split(old_ref[:, 4 * HALF : 4 * HALF + TRACE])
        ends_ref[0] = old_ref[:, HALF : 2 * HALF]
        ends_ref[1] = old_ref[:, 3 * HALF : 4 * HALF] + product(gain, split(value))

    inflow = split(ends_ref[0])
    incoming = split(ends_ref[1])
    for element in range(2):
        known = keep_ref[element]
        out_ref[element] = (
            known[:, HALF : 2 * HALF]
            + product(split(known[:, :TRACE]), inflow)
            + product(split(known[:, 2 * HALF : 2 * HALF + TRACE]), incoming)
        )


def call(kernel, shapes, operands, flops, specs=None, scratch=(), limit=8 * 1024):
    moved = 4 * sum(v.size for v in operands) + 4 * sum(s.size for s in shapes)
    single = len(shapes) == 1
    return pl.pallas_call(
        kernel,
        out_shape=shapes[0] if single else shapes,
        in_specs=specs or [VMEM] * len(operands),
        out_specs=VMEM if single else [VMEM] * len(shapes),
        scratch_shapes=list(scratch),
        compiler_params=pltpu.CompilerParams(vmem_limit_bytes=limit * 1024),
        cost_estimate=pl.CostEstimate(flops=flops, bytes_accessed=moved, transcendentals=0),
    )(*operands)


def shape(*dims):
    return jax.ShapeDtypeStruct(dims, F32)


LEVELS = (
    ((0, 0, 1), "whole"),
    ((0, 1, 0), "whole"),
    ((0, 2, 0), "half"),
    ((0, 6, 0), "half"),
    ((1, 0, 0), "whole"),
    ((3, 0, 0), "top"),
)


def exchange(value, level):
    (across, along, core), sends = LEVELS[level]
    mask = (across * 8 + along) * 2 + core
    count = lax.axis_size("stream")
    if sends == "half":
        groups = [[k, k + 1, k ^ mask, (k ^ mask) + 1] for k in range(0, count, 2) if k < k ^ mask]
    else:
        groups = [[k, k ^ mask] for k in range(count) if k < k ^ mask]
    gathered = lax.all_gather(value, "stream", axis_index_groups=groups)
    return gathered.reshape(2, TRACE, value.shape[-1])


def shards(rhs, inverse, lower, upper, upwind, rows, target):
    groups = lax.axis_size("azi")
    local = rhs.shape[0]
    top = len(LEVELS) - 1
    target = target.reshape(1, -1)
    rows, target, upwind = [pltpu.with_memory_space_constraint(v, pltpu.HBM) for v in (rows, target, upwind)]
    partial, crosses = call(
        wake_kernel,
        [shape(groups * local, BLOCK), shape(8, HALF)],
        [target, rows, upwind],
        10**10,
        specs=[HBM, HBM, HBM],
        scratch=[
            pltpu.VMEM(target.shape, jnp.int32),
            pltpu.VMEM(rows.shape, F32),
            pltpu.SMEM(upwind.shape, jnp.int32),
            pltpu.SemaphoreType.DMA((3,)),
        ],
    )
    parts = lax.all_to_all(partial.reshape(groups, local, BLOCK), "azi", 0, 0)
    parts = jnp.swapaxes(parts, 0, 1)
    total, keep = call(
        local_kernel,
        [shape(TRACE, 4 * HALF), shape(local, BLOCK, 3 * HALF)],
        [*face_rows(), crosses, parts, lower, upper, inverse, rhs],
        2 * 10**9,
        limit=24 * 1024,
    )
    state = []
    for level in range(top):
        sends = LEVELS[level + 1][1]
        height = TRACE // 2 if sends == "half" else TRACE
        width = 2 * HALF if sends == "top" else 4 * HALF
        total, after = call(
            functools.partial(combine_kernel, level, sends),
            [shape(height, width), shape(TRACE, 5 * HALF)],
            [exchange(total, level)] + state,
            3 * 10**7,
        )
        state = [after]
    return call(
        functools.partial(last_kernel, top),
        [shape(local, BLOCK, COLUMNS)],
        [exchange(total, top), state[0], keep],
        10**8,
        scratch=[pltpu.VMEM((2, TRACE, COLUMNS), F32)],
    )


def solution(mesh):
    both = ("stream", "azi")
    return jax.shard_map(
        shards,
        mesh=mesh,
        in_specs=(
            P(both, None, None),
            P(both, None, None),
            P(both, None, None),
            P(both, None, None),
            P(both, None),
            P(both, None),
            P(both),
        ),
        out_specs=P(both, None, None),
        check_vma=False,
    )
```

```python
import functools

import jax
import jax.numpy as jnp
import numpy as np
from jax import lax
from jax.experimental import pallas as pl
from jax.experimental.pallas import tpu as pltpu
from jax.sharding import PartitionSpec as P

TRACE = 80
BLOCK = 320
COLUMNS = 128
PLANE = 16
CUBE = 64
HALF = 128
F32 = jnp.float32
BF16 = jnp.bfloat16
VMEM = pl.BlockSpec(memory_space=pltpu.VMEM)
SMEM = pl.BlockSpec(memory_space=pltpu.SMEM)
HBM = pl.BlockSpec(memory_space=pltpu.HBM)


def split(value):
    high = value.astype(BF16)
    return high, (value - high.astype(F32)).astype(BF16)


def dot(left, right):
    return jnp.dot(left, right, preferred_element_type=F32)


def product(left, right):
    return dot(left[0], right[0]) + (dot(left[0], right[1]) + dot(left[1], right[0]))


def select_rows(onehot, value):
    return dot(onehot, value[0]), dot(onehot, value[1])


def fetch(sources, buffers, sems):
    copies = [pltpu.make_async_copy(a, b, sems.at[i]) for i, (a, b) in enumerate(zip(sources, buffers))]
    for copy in copies:
        copy.start()
    return copies


def wake_kernel(target_hbm, rows_hbm, upwind_hbm, out_ref, crosses_ref, target_ref, rows_ref, upwind_ref, sems):
    for copy in fetch((target_hbm, rows_hbm, upwind_hbm), (target_ref, rows_ref, upwind_ref), sems):
        copy.wait()
    ids = lax.broadcasted_iota(jnp.int32, (out_ref.shape[0], target_ref.shape[1]), 0)
    onehot = jnp.where(ids == target_ref[...], 1.0, 0.0).astype(BF16)
    high, low = split(rows_ref[...])
    out_ref[...] = dot(onehot, high) + dot(onehot, low)
    face = lax.broadcasted_iota(jnp.int32, crosses_ref.shape, 0)
    crosses = jnp.zeros(crosses_ref.shape, F32)
    for at in range(3):
        crosses = jnp.where((face == at) & (upwind_ref[1, at] == 2), 1.0, crosses)
    crosses_ref[...] = crosses


def face_block(ref, element, face):
    return ref[element, :, face * TRACE : (face + 1) * TRACE]


def face_rows():
    trace = np.arange(TRACE)
    field, upper, lower = trace // PLANE, trace // 4 % 4, trace % 4
    take = np.zeros((2, 3 * TRACE, BLOCK), np.float32)
    for odd in range(2):
        side = 3 * odd
        places = (side * 16 + upper * 4 + lower, upper * 16 + side * 4 + lower, upper * 16 + lower * 4 + side)
        for face, place in enumerate(places):
            take[odd, face * TRACE + trace, field * CUBE + place] = 1.0
    return jnp.asarray(take, BF16), jnp.asarray(take.transpose(0, 2, 1), BF16)


WHOLE = 256


def left_parts(value):
    high, low = split(value)
    ends = [part[:, WHOLE:].astype(F32) for part in (high, low, high)]
    return high[:, :WHOLE], low[:, :WHOLE], jnp.concatenate(ends, axis=1).astype(BF16)


def right_parts(value):
    high, low = split(value)
    ends = [part[WHOLE:] for part in (high, high, low)]
    return high[:WHOLE], low[:WHOLE], jnp.concatenate(ends, axis=0)


def long_product(left, right):
    return (dot(left[0], right[0]) + dot(left[2], right[2])) + (dot(left[0], right[1]) + dot(left[1], right[0]))


def last_plane(value):
    return jnp.concatenate(
        [value[at + CUBE - PLANE : at + CUBE] for at in range(0, BLOCK, CUBE)], axis=0
    )


def pack(first, second, third, fourth):
    lead = TRACE
    spare = HALF - lead
    mid = third[:, :HALF]
    return jnp.concatenate(
        [
            first[:, :lead],
            mid[:, :spare],
            first[:, HALF:],
            fourth[:, :lead],
            mid[:, spare:lead],
            jnp.zeros((TRACE, 2 * spare - lead), F32),
            third[:, HALF:],
        ],
        axis=1,
    )


def unpack(value):
    lead = TRACE
    spare = HALF - lead
    zeros = jnp.zeros((TRACE, spare), F32)
    forward = value[:, : 2 * HALF]
    mixed = jnp.concatenate(
        [
            value[:, lead:HALF],
            value[:, 2 * HALF + lead : 2 * HALF + lead + (lead - spare)],
            zeros,
            value[:, 3 * HALF :],
        ],
        axis=1,
    )
    return forward, mixed, value[:, 2 * HALF : 2 * HALF + lead]


def expand(block, take):
    high, low = split(block)
    return dot(high, take) + dot(low, take)


def local_kernel(take_ref, put_ref, crosses_ref, wake_ref, low_ref, up_ref, inv_ref, rhs_ref, total_ref, keep_ref):
    put_even, put_odd = put_ref[0], put_ref[1]
    take_even, take_odd = take_ref[0], take_ref[1]
    ones = jnp.ones((wake_ref.shape[1], COLUMNS), BF16)
    spare = jnp.zeros((3 * TRACE, HALF - TRACE), F32)
    at = [slice(face * TRACE, (face + 1) * TRACE) for face in range(3)]

    def source(element):
        high, low = split(wake_ref[element])
        dims = (((0,), (0,)), ((), ()))
        wake = lax.dot_general(high, ones, dims, preferred_element_type=F32)
        wake += lax.dot_general(low, ones, dims, preferred_element_type=F32)
        return rhs_ref[element] + wake

    def put(onehot, rows):
        return sum(select_rows(onehot, split(rows)))

    crosses = [crosses_ref[face : face + 1, :1] > 0.5 for face in range(3)]

    def kept(values, crossing):
        return [jnp.where(cross == crossing, v, 0.0) for cross, v in zip(crosses, values)]

    def wide(values):
        return jnp.concatenate([jnp.concatenate(values, axis=0), spare], axis=1)

    from_first = put(put_even, wide([face_block(low_ref, 0, face) for face in range(3)]))
    blocks = [face_block(low_ref, 1, face) for face in range(3)]
    from_second = put(put_even, wide(kept(blocks, True)))
    inside = [expand(blocks[face], take_odd[at[face]]) for face in range(3)]
    down = left_parts(put(put_even, jnp.concatenate(kept(inside, False), axis=0)))
    inside = [expand(face_block(up_ref, 1, face), take_even[at[face]]) for face in range(3)]
    up = left_parts(put(put_odd, jnp.concatenate(kept(inside, False), axis=0)))
    leave_second = left_parts(sum(kept(inside, True)))
    leave_first = left_parts(expand(up_ref[0], take_even))

    inverse = left_parts(inv_ref[0])
    later_inverse = left_parts(inv_ref[1])
    first = long_product(inverse, right_parts(jnp.concatenate([-from_first, source(0)], axis=1)))

    side = put_odd[:, :HALF]
    lane = lax.broadcasted_iota(jnp.int32, (BLOCK, HALF), 1)
    high, low = split(inv_ref[1])
    returned = -(dot(high, side) + dot(low, side))
    returned = jnp.where(lane < TRACE, returned, 0.0)
    returned_pair = right_parts(returned)
    keep_ref[1, :, 2 * HALF :] = returned

    inner = long_product(down, right_parts(first))
    earlier = -long_product(inverse, right_parts(long_product(up, returned_pair)))
    keep_ref[0, :, 2 * HALF :] = earlier

    base = jnp.concatenate([-from_second, source(1)], axis=1)
    second = long_product(later_inverse, right_parts(base - inner))
    keep_ref[1, :, : 2 * HALF] = second
    second_pair = right_parts(second)
    back = long_product(leave_second, returned_pair) + long_product(leave_first, right_parts(earlier))
    inner = long_product(up, second_pair)
    first = first - long_product(inverse, right_parts(inner))
    keep_ref[0, :, : 2 * HALF] = first
    mixed = long_product(leave_second, second_pair) + long_product(leave_first, right_parts(first))
    total_ref[...] = pack(last_plane(second), None, mixed, back)


def is_upper(level):
    device = lax.axis_index("stream")
    if level == 0:
        return (device & 1) == 1
    chips = lax.axis_size("stream") // 2
    place = (device >> 1) + chips - OFFSET * (device & 1)
    return ((place >> (level - 1)) & 1) == 1


def combine_kernel(level, pair_ref, *refs):
    total_ref, state_ref = refs[-2:]
    forward1, mixed1, back1 = unpack(pair_ref[0])
    forward2, mixed2, back2 = unpack(pair_ref[1])
    lane = lax.broadcasted_iota(jnp.int32, (TRACE, 2 * HALF), 1)
    columns = lane >= HALF
    forward1 = jnp.where(columns | (lane < TRACE), forward1, 0.0)
    forward_pair = split(forward1)
    cross = product(split(mixed2[:, :TRACE]), forward_pair) + jnp.where(columns, mixed2, 0.0)
    forward = product(split(forward2[:, :TRACE]), forward_pair)
    forward = forward + jnp.where(columns, forward2, 0.0)
    back_pair = split(back1)
    mixed = mixed1 + product(back_pair, split(cross))
    back = product(back_pair, split(back2))
    if level == 0:
        chip = lax.axis_index("stream") >> 1
        begins, ends = chip == 0, chip == lax.axis_size("stream") // 2 - 1
        forward = jnp.where(ends | (begins & jnp.logical_not(columns)), 0.0, forward)
        mixed = jnp.where(begins, 0.0, mixed)
        back = jnp.where(begins | ends, 0.0, back)
    total_ref[...] = pack(forward, None, mixed, back)

    upper = is_upper(level)
    back2 = jnp.concatenate([back2, jnp.zeros((TRACE, HALF - TRACE), F32)], axis=1)
    if level == 0:
        row = lax.broadcasted_iota(jnp.int32, (TRACE, 2 * HALF), 0)
        eye = jnp.where(lane == row, 1.0, 0.0)
        state_ref[:, : 2 * HALF] = jnp.where(upper, forward1, eye)
        state_ref[:, 2 * HALF : 4 * HALF] = jnp.where(upper, 0.0, cross)
        state_ref[:, 4 * HALF :] = jnp.where(upper, eye[:, :HALF], back2)
        return
    old_ref = refs[0]

    @pl.when(upper)
    def _():
        here = old_ref[:, : 2 * HALF]
        back = old_ref[:, 2 * HALF : 4 * HALF]
        state_ref[:, : 2 * HALF] = product(split(here[:, :TRACE]), forward_pair) + jnp.where(columns, here, 0.0)
        state_ref[:, 2 * HALF : 4 * HALF] = product(split(back[:, :TRACE]), forward_pair) + jnp.where(columns, back, 0.0)
        state_ref[:, 4 * HALF :] = old_ref[:, 4 * HALF :]

    @pl.when(jnp.logical_not(upper))
    def _():
        gain = split(old_ref[:, 4 * HALF : 4 * HALF + TRACE])
        state_ref[:, : 2 * HALF] = old_ref[:, : 2 * HALF]
        state_ref[:, 2 * HALF : 4 * HALF] = old_ref[:, 2 * HALF : 4 * HALF] + product(gain, split(cross))
        state_ref[:, 4 * HALF :] = product(gain, split(back2))


def last_kernel(level, pair_ref, state_ref, keep_ref, out_ref):
    upper = is_upper(level)
    mine = unpack(jnp.where(upper, pair_ref[1], pair_ref[0]))
    other = unpack(jnp.where(upper, pair_ref[0], pair_ref[1]))

    def apply(matrix, value, added):
        return product(split(matrix[:, :TRACE]), split(value)) + added

    starts, other_starts = mine[0][:, HALF:], other[0][:, HALF:]
    inflow = apply(other[0], starts, other_starts)
    outflow = apply(mine[0], other_starts, starts)
    returned = apply(mine[1], inflow, mine[1][:, HALF:])
    incoming = apply(other[2], returned, apply(other[1], outflow, other[1][:, HALF:]))
    here = apply(state_ref[:, 2 * HALF : 3 * HALF], inflow, state_ref[:, 3 * HALF : 4 * HALF])
    incoming = split(apply(state_ref[:, 4 * HALF :], incoming, here))
    inflow = split(apply(state_ref[:, :HALF], inflow, state_ref[:, HALF : 2 * HALF]))
    for element in range(2):
        known = keep_ref[element]
        out_ref[element] = (
            known[:, HALF : 2 * HALF]
            + product(split(known[:, :TRACE]), inflow)
            + product(split(known[:, 2 * HALF : 2 * HALF + TRACE]), incoming)
        )


def call(kernel, shapes, operands, flops, specs=None, scratch=(), limit=8 * 1024):
    moved = 4 * sum(v.size for v in operands) + 4 * sum(s.size for s in shapes)
    single = len(shapes) == 1
    return pl.pallas_call(
        kernel,
        out_shape=shapes[0] if single else shapes,
        in_specs=specs or [VMEM] * len(operands),
        out_specs=VMEM if single else [VMEM] * len(shapes),
        scratch_shapes=list(scratch),
        compiler_params=pltpu.CompilerParams(vmem_limit_bytes=limit * 1024),
        cost_estimate=pl.CostEstimate(flops=flops, bytes_accessed=moved, transcendentals=0),
    )(*operands)


def shape(*dims):
    return jax.ShapeDtypeStruct(dims, F32)


OFFSET = 10
MASKS = (1, 2, 6, 8, 24)


def exchange(value, level):
    chips = lax.axis_size("stream") // 2
    if level == 0:
        groups = [[2 * chip, 2 * chip + 1] for chip in range(chips)]
    else:
        mask = MASKS[level - 1]
        groups = [
            [(place + OFFSET * core) % chips * 2 + core for place in (first, first ^ mask)]
            for core in range(2)
            for first in range(chips)
            if first < first ^ mask
        ]
    return lax.all_gather(value, "stream", axis_index_groups=groups)


def shards(rhs, inverse, lower, upper, upwind, rows, target):
    groups = lax.axis_size("azi")
    local = rhs.shape[0]
    top = len(MASKS)
    target = target.reshape(1, -1)
    rows, target, upwind = [pltpu.with_memory_space_constraint(v, pltpu.HBM) for v in (rows, target, upwind)]
    partial, crosses = call(
        wake_kernel,
        [shape(groups * local, BLOCK), shape(8, HALF)],
        [target, rows, upwind],
        10**10,
        specs=[HBM, HBM, HBM],
        scratch=[
            pltpu.VMEM(target.shape, jnp.int32),
            pltpu.VMEM(rows.shape, F32),
            pltpu.SMEM(upwind.shape, jnp.int32),
            pltpu.SemaphoreType.DMA((3,)),
        ],
    )
    parts = lax.all_to_all(partial.reshape(groups, local, BLOCK), "azi", 0, 0)
    parts = jnp.swapaxes(parts, 0, 1)
    total, keep = call(
        local_kernel,
        [shape(TRACE, 4 * HALF), shape(local, BLOCK, 3 * HALF)],
        [*face_rows(), crosses, parts, lower, upper, inverse, rhs],
        2 * 10**9,
        limit=24 * 1024,
    )
    state = []
    for level in range(top):
        total, after = call(
            functools.partial(combine_kernel, level),
            [shape(TRACE, 4 * HALF), shape(TRACE, 5 * HALF)],
            [exchange(total, level)] + state,
            3 * 10**7,
        )
        state = [after]
    return call(
        functools.partial(last_kernel, top),
        [shape(local, BLOCK, COLUMNS)],
        [exchange(total, top), state[0], keep],
        10**8,
    )


def solution(mesh):
    both = ("stream", "azi")
    return jax.shard_map(
        shards,
        mesh=mesh,
        in_specs=(
            P(both, None, None),
            P(both, None, None),
            P(both, None, None),
            P(both, None, None),
            P(both, None),
            P(both, None),
            P(both),
        ),
        out_specs=P(both, None, None),
        check_vma=False,
    )
```

```python
import functools

import jax
import jax.numpy as jnp
import numpy as np
from jax import lax
from jax.experimental import pallas as pl
from jax.experimental.pallas import tpu as pltpu
from jax.sharding import PartitionSpec as P

TRACE = 80
BLOCK = 320
COLUMNS = 128
PLANE = 16
CUBE = 64
HALF = 128
F32 = jnp.float32
BF16 = jnp.bfloat16
VMEM = pl.BlockSpec(memory_space=pltpu.VMEM)
SMEM = pl.BlockSpec(memory_space=pltpu.SMEM)
HBM = pl.BlockSpec(memory_space=pltpu.HBM)


def split(value):
    high = value.astype(BF16)
    return high, (value - high.astype(F32)).astype(BF16)


def dot(left, right):
    return jnp.dot(left, right, preferred_element_type=F32)


def product(left, right):
    return dot(left[0], right[0]) + (dot(left[0], right[1]) + dot(left[1], right[0]))


def select_rows(onehot, value):
    return dot(onehot, value[0]), dot(onehot, value[1])


def fetch(sources, buffers, sems):
    copies = [pltpu.make_async_copy(a, b, sems.at[i]) for i, (a, b) in enumerate(zip(sources, buffers))]
    for copy in copies:
        copy.start()
    return copies


def wake_kernel(target_hbm, rows_hbm, upwind_hbm, out_ref, crosses_ref, target_ref, rows_ref, upwind_ref, sems):
    for copy in fetch((target_hbm, rows_hbm, upwind_hbm), (target_ref, rows_ref, upwind_ref), sems):
        copy.wait()
    ids = lax.broadcasted_iota(jnp.int32, (out_ref.shape[0], target_ref.shape[1]), 0)
    onehot = jnp.where(ids == target_ref[...], 1.0, 0.0).astype(BF16)
    high, low = split(rows_ref[...])
    out_ref[...] = dot(onehot, high) + dot(onehot, low)
    face = lax.broadcasted_iota(jnp.int32, crosses_ref.shape, 0)
    crosses = jnp.zeros(crosses_ref.shape, F32)
    for at in range(3):
        crosses = jnp.where((face == at) & (upwind_ref[1, at] == 2), 1.0, crosses)
    crosses_ref[...] = crosses


def face_block(ref, element, face):
    return ref[element, :, face * TRACE : (face + 1) * TRACE]


def face_rows():
    trace = np.arange(TRACE)
    field, upper, lower = trace // PLANE, trace // 4 % 4, trace % 4
    take = np.zeros((2, 3 * TRACE, BLOCK), np.float32)
    for odd in range(2):
        side = 3 * odd
        places = (side * 16 + upper * 4 + lower, upper * 16 + side * 4 + lower, upper * 16 + lower * 4 + side)
        for face, place in enumerate(places):
            take[odd, face * TRACE + trace, field * CUBE + place] = 1.0
    return jnp.asarray(take, BF16), jnp.asarray(take.transpose(0, 2, 1), BF16)


WHOLE = 256


def left_parts(value):
    high, low = split(value)
    ends = [part[:, WHOLE:].astype(F32) for part in (high, low, high)]
    return high[:, :WHOLE], low[:, :WHOLE], jnp.concatenate(ends, axis=1).astype(BF16)


def right_parts(value):
    high, low = split(value)
    ends = [part[WHOLE:] for part in (high, high, low)]
    return high[:WHOLE], low[:WHOLE], jnp.concatenate(ends, axis=0)


def long_product(left, right):
    return (dot(left[0], right[0]) + dot(left[2], right[2])) + (dot(left[0], right[1]) + dot(left[1], right[0]))


def last_plane(value):
    return jnp.concatenate(
        [value[at + CUBE - PLANE : at + CUBE] for at in range(0, BLOCK, CUBE)], axis=0
    )


def pack(first, second, third, fourth):
    lead = TRACE
    spare = HALF - lead
    mid = third[:, :HALF]
    return jnp.concatenate(
        [
            first[:, :lead],
            mid[:, :spare],
            first[:, HALF:],
            fourth[:, :lead],
            mid[:, spare:lead],
            jnp.zeros((TRACE, 2 * spare - lead), F32),
            third[:, HALF:],
        ],
        axis=1,
    )


def unpack(value):
    lead = TRACE
    spare = HALF - lead
    zeros = jnp.zeros((TRACE, spare), F32)
    forward = value[:, : 2 * HALF]
    mixed = jnp.concatenate(
        [
            value[:, lead:HALF],
            value[:, 2 * HALF + lead : 2 * HALF + lead + (lead - spare)],
            zeros,
            value[:, 3 * HALF :],
        ],
        axis=1,
    )
    return forward, mixed, value[:, 2 * HALF : 2 * HALF + lead]


def expand(block, take):
    high, low = split(block)
    return dot(high, take) + dot(low, take)


def local_kernel(take_ref, put_ref, crosses_ref, wake_ref, low_ref, up_ref, inv_ref, rhs_ref, total_ref, keep_ref):
    put_even, put_odd = put_ref[0], put_ref[1]
    take_even, take_odd = take_ref[0], take_ref[1]
    ones = jnp.ones((wake_ref.shape[1], COLUMNS), BF16)
    spare = jnp.zeros((3 * TRACE, HALF - TRACE), F32)
    at = [slice(face * TRACE, (face + 1) * TRACE) for face in range(3)]

    def source(element):
        high, low = split(wake_ref[element])
        dims = (((0,), (0,)), ((), ()))
        wake = lax.dot_general(high, ones, dims, preferred_element_type=F32)
        wake += lax.dot_general(low, ones, dims, preferred_element_type=F32)
        return rhs_ref[element] + wake

    def put(onehot, rows):
        return sum(select_rows(onehot, split(rows)))

    crosses = [crosses_ref[face : face + 1, :1] > 0.5 for face in range(3)]

    def kept(values, crossing):
        return [jnp.where(cross == crossing, v, 0.0) for cross, v in zip(crosses, values)]

    def wide(values):
        return jnp.concatenate([jnp.concatenate(values, axis=0), spare], axis=1)

    from_first = put(put_even, wide([face_block(low_ref, 0, face) for face in range(3)]))
    blocks = [face_block(low_ref, 1, face) for face in range(3)]
    from_second = put(put_even, wide(kept(blocks, True)))
    inside = [expand(blocks[face], take_odd[at[face]]) for face in range(3)]
    down = left_parts(put(put_even, jnp.concatenate(kept(inside, False), axis=0)))
    inside = [expand(face_block(up_ref, 1, face), take_even[at[face]]) for face in range(3)]
    up = left_parts(put(put_odd, jnp.concatenate(kept(inside, False), axis=0)))
    leave_second = left_parts(sum(kept(inside, True)))
    leave_first = left_parts(expand(up_ref[0], take_even))

    inverse = left_parts(inv_ref[0])
    later_inverse = left_parts(inv_ref[1])
    first = long_product(inverse, right_parts(jnp.concatenate([-from_first, source(0)], axis=1)))

    side = put_odd[:, :HALF]
    lane = lax.broadcasted_iota(jnp.int32, (BLOCK, HALF), 1)
    high, low = split(inv_ref[1])
    returned = -(dot(high, side) + dot(low, side))
    returned = jnp.where(lane < TRACE, returned, 0.0)
    returned_pair = right_parts(returned)
    keep_ref[1, :, 2 * HALF :] = returned

    inner = long_product(down, right_parts(first))
    earlier = -long_product(inverse, right_parts(long_product(up, returned_pair)))
    keep_ref[0, :, 2 * HALF :] = earlier

    base = jnp.concatenate([-from_second, source(1)], axis=1)
    second = long_product(later_inverse, right_parts(base - inner))
    keep_ref[1, :, : 2 * HALF] = second
    second_pair = right_parts(second)
    back = long_product(leave_second, returned_pair) + long_product(leave_first, right_parts(earlier))
    inner = long_product(up, second_pair)
    first = first - long_product(inverse, right_parts(inner))
    keep_ref[0, :, : 2 * HALF] = first
    mixed = long_product(leave_second, second_pair) + long_product(leave_first, right_parts(first))
    total_ref[...] = pack(last_plane(second), None, mixed, back)


def is_upper(level):
    device = lax.axis_index("stream")
    if level == 0:
        return (device & 1) == 1
    chips = lax.axis_size("stream") // 2
    place = (device >> 1) + chips - OFFSET * (device & 1)
    return ((place >> (level - 1)) & 1) == 1


def combine_kernel(level, halves, pair_ref, *refs):
    total_ref, state_ref = refs[-2:]
    forward1, mixed1, back1 = unpack(pair_ref[0])
    forward2, mixed2, back2 = unpack(pair_ref[1])
    lane = lax.broadcasted_iota(jnp.int32, (TRACE, 2 * HALF), 1)
    columns = lane >= HALF
    forward1 = jnp.where(columns | (lane < TRACE), forward1, 0.0)
    forward_pair = split(forward1)
    cross = product(split(mixed2[:, :TRACE]), forward_pair) + jnp.where(columns, mixed2, 0.0)
    forward = product(split(forward2[:, :TRACE]), forward_pair)
    forward = forward + jnp.where(columns, forward2, 0.0)
    back_pair = split(back1)
    mixed = mixed1 + product(back_pair, split(cross))
    back = product(back_pair, split(back2))
    if level == 0:
        chip = lax.axis_index("stream") >> 1
        begins, ends = chip == 0, chip == lax.axis_size("stream") // 2 - 1
        forward = jnp.where(ends | (begins & jnp.logical_not(columns)), 0.0, forward)
        mixed = jnp.where(begins, 0.0, mixed)
        back = jnp.where(begins | ends, 0.0, back)
    total = pack(forward, None, mixed, back)
    if halves:
        half = TRACE // 2
        total = jnp.where((lax.axis_index("stream") & 1) == 1, total[half:], total[:half])
    total_ref[...] = total

    upper = is_upper(level)
    back2 = jnp.concatenate([back2, jnp.zeros((TRACE, HALF - TRACE), F32)], axis=1)
    if level == 0:
        row = lax.broadcasted_iota(jnp.int32, (TRACE, 2 * HALF), 0)
        eye = jnp.where(lane == row, 1.0, 0.0)
        state_ref[:, : 2 * HALF] = jnp.where(upper, forward1, eye)
        state_ref[:, 2 * HALF : 4 * HALF] = jnp.where(upper, 0.0, cross)
        state_ref[:, 4 * HALF :] = jnp.where(upper, eye[:, :HALF], back2)
        return
    old_ref = refs[0]

    @pl.when(upper)
    def _():
        here = old_ref[:, : 2 * HALF]
        back = old_ref[:, 2 * HALF : 4 * HALF]
        state_ref[:, : 2 * HALF] = product(split(here[:, :TRACE]), forward_pair) + jnp.where(columns, here, 0.0)
        state_ref[:, 2 * HALF : 4 * HALF] = product(split(back[:, :TRACE]), forward_pair) + jnp.where(columns, back, 0.0)
        state_ref[:, 4 * HALF :] = old_ref[:, 4 * HALF :]

    @pl.when(jnp.logical_not(upper))
    def _():
        gain = split(old_ref[:, 4 * HALF : 4 * HALF + TRACE])
        state_ref[:, : 2 * HALF] = old_ref[:, : 2 * HALF]
        state_ref[:, 2 * HALF : 4 * HALF] = old_ref[:, 2 * HALF : 4 * HALF] + product(gain, split(cross))
        state_ref[:, 4 * HALF :] = product(gain, split(back2))


def last_kernel(level, pair_ref, state_ref, keep_ref, out_ref):
    upper = is_upper(level)
    mine = unpack(jnp.where(upper, pair_ref[1], pair_ref[0]))
    other = unpack(jnp.where(upper, pair_ref[0], pair_ref[1]))

    def apply(matrix, value, added):
        return product(split(matrix[:, :TRACE]), split(value)) + added

    starts, other_starts = mine[0][:, HALF:], other[0][:, HALF:]
    inflow = apply(other[0], starts, other_starts)
    outflow = apply(mine[0], other_starts, starts)
    returned = apply(mine[1], inflow, mine[1][:, HALF:])
    incoming = apply(other[2], returned, apply(other[1], outflow, other[1][:, HALF:]))
    here = apply(state_ref[:, 2 * HALF : 3 * HALF], inflow, state_ref[:, 3 * HALF : 4 * HALF])
    incoming = split(apply(state_ref[:, 4 * HALF :], incoming, here))
    inflow = split(apply(state_ref[:, :HALF], inflow, state_ref[:, HALF : 2 * HALF]))
    for element in range(2):
        known = keep_ref[element]
        out_ref[element] = (
            known[:, HALF : 2 * HALF]
            + product(split(known[:, :TRACE]), inflow)
            + product(split(known[:, 2 * HALF : 2 * HALF + TRACE]), incoming)
        )


def call(kernel, shapes, operands, flops, specs=None, scratch=(), limit=8 * 1024):
    moved = 4 * sum(v.size for v in operands) + 4 * sum(s.size for s in shapes)
    single = len(shapes) == 1
    return pl.pallas_call(
        kernel,
        out_shape=shapes[0] if single else shapes,
        in_specs=specs or [VMEM] * len(operands),
        out_specs=VMEM if single else [VMEM] * len(shapes),
        scratch_shapes=list(scratch),
        compiler_params=pltpu.CompilerParams(vmem_limit_bytes=limit * 1024),
        cost_estimate=pl.CostEstimate(flops=flops, bytes_accessed=moved, transcendentals=0),
    )(*operands)


def shape(*dims):
    return jax.ShapeDtypeStruct(dims, F32)


OFFSET = 8
MASKS = (1, 2, 6, 8, 24)
HALVES = (2, 3)


def exchange(value, level):
    chips = lax.axis_size("stream") // 2
    mask = MASKS[level - 1] if level else 0
    pairs = [(first, first ^ mask) for first in range(chips) if first < first ^ mask]
    if level == 0:
        groups = [[2 * chip, 2 * chip + 1] for chip in range(chips)]
    elif level in HALVES:
        groups = [[2 * place + core for place in pair for core in range(2)] for pair in pairs]
    else:
        groups = [
            [(place + OFFSET * core) % chips * 2 + core for place in pair] for core in range(2) for pair in pairs
        ]
    gathered = lax.all_gather(value, "stream", axis_index_groups=groups)
    return gathered.reshape(2, TRACE, value.shape[-1])


def shards(rhs, inverse, lower, upper, upwind, rows, target):
    groups = lax.axis_size("azi")
    local = rhs.shape[0]
    top = len(MASKS)
    target = target.reshape(1, -1)
    rows, target, upwind = [pltpu.with_memory_space_constraint(v, pltpu.HBM) for v in (rows, target, upwind)]
    partial, crosses = call(
        wake_kernel,
        [shape(groups * local, BLOCK), shape(8, HALF)],
        [target, rows, upwind],
        10**10,
        specs=[HBM, HBM, HBM],
        scratch=[
            pltpu.VMEM(target.shape, jnp.int32),
            pltpu.VMEM(rows.shape, F32),
            pltpu.SMEM(upwind.shape, jnp.int32),
            pltpu.SemaphoreType.DMA((3,)),
        ],
    )
    parts = lax.all_to_all(partial.reshape(groups, local, BLOCK), "azi", 0, 0)
    parts = jnp.swapaxes(parts, 0, 1)
    total, keep = call(
        local_kernel,
        [shape(TRACE, 4 * HALF), shape(local, BLOCK, 3 * HALF)],
        [*face_rows(), crosses, parts, lower, upper, inverse, rhs],
        2 * 10**9,
        limit=24 * 1024,
    )
    state = []
    for level in range(top):
        halves = level + 1 in HALVES
        total, after = call(
            functools.partial(combine_kernel, level, halves),
            [shape(TRACE // 2 if halves else TRACE, 4 * HALF), shape(TRACE, 5 * HALF)],
            [exchange(total, level)] + state,
            3 * 10**7,
        )
        state = [after]
    return call(
        functools.partial(last_kernel, top),
        [shape(local, BLOCK, COLUMNS)],
        [exchange(total, top), state[0], keep],
        10**8,
    )


def solution(mesh):
    both = ("stream", "azi")
    return jax.shard_map(
        shards,
        mesh=mesh,
        in_specs=(
            P(both, None, None),
            P(both, None, None),
            P(both, None, None),
            P(both, None, None),
            P(both, None),
            P(both, None),
            P(both),
        ),
        out_specs=P(both, None, None),
        check_vma=False,
    )
```

```python
import functools

import jax
import jax.numpy as jnp
import numpy as np
from jax import lax
from jax.experimental import pallas as pl
from jax.experimental.pallas import tpu as pltpu
from jax.sharding import PartitionSpec as P

TRACE = 80
BLOCK = 320
COLUMNS = 128
PLANE = 16
CUBE = 64
HALF = 128
F32 = jnp.float32
BF16 = jnp.bfloat16
VMEM = pl.BlockSpec(memory_space=pltpu.VMEM)
SMEM = pl.BlockSpec(memory_space=pltpu.SMEM)
HBM = pl.BlockSpec(memory_space=pltpu.HBM)


def split(value):
    high = value.astype(BF16)
    return high, (value - high.astype(F32)).astype(BF16)


def dot(left, right):
    return jnp.dot(left, right, preferred_element_type=F32)


def product(left, right):
    return dot(left[0], right[0]) + (dot(left[0], right[1]) + dot(left[1], right[0]))


def select_rows(onehot, value):
    return dot(onehot, value[0]), dot(onehot, value[1])


def fetch(sources, buffers, sems):
    copies = [pltpu.make_async_copy(a, b, sems.at[i]) for i, (a, b) in enumerate(zip(sources, buffers))]
    for copy in copies:
        copy.start()
    return copies


def wake_kernel(target_hbm, rows_hbm, upwind_hbm, out_ref, crosses_ref, target_ref, rows_ref, upwind_ref, sems):
    for copy in fetch((target_hbm, rows_hbm, upwind_hbm), (target_ref, rows_ref, upwind_ref), sems):
        copy.wait()
    ids = lax.broadcasted_iota(jnp.int32, (out_ref.shape[0], target_ref.shape[1]), 0)
    onehot = jnp.where(ids == target_ref[...], 1.0, 0.0).astype(BF16)
    high, low = split(rows_ref[...])
    out_ref[...] = dot(onehot, high) + dot(onehot, low)
    face = lax.broadcasted_iota(jnp.int32, crosses_ref.shape, 0)
    crosses = jnp.zeros(crosses_ref.shape, F32)
    for at in range(3):
        crosses = jnp.where((face == at) & (upwind_ref[1, at] == 2), 1.0, crosses)
    crosses_ref[...] = crosses


def face_block(ref, element, face):
    return ref[element, :, face * TRACE : (face + 1) * TRACE]


def face_rows():
    trace = np.arange(TRACE)
    field, upper, lower = trace // PLANE, trace // 4 % 4, trace % 4
    take = np.zeros((2, 3 * TRACE, BLOCK), np.float32)
    for odd in range(2):
        side = 3 * odd
        places = (side * 16 + upper * 4 + lower, upper * 16 + side * 4 + lower, upper * 16 + lower * 4 + side)
        for face, place in enumerate(places):
            take[odd, face * TRACE + trace, field * CUBE + place] = 1.0
    return jnp.asarray(take, BF16), jnp.asarray(take.transpose(0, 2, 1), BF16)


WHOLE = 256


def left_parts(value):
    high, low = split(value)
    ends = [part[:, WHOLE:].astype(F32) for part in (high, low, high)]
    return high[:, :WHOLE], low[:, :WHOLE], jnp.concatenate(ends, axis=1).astype(BF16)


def right_parts(value):
    high, low = split(value)
    ends = [part[WHOLE:] for part in (high, high, low)]
    return high[:WHOLE], low[:WHOLE], jnp.concatenate(ends, axis=0)


def long_product(left, right):
    return (dot(left[0], right[0]) + dot(left[2], right[2])) + (dot(left[0], right[1]) + dot(left[1], right[0]))


def last_plane(value):
    return jnp.concatenate(
        [value[at + CUBE - PLANE : at + CUBE] for at in range(0, BLOCK, CUBE)], axis=0
    )


def pack(first, second, third, fourth):
    lead = TRACE
    spare = HALF - lead
    mid = third[:, :HALF]
    return jnp.concatenate(
        [
            first[:, :lead],
            mid[:, :spare],
            first[:, HALF:],
            fourth[:, :lead],
            mid[:, spare:lead],
            jnp.zeros((TRACE, 2 * spare - lead), F32),
            third[:, HALF:],
        ],
        axis=1,
    )


def unpack(value):
    lead = TRACE
    spare = HALF - lead
    zeros = jnp.zeros((TRACE, spare), F32)
    forward = value[:, : 2 * HALF]
    mixed = jnp.concatenate(
        [
            value[:, lead:HALF],
            value[:, 2 * HALF + lead : 2 * HALF + lead + (lead - spare)],
            zeros,
            value[:, 3 * HALF :],
        ],
        axis=1,
    )
    return forward, mixed, value[:, 2 * HALF : 2 * HALF + lead]


def expand(block, take):
    high, low = split(block)
    return dot(high, take) + dot(low, take)


def local_kernel(take_ref, put_ref, crosses_ref, wake_ref, low_ref, up_ref, inv_ref, rhs_ref, total_ref, keep_ref):
    put_even, put_odd = put_ref[0], put_ref[1]
    take_even, take_odd = take_ref[0], take_ref[1]
    ones = jnp.ones((wake_ref.shape[1], COLUMNS), BF16)
    spare = jnp.zeros((3 * TRACE, HALF - TRACE), F32)
    at = [slice(face * TRACE, (face + 1) * TRACE) for face in range(3)]

    def source(element):
        high, low = split(wake_ref[element])
        dims = (((0,), (0,)), ((), ()))
        wake = lax.dot_general(high, ones, dims, preferred_element_type=F32)
        wake += lax.dot_general(low, ones, dims, preferred_element_type=F32)
        return rhs_ref[element] + wake

    def put(onehot, rows):
        return sum(select_rows(onehot, split(rows)))

    crosses = [crosses_ref[face : face + 1, :1] > 0.5 for face in range(3)]

    def kept(values, crossing):
        return [jnp.where(cross == crossing, v, 0.0) for cross, v in zip(crosses, values)]

    def wide(values):
        return jnp.concatenate([jnp.concatenate(values, axis=0), spare], axis=1)

    from_first = put(put_even, wide([face_block(low_ref, 0, face) for face in range(3)]))
    blocks = [face_block(low_ref, 1, face) for face in range(3)]
    from_second = put(put_even, wide(kept(blocks, True)))
    inside = [expand(blocks[face], take_odd[at[face]]) for face in range(3)]
    down = left_parts(put(put_even, jnp.concatenate(kept(inside, False), axis=0)))
    inside = [expand(face_block(up_ref, 1, face), take_even[at[face]]) for face in range(3)]
    up = left_parts(put(put_odd, jnp.concatenate(kept(inside, False), axis=0)))
    leave_second = left_parts(sum(kept(inside, True)))
    leave_first = left_parts(expand(up_ref[0], take_even))

    inverse = left_parts(inv_ref[0])
    later_inverse = left_parts(inv_ref[1])
    first = long_product(inverse, right_parts(jnp.concatenate([-from_first, source(0)], axis=1)))

    side = put_odd[:, :HALF]
    lane = lax.broadcasted_iota(jnp.int32, (BLOCK, HALF), 1)
    high, low = split(inv_ref[1])
    returned = -(dot(high, side) + dot(low, side))
    returned = jnp.where(lane < TRACE, returned, 0.0)
    returned_pair = right_parts(returned)
    keep_ref[1, :, 2 * HALF :] = returned

    inner = long_product(down, right_parts(first))
    earlier = -long_product(inverse, right_parts(long_product(up, returned_pair)))
    keep_ref[0, :, 2 * HALF :] = earlier

    base = jnp.concatenate([-from_second, source(1)], axis=1)
    second = long_product(later_inverse, right_parts(base - inner))
    keep_ref[1, :, : 2 * HALF] = second
    second_pair = right_parts(second)
    back = long_product(leave_second, returned_pair) + long_product(leave_first, right_parts(earlier))
    inner = long_product(up, second_pair)
    first = first - long_product(inverse, right_parts(inner))
    keep_ref[0, :, : 2 * HALF] = first
    mixed = long_product(leave_second, second_pair) + long_product(leave_first, right_parts(first))
    total_ref[...] = pack(last_plane(second), None, mixed, back)


def is_upper(level):
    return (lax.axis_index("stream") >> level) & 1


def merge(run1, run2):
    forward1, mixed1, back1 = run1
    forward2, mixed2, back2 = run2
    lane = lax.broadcasted_iota(jnp.int32, (TRACE, 2 * HALF), 1)
    columns = lane >= HALF
    forward1 = jnp.where(columns | (lane < TRACE), forward1, 0.0)
    forward_pair = split(forward1)
    cross = product(split(mixed2[:, :TRACE]), forward_pair) + jnp.where(columns, mixed2, 0.0)
    forward = product(split(forward2[:, :TRACE]), forward_pair)
    forward = forward + jnp.where(columns, forward2, 0.0)
    back_pair = split(back1)
    mixed = mixed1 + product(back_pair, split(cross))
    back = product(back_pair, split(back2))
    back2 = jnp.concatenate([back2, jnp.zeros((TRACE, HALF - TRACE), F32)], axis=1)
    return (forward, mixed, back), (forward1, cross, back2)


def track(upper, pieces, old_ref, state_ref):
    forward1, cross, back2 = pieces
    columns = lax.broadcasted_iota(jnp.int32, (TRACE, 2 * HALF), 1) >= HALF

    @pl.when(upper)
    def _():
        forward_pair = split(forward1)
        here = old_ref[:, : 2 * HALF]
        back = old_ref[:, 2 * HALF : 4 * HALF]
        state_ref[:, : 2 * HALF] = product(split(here[:, :TRACE]), forward_pair) + jnp.where(columns, here, 0.0)
        state_ref[:, 2 * HALF : 4 * HALF] = product(split(back[:, :TRACE]), forward_pair) + jnp.where(columns, back, 0.0)
        state_ref[:, 4 * HALF :] = old_ref[:, 4 * HALF :]

    @pl.when(jnp.logical_not(upper))
    def _():
        gain = split(old_ref[:, 4 * HALF : 4 * HALF + TRACE])
        state_ref[:, : 2 * HALF] = old_ref[:, : 2 * HALF]
        state_ref[:, 2 * HALF : 4 * HALF] = old_ref[:, 2 * HALF : 4 * HALF] + product(gain, split(cross))
        state_ref[:, 4 * HALF :] = product(gain, split(back2))


def first_kernel(pair_ref, total_ref, half_ref, state_ref):
    upper = is_upper(0) == 1
    total, (forward1, cross, back2) = merge(unpack(pair_ref[0]), unpack(pair_ref[1]))
    total = pack(total[0], None, total[1], total[2])
    total_ref[...] = total
    half_ref[...] = jnp.where(upper, total[TRACE // 2 :], total[: TRACE // 2])
    lane = lax.broadcasted_iota(jnp.int32, (TRACE, 2 * HALF), 1)
    row = lax.broadcasted_iota(jnp.int32, (TRACE, 2 * HALF), 0)
    eye = jnp.where(lane == row, 1.0, 0.0)
    state_ref[:, : 2 * HALF] = jnp.where(upper, forward1, eye)
    state_ref[:, 2 * HALF : 4 * HALF] = jnp.where(upper, 0.0, cross)
    state_ref[:, 4 * HALF :] = jnp.where(upper, eye[:, :HALF], back2)


def four_kernel(own_ref, others_ref, old_ref, half_ref, state_ref, middle_ref):
    odd, late = is_upper(1) == 1, is_upper(2) == 1
    own, near, far = own_ref[...], others_ref[0, :TRACE], others_ref[1, :TRACE]
    middle = jnp.concatenate([others_ref[0, TRACE:], others_ref[1, TRACE:]], axis=0)

    def ordered(swap, one, two):
        return unpack(jnp.where(swap, two, one)), unpack(jnp.where(swap, one, two))

    mine, pieces = merge(*ordered(odd, own, near))
    other, _ = merge(*ordered(odd, middle, far))
    track(odd, pieces, old_ref, middle_ref)
    earlier = [jnp.where(late, b, a) for a, b in zip(mine, other)]
    later = [jnp.where(late, a, b) for a, b in zip(mine, other)]
    total, pieces = merge(earlier, later)
    total = pack(total[0], None, total[1], total[2])
    half_ref[...] = jnp.where(is_upper(0) == 1, total[TRACE // 2 :], total[: TRACE // 2])
    track(late, pieces, middle_ref, state_ref)


def combine_kernel(level, sends, pair_ref, old_ref, total_ref, state_ref):
    total, pieces = merge(unpack(pair_ref[0]), unpack(pair_ref[1]))
    if sends == "top":
        total_ref[...] = jnp.where(is_upper(level + 1) == 1, total[1], total[0])
    else:
        total_ref[...] = pack(total[0], None, total[1], total[2])
    track(is_upper(level) == 1, pieces, old_ref, state_ref)


def last_kernel(level, pair_ref, old_ref, keep_ref, out_ref, ends_ref):
    @pl.when(is_upper(level) == 1)
    def _():
        inflow = split(pair_ref[0, :, HALF:])
        ends_ref[0] = old_ref[:, HALF : 2 * HALF] + product(split(old_ref[:, :TRACE]), inflow)
        ends_ref[1] = old_ref[:, 3 * HALF : 4 * HALF] + product(split(old_ref[:, 2 * HALF : 2 * HALF + TRACE]), inflow)

    @pl.when(is_upper(level) == 0)
    def _():
        outflow = split(pair_ref[0, :, HALF:])
        value = pair_ref[1, :, HALF:] + product(split(pair_ref[1, :, :TRACE]), outflow)
        gain = split(old_ref[:, 4 * HALF : 4 * HALF + TRACE])
        ends_ref[0] = old_ref[:, HALF : 2 * HALF]
        ends_ref[1] = old_ref[:, 3 * HALF : 4 * HALF] + product(gain, split(value))

    inflow = split(ends_ref[0])
    incoming = split(ends_ref[1])
    for element in range(2):
        known = keep_ref[element]
        out_ref[element] = (
            known[:, HALF : 2 * HALF]
            + product(split(known[:, :TRACE]), inflow)
            + product(split(known[:, 2 * HALF : 2 * HALF + TRACE]), incoming)
        )


def call(kernel, shapes, operands, flops, specs=None, scratch=(), limit=8 * 1024):
    moved = 4 * sum(v.size for v in operands) + 4 * sum(s.size for s in shapes)
    single = len(shapes) == 1
    return pl.pallas_call(
        kernel,
        out_shape=shapes[0] if single else shapes,
        in_specs=specs or [VMEM] * len(operands),
        out_specs=VMEM if single else [VMEM] * len(shapes),
        scratch_shapes=list(scratch),
        compiler_params=pltpu.CompilerParams(vmem_limit_bytes=limit * 1024),
        cost_estimate=pl.CostEstimate(flops=flops, bytes_accessed=moved, transcendentals=0),
    )(*operands)


def shape(*dims):
    return jax.ShapeDtypeStruct(dims, F32)


def gather(value, masks):
    count = lax.axis_size("stream")
    masks = [(across * 8 + along) * 2 + core for across, along, core in masks]
    seen, groups = set(), []
    for device in range(count):
        if device in seen:
            continue
        group = {device}
        for mask in masks:
            group |= {member ^ mask for member in group}
        seen |= group
        groups.append(sorted(group))
    return lax.all_gather(value, "stream", axis_index_groups=groups)


def swap(value, along):
    count = lax.axis_size("stream")
    return lax.ppermute(value, "stream", [(k, k ^ (2 * along[k % 2])) for k in range(count)])


def shards(rhs, inverse, lower, upper, upwind, rows, target):
    groups = lax.axis_size("azi")
    local = rhs.shape[0]
    target = target.reshape(1, -1)
    rows, target, upwind = [pltpu.with_memory_space_constraint(v, pltpu.HBM) for v in (rows, target, upwind)]
    partial, crosses = call(
        wake_kernel,
        [shape(groups * local, BLOCK), shape(8, HALF)],
        [target, rows, upwind],
        10**10,
        specs=[HBM, HBM, HBM],
        scratch=[
            pltpu.VMEM(target.shape, jnp.int32),
            pltpu.VMEM(rows.shape, F32),
            pltpu.SMEM(upwind.shape, jnp.int32),
            pltpu.SemaphoreType.DMA((3,)),
        ],
    )
    parts = lax.all_to_all(partial.reshape(groups, local, BLOCK), "azi", 0, 0)
    parts = jnp.swapaxes(parts, 0, 1)
    total, keep = call(
        local_kernel,
        [shape(TRACE, 4 * HALF), shape(local, BLOCK, 3 * HALF)],
        [*face_rows(), crosses, parts, lower, upper, inverse, rhs],
        2 * 10**9,
        limit=24 * 1024,
    )
    full, half, state = shape(TRACE, 4 * HALF), shape(TRACE // 2, 4 * HALF), shape(TRACE, 5 * HALF)
    total, part, tracked = call(first_kernel, [full, half, state], [gather(total, [(0, 0, 1)])], 3 * 10**7)
    received = jnp.concatenate([swap(total, (1, 3)), swap(part, (2, 2))], axis=0)
    received = gather(received, [(0, 0, 1)])
    part, tracked = call(
        four_kernel,
        [half, state],
        [total, received, tracked],
        10**8,
        scratch=[pltpu.VMEM((TRACE, 5 * HALF), F32)],
    )
    pair = gather(part, [(0, 0, 1), (0, 6, 0)]).reshape(2, TRACE, 4 * HALF)
    total, tracked = call(functools.partial(combine_kernel, 3, "whole"), [full, state], [pair, tracked], 3 * 10**7)
    pair = gather(total, [(1, 0, 0)])
    crossing = shape(TRACE, 2 * HALF)
    total, tracked = call(functools.partial(combine_kernel, 4, "top"), [crossing, state], [pair, tracked], 3 * 10**7)
    return call(
        functools.partial(last_kernel, 5),
        [shape(local, BLOCK, COLUMNS)],
        [gather(total, [(3, 0, 0)]), tracked, keep],
        10**8,
        scratch=[pltpu.VMEM((2, TRACE, COLUMNS), F32)],
    )


def solution(mesh):
    both = ("stream", "azi")
    return jax.shard_map(
        shards,
        mesh=mesh,
        in_specs=(
            P(both, None, None),
            P(both, None, None),
            P(both, None, None),
            P(both, None, None),
            P(both, None),
            P(both, None),
            P(both),
        ),
        out_specs=P(both, None, None),
        check_vma=False,
    )
```

```python
import functools

import jax
import jax.numpy as jnp
import numpy as np
from jax import lax
from jax.experimental import pallas as pl
from jax.experimental.pallas import tpu as pltpu
from jax.sharding import PartitionSpec as P

TRACE = 80
BLOCK = 320
COLUMNS = 128
PLANE = 16
CUBE = 64
HALF = 128
F32 = jnp.float32
BF16 = jnp.bfloat16
VMEM = pl.BlockSpec(memory_space=pltpu.VMEM)
SMEM = pl.BlockSpec(memory_space=pltpu.SMEM)
HBM = pl.BlockSpec(memory_space=pltpu.HBM)


def split(value):
    high = value.astype(BF16)
    return high, (value - high.astype(F32)).astype(BF16)


def dot(left, right):
    return jnp.dot(left, right, preferred_element_type=F32)


def product(left, right):
    return dot(left[0], right[0]) + (dot(left[0], right[1]) + dot(left[1], right[0]))


def select_rows(onehot, value):
    return dot(onehot, value[0]), dot(onehot, value[1])


def fetch(sources, buffers, sems):
    copies = [pltpu.make_async_copy(a, b, sems.at[i]) for i, (a, b) in enumerate(zip(sources, buffers))]
    for copy in copies:
        copy.start()
    return copies


def wake_kernel(target_hbm, rows_hbm, upwind_hbm, out_ref, crosses_ref, target_ref, rows_ref, upwind_ref, sems):
    for copy in fetch((target_hbm, rows_hbm, upwind_hbm), (target_ref, rows_ref, upwind_ref), sems):
        copy.wait()
    ids = lax.broadcasted_iota(jnp.int32, (out_ref.shape[0], target_ref.shape[1]), 0)
    onehot = jnp.where(ids == target_ref[...], 1.0, 0.0).astype(BF16)
    high, low = split(rows_ref[...])
    out_ref[...] = dot(onehot, high) + dot(onehot, low)
    face = lax.broadcasted_iota(jnp.int32, crosses_ref.shape, 0)
    crosses = jnp.zeros(crosses_ref.shape, F32)
    for at in range(3):
        crosses = jnp.where((face == at) & (upwind_ref[1, at] == 2), 1.0, crosses)
    crosses_ref[...] = crosses


def face_block(ref, element, face):
    return ref[element, :, face * TRACE : (face + 1) * TRACE]


def face_rows():
    trace = np.arange(TRACE)
    field, upper, lower = trace // PLANE, trace // 4 % 4, trace % 4
    take = np.zeros((2, 3 * TRACE, BLOCK), np.float32)
    for odd in range(2):
        side = 3 * odd
        places = (side * 16 + upper * 4 + lower, upper * 16 + side * 4 + lower, upper * 16 + lower * 4 + side)
        for face, place in enumerate(places):
            take[odd, face * TRACE + trace, field * CUBE + place] = 1.0
    return jnp.asarray(take, BF16), jnp.asarray(take.transpose(0, 2, 1), BF16)


WHOLE = 256


def left_parts(value):
    high, low = split(value)
    ends = [part[:, WHOLE:].astype(F32) for part in (high, low, high)]
    return high[:, :WHOLE], low[:, :WHOLE], jnp.concatenate(ends, axis=1).astype(BF16)


def right_parts(value):
    high, low = split(value)
    ends = [part[WHOLE:] for part in (high, high, low)]
    return high[:WHOLE], low[:WHOLE], jnp.concatenate(ends, axis=0)


def long_product(left, right):
    return (dot(left[0], right[0]) + dot(left[2], right[2])) + (dot(left[0], right[1]) + dot(left[1], right[0]))


def last_plane(value):
    return jnp.concatenate(
        [value[at + CUBE - PLANE : at + CUBE] for at in range(0, BLOCK, CUBE)], axis=0
    )


def pack(first, second, third, fourth):
    lead = TRACE
    spare = HALF - lead
    mid = third[:, :HALF]
    return jnp.concatenate(
        [
            first[:, :lead],
            mid[:, :spare],
            first[:, HALF:],
            fourth[:, :lead],
            mid[:, spare:lead],
            jnp.zeros((TRACE, 2 * spare - lead), F32),
            third[:, HALF:],
        ],
        axis=1,
    )


def unpack(value):
    lead = TRACE
    spare = HALF - lead
    zeros = jnp.zeros((TRACE, spare), F32)
    forward = value[:, : 2 * HALF]
    mixed = jnp.concatenate(
        [
            value[:, lead:HALF],
            value[:, 2 * HALF + lead : 2 * HALF + lead + (lead - spare)],
            zeros,
            value[:, 3 * HALF :],
        ],
        axis=1,
    )
    return forward, mixed, value[:, 2 * HALF : 2 * HALF + lead]


def expand(block, take):
    high, low = split(block)
    return dot(high, take) + dot(low, take)


def local_kernel(take_ref, put_ref, crosses_ref, wake_ref, low_ref, up_ref, inv_ref, rhs_ref, total_ref, keep_ref):
    put_even, put_odd = put_ref[0], put_ref[1]
    take_even, take_odd = take_ref[0], take_ref[1]
    ones = jnp.ones((wake_ref.shape[1], COLUMNS), BF16)
    spare = jnp.zeros((3 * TRACE, HALF - TRACE), F32)
    at = [slice(face * TRACE, (face + 1) * TRACE) for face in range(3)]

    def source(element):
        high, low = split(wake_ref[element])
        dims = (((0,), (0,)), ((), ()))
        wake = lax.dot_general(high, ones, dims, preferred_element_type=F32)
        wake += lax.dot_general(low, ones, dims, preferred_element_type=F32)
        return rhs_ref[element] + wake

    def put(onehot, rows):
        return sum(select_rows(onehot, split(rows)))

    crosses = [crosses_ref[face : face + 1, :1] > 0.5 for face in range(3)]

    def kept(values, crossing):
        return [jnp.where(cross == crossing, v, 0.0) for cross, v in zip(crosses, values)]

    def wide(values):
        return jnp.concatenate([jnp.concatenate(values, axis=0), spare], axis=1)

    from_first = put(put_even, wide([face_block(low_ref, 0, face) for face in range(3)]))
    blocks = [face_block(low_ref, 1, face) for face in range(3)]
    from_second = put(put_even, wide(kept(blocks, True)))
    inside = [expand(blocks[face], take_odd[at[face]]) for face in range(3)]
    down = left_parts(put(put_even, jnp.concatenate(kept(inside, False), axis=0)))
    inside = [expand(face_block(up_ref, 1, face), take_even[at[face]]) for face in range(3)]
    up = left_parts(put(put_odd, jnp.concatenate(kept(inside, False), axis=0)))
    leave_second = left_parts(sum(kept(inside, True)))
    leave_first = left_parts(expand(up_ref[0], take_even))

    inverse = left_parts(inv_ref[0])
    later_inverse = left_parts(inv_ref[1])
    first = long_product(inverse, right_parts(jnp.concatenate([-from_first, source(0)], axis=1)))

    side = put_odd[:, :HALF]
    lane = lax.broadcasted_iota(jnp.int32, (BLOCK, HALF), 1)
    high, low = split(inv_ref[1])
    returned = -(dot(high, side) + dot(low, side))
    returned = jnp.where(lane < TRACE, returned, 0.0)
    returned_pair = right_parts(returned)
    keep_ref[1, :, 2 * HALF :] = returned

    inner = long_product(down, right_parts(first))
    earlier = -long_product(inverse, right_parts(long_product(up, returned_pair)))
    keep_ref[0, :, 2 * HALF :] = earlier

    base = jnp.concatenate([-from_second, source(1)], axis=1)
    second = long_product(later_inverse, right_parts(base - inner))
    keep_ref[1, :, : 2 * HALF] = second
    second_pair = right_parts(second)
    back = long_product(leave_second, returned_pair) + long_product(leave_first, right_parts(earlier))
    inner = long_product(up, second_pair)
    first = first - long_product(inverse, right_parts(inner))
    keep_ref[0, :, : 2 * HALF] = first
    mixed = long_product(leave_second, second_pair) + long_product(leave_first, right_parts(first))
    total_ref[...] = pack(last_plane(second), None, mixed, back)


def is_upper(level):
    return (lax.axis_index("stream") >> level) & 1


def merge(run1, run2):
    forward1, mixed1, back1 = run1
    forward2, mixed2, back2 = run2
    lane = lax.broadcasted_iota(jnp.int32, (TRACE, 2 * HALF), 1)
    columns = lane >= HALF
    forward1 = jnp.where(columns | (lane < TRACE), forward1, 0.0)
    forward_pair = split(forward1)
    cross = product(split(mixed2[:, :TRACE]), forward_pair) + jnp.where(columns, mixed2, 0.0)
    forward = product(split(forward2[:, :TRACE]), forward_pair)
    forward = forward + jnp.where(columns, forward2, 0.0)
    back_pair = split(back1)
    mixed = mixed1 + product(back_pair, split(cross))
    back = product(back_pair, split(back2))
    back2 = jnp.concatenate([back2, jnp.zeros((TRACE, HALF - TRACE), F32)], axis=1)
    return (forward, mixed, back), (forward1, cross, back2)


def track(upper, pieces, old_ref, state_ref):
    forward1, cross, back2 = pieces
    columns = lax.broadcasted_iota(jnp.int32, (TRACE, 2 * HALF), 1) >= HALF

    @pl.when(upper)
    def _():
        forward_pair = split(forward1)
        here = old_ref[:, : 2 * HALF]
        back = old_ref[:, 2 * HALF : 4 * HALF]
        state_ref[:, : 2 * HALF] = product(split(here[:, :TRACE]), forward_pair) + jnp.where(columns, here, 0.0)
        state_ref[:, 2 * HALF : 4 * HALF] = product(split(back[:, :TRACE]), forward_pair) + jnp.where(columns, back, 0.0)
        state_ref[:, 4 * HALF :] = old_ref[:, 4 * HALF :]

    @pl.when(jnp.logical_not(upper))
    def _():
        gain = split(old_ref[:, 4 * HALF : 4 * HALF + TRACE])
        state_ref[:, : 2 * HALF] = old_ref[:, : 2 * HALF]
        state_ref[:, 2 * HALF : 4 * HALF] = old_ref[:, 2 * HALF : 4 * HALF] + product(gain, split(cross))
        state_ref[:, 4 * HALF :] = product(gain, split(back2))


def spread_half(total, half_ref):
    packed = pack(total[0], None, total[1], total[2])
    half = TRACE // 2
    packed = jnp.where(is_upper(0) == 1, packed[half:], packed[:half])
    for chip in range(half_ref.shape[0]):
        half_ref[chip] = packed


def run_of(halves_ref, chip):
    return unpack(jnp.concatenate([halves_ref[0, chip], halves_ref[1, chip]], axis=0))


def first_kernel(pair_ref, half_ref, state_ref):
    upper = is_upper(0) == 1
    total, (forward1, cross, back2) = merge(unpack(pair_ref[0]), unpack(pair_ref[1]))
    spread_half(total, half_ref)
    lane = lax.broadcasted_iota(jnp.int32, (TRACE, 2 * HALF), 1)
    row = lax.broadcasted_iota(jnp.int32, (TRACE, 2 * HALF), 0)
    eye = jnp.where(lane == row, 1.0, 0.0)
    state_ref[:, : 2 * HALF] = jnp.where(upper, forward1, eye)
    state_ref[:, 2 * HALF : 4 * HALF] = jnp.where(upper, 0.0, cross)
    state_ref[:, 4 * HALF :] = jnp.where(upper, eye[:, :HALF], back2)


def four_kernel(halves_ref, old_ref, half_ref, state_ref, middle_ref):
    odd, late = is_upper(1) == 1, is_upper(2) == 1
    front, front_pieces = merge(run_of(halves_ref, 0), run_of(halves_ref, 1))
    rear, rear_pieces = merge(run_of(halves_ref, 2), run_of(halves_ref, 3))
    total, pieces = merge(front, rear)
    total = pack(total[0], None, total[1], total[2])
    half_ref[...] = jnp.where(is_upper(0) == 1, total[TRACE // 2 :], total[: TRACE // 2])
    track(odd, [jnp.where(late, b, a) for a, b in zip(front_pieces, rear_pieces)], old_ref, middle_ref)
    track(late, pieces, middle_ref, state_ref)


def combine_kernel(level, pair_ref, old_ref, half_ref, state_ref):
    total, pieces = merge(unpack(pair_ref[0]), unpack(pair_ref[1]))
    spread_half(total, half_ref)
    track(is_upper(level) == 1, pieces, old_ref, state_ref)


def last_kernel(level, halves_ref, state_ref, keep_ref, out_ref):
    mine = lax.axis_index("stream") >> level
    runs = [run_of(halves_ref, line) for line in range(4)]

    def apply(matrix, value, added):
        return product(split(matrix[:, :TRACE]), split(value)) + added

    zeros = jnp.zeros((TRACE, COLUMNS), F32)
    flow = [zeros, runs[0][0][:, HALF:]]
    for line in (1, 2):
        flow.append(apply(runs[line][0], flow[line], runs[line][0][:, HALF:]))
    back = [zeros]
    for line in (3, 2, 1):
        value = apply(runs[line][1], flow[line], runs[line][1][:, HALF:])
        back.insert(0, value if line == 3 else apply(runs[line][2], back[0], value))
    inflow, incoming = flow[0], back[0]
    for line in (1, 2, 3):
        inflow = jnp.where(mine == line, flow[line], inflow)
        incoming = jnp.where(mine == line, back[line], incoming)
    here = apply(state_ref[:, 2 * HALF : 3 * HALF], inflow, state_ref[:, 3 * HALF : 4 * HALF])
    incoming = split(apply(state_ref[:, 4 * HALF :], incoming, here))
    inflow = split(apply(state_ref[:, :HALF], inflow, state_ref[:, HALF : 2 * HALF]))
    for element in range(2):
        known = keep_ref[element]
        out_ref[element] = (
            known[:, HALF : 2 * HALF]
            + product(split(known[:, :TRACE]), inflow)
            + product(split(known[:, 2 * HALF : 2 * HALF + TRACE]), incoming)
        )


def call(kernel, shapes, operands, flops, specs=None, scratch=(), limit=8 * 1024):
    moved = 4 * sum(v.size for v in operands) + 4 * sum(s.size for s in shapes)
    single = len(shapes) == 1
    return pl.pallas_call(
        kernel,
        out_shape=shapes[0] if single else shapes,
        in_specs=specs or [VMEM] * len(operands),
        out_specs=VMEM if single else [VMEM] * len(shapes),
        scratch_shapes=list(scratch),
        compiler_params=pltpu.CompilerParams(vmem_limit_bytes=limit * 1024),
        cost_estimate=pl.CostEstimate(flops=flops, bytes_accessed=moved, transcendentals=0),
    )(*operands)


def shape(*dims):
    return jax.ShapeDtypeStruct(dims, F32)


def groups_of(masks):
    masks = [(across * 8 + along) * 2 + core for across, along, core in masks]
    seen, groups = set(), []
    for device in range(lax.axis_size("stream")):
        if device in seen:
            continue
        group = {device}
        for mask in masks:
            group |= {member ^ mask for member in group}
        seen |= group
        groups.append(sorted(group))
    return groups


def gather(value, masks):
    return lax.all_gather(value, "stream", axis_index_groups=groups_of(masks))


def share(halves, masks):
    halves = lax.all_to_all(halves, "stream", 0, 0, axis_index_groups=groups_of(masks))
    return gather(halves, [(0, 0, 1)])


def shards(rhs, inverse, lower, upper, upwind, rows, target):
    groups = lax.axis_size("azi")
    local = rhs.shape[0]
    target = target.reshape(1, -1)
    rows, target, upwind = [pltpu.with_memory_space_constraint(v, pltpu.HBM) for v in (rows, target, upwind)]
    partial, crosses = call(
        wake_kernel,
        [shape(groups * local, BLOCK), shape(8, HALF)],
        [target, rows, upwind],
        10**10,
        specs=[HBM, HBM, HBM],
        scratch=[
            pltpu.VMEM(target.shape, jnp.int32),
            pltpu.VMEM(rows.shape, F32),
            pltpu.SMEM(upwind.shape, jnp.int32),
            pltpu.SemaphoreType.DMA((3,)),
        ],
    )
    parts = lax.all_to_all(partial.reshape(groups, local, BLOCK), "azi", 0, 0)
    parts = jnp.swapaxes(parts, 0, 1)
    total, keep = call(
        local_kernel,
        [shape(TRACE, 4 * HALF), shape(local, BLOCK, 3 * HALF)],
        [*face_rows(), crosses, parts, lower, upper, inverse, rhs],
        2 * 10**9,
        limit=24 * 1024,
    )
    half, state = shape(TRACE // 2, 4 * HALF), shape(TRACE, 5 * HALF)
    halves = shape(4, TRACE // 2, 4 * HALF)
    parts, tracked = call(first_kernel, [halves, state], [gather(total, [(0, 0, 1)])], 3 * 10**7)
    part, tracked = call(
        four_kernel,
        [half, state],
        [share(parts, [(0, 1, 0), (0, 2, 0)]), tracked],
        10**8,
        scratch=[pltpu.VMEM((TRACE, 5 * HALF), F32)],
    )
    pair = gather(part, [(0, 0, 1), (0, 6, 0)]).reshape(2, TRACE, 4 * HALF)
    parts, tracked = call(functools.partial(combine_kernel, 3), [halves, state], [pair, tracked], 3 * 10**7)
    return call(
        functools.partial(last_kernel, 4),
        [shape(local, BLOCK, COLUMNS)],
        [share(parts, [(1, 0, 0), (2, 0, 0)]), tracked, keep],
        10**8,
    )


def solution(mesh):
    both = ("stream", "azi")
    return jax.shard_map(
        shards,
        mesh=mesh,
        in_specs=(
            P(both, None, None),
            P(both, None, None),
            P(both, None, None),
            P(both, None, None),
            P(both, None),
            P(both, None),
            P(both),
        ),
        out_specs=P(both, None, None),
        check_vma=False,
    )
```

```python
import functools

import jax
import jax.numpy as jnp
import numpy as np
from jax import lax
from jax.experimental import pallas as pl
from jax.experimental.pallas import tpu as pltpu
from jax.sharding import PartitionSpec as P

TRACE = 80
BLOCK = 320
COLUMNS = 128
PLANE = 16
CUBE = 64
HALF = 128
F32 = jnp.float32
BF16 = jnp.bfloat16
VMEM = pl.BlockSpec(memory_space=pltpu.VMEM)
SMEM = pl.BlockSpec(memory_space=pltpu.SMEM)
HBM = pl.BlockSpec(memory_space=pltpu.HBM)


def split(value):
    high = value.astype(BF16)
    return high, (value - high.astype(F32)).astype(BF16)


def dot(left, right):
    return jnp.dot(left, right, preferred_element_type=F32)


def product(left, right):
    return dot(left[0], right[0]) + (dot(left[0], right[1]) + dot(left[1], right[0]))


def select_rows(onehot, value):
    return dot(onehot, value[0]), dot(onehot, value[1])


def fetch(sources, buffers, sems):
    copies = [pltpu.make_async_copy(a, b, sems.at[i]) for i, (a, b) in enumerate(zip(sources, buffers))]
    for copy in copies:
        copy.start()
    return copies


def wake_kernel(target_hbm, rows_hbm, upwind_hbm, out_ref, crosses_ref, target_ref, rows_ref, upwind_ref, sems):
    for copy in fetch((target_hbm, rows_hbm, upwind_hbm), (target_ref, rows_ref, upwind_ref), sems):
        copy.wait()
    ids = lax.broadcasted_iota(jnp.int32, (out_ref.shape[0], target_ref.shape[1]), 0)
    onehot = jnp.where(ids == target_ref[...], 1.0, 0.0).astype(BF16)
    high, low = split(rows_ref[...])
    out_ref[...] = dot(onehot, high) + dot(onehot, low)
    face = lax.broadcasted_iota(jnp.int32, crosses_ref.shape, 0)
    crosses = jnp.zeros(crosses_ref.shape, F32)
    for at in range(3):
        crosses = jnp.where((face == at) & (upwind_ref[1, at] == 2), 1.0, crosses)
    crosses_ref[...] = crosses


def face_block(ref, element, face):
    return ref[element, :, face * TRACE : (face + 1) * TRACE]


def face_rows():
    trace = np.arange(TRACE)
    field, upper, lower = trace // PLANE, trace // 4 % 4, trace % 4
    take = np.zeros((2, 3 * TRACE, BLOCK), np.float32)
    for odd in range(2):
        side = 3 * odd
        places = (side * 16 + upper * 4 + lower, upper * 16 + side * 4 + lower, upper * 16 + lower * 4 + side)
        for face, place in enumerate(places):
            take[odd, face * TRACE + trace, field * CUBE + place] = 1.0
    return jnp.asarray(take, BF16), jnp.asarray(take.transpose(0, 2, 1), BF16)


WHOLE = 256


def left_parts(value):
    high, low = split(value)
    ends = [part[:, WHOLE:].astype(F32) for part in (high, low, high)]
    return high[:, :WHOLE], low[:, :WHOLE], jnp.concatenate(ends, axis=1).astype(BF16)


def right_parts(value):
    high, low = split(value)
    ends = [part[WHOLE:] for part in (high, high, low)]
    return high[:WHOLE], low[:WHOLE], jnp.concatenate(ends, axis=0)


def long_product(left, right):
    return (dot(left[0], right[0]) + dot(left[2], right[2])) + (dot(left[0], right[1]) + dot(left[1], right[0]))


def last_plane(value):
    return jnp.concatenate(
        [value[at + CUBE - PLANE : at + CUBE] for at in range(0, BLOCK, CUBE)], axis=0
    )


def pack(first, second, third, fourth):
    lead = TRACE
    spare = HALF - lead
    mid = third[:, :HALF]
    return jnp.concatenate(
        [
            first[:, :lead],
            mid[:, :spare],
            first[:, HALF:],
            fourth[:, :lead],
            mid[:, spare:lead],
            jnp.zeros((TRACE, 2 * spare - lead), F32),
            third[:, HALF:],
        ],
        axis=1,
    )


def unpack(value):
    lead = TRACE
    spare = HALF - lead
    zeros = jnp.zeros((TRACE, spare), F32)
    forward = value[:, : 2 * HALF]
    mixed = jnp.concatenate(
        [
            value[:, lead:HALF],
            value[:, 2 * HALF + lead : 2 * HALF + lead + (lead - spare)],
            zeros,
            value[:, 3 * HALF :],
        ],
        axis=1,
    )
    return forward, mixed, value[:, 2 * HALF : 2 * HALF + lead]


def expand(block, take):
    high, low = split(block)
    return dot(high, take) + dot(low, take)


def local_kernel(take_ref, put_ref, crosses_ref, wake_ref, low_ref, up_ref, inv_ref, rhs_ref, total_ref, keep_ref):
    put_even, put_odd = put_ref[0], put_ref[1]
    take_even, take_odd = take_ref[0], take_ref[1]
    ones = jnp.ones((wake_ref.shape[1], COLUMNS), BF16)
    spare = jnp.zeros((3 * TRACE, HALF - TRACE), F32)
    at = [slice(face * TRACE, (face + 1) * TRACE) for face in range(3)]

    def source(element):
        high, low = split(wake_ref[element])
        dims = (((0,), (0,)), ((), ()))
        wake = lax.dot_general(high, ones, dims, preferred_element_type=F32)
        wake += lax.dot_general(low, ones, dims, preferred_element_type=F32)
        return rhs_ref[element] + wake

    def put(onehot, rows):
        return sum(select_rows(onehot, split(rows)))

    crosses = [crosses_ref[face : face + 1, :1] > 0.5 for face in range(3)]

    def kept(values, crossing):
        return [jnp.where(cross == crossing, v, 0.0) for cross, v in zip(crosses, values)]

    def wide(values):
        return jnp.concatenate([jnp.concatenate(values, axis=0), spare], axis=1)

    from_first = put(put_even, wide([face_block(low_ref, 0, face) for face in range(3)]))
    blocks = [face_block(low_ref, 1, face) for face in range(3)]
    from_second = put(put_even, wide(kept(blocks, True)))
    inside = [expand(blocks[face], take_odd[at[face]]) for face in range(3)]
    down = left_parts(put(put_even, jnp.concatenate(kept(inside, False), axis=0)))
    inside = [expand(face_block(up_ref, 1, face), take_even[at[face]]) for face in range(3)]
    up = left_parts(put(put_odd, jnp.concatenate(kept(inside, False), axis=0)))
    leave_second = left_parts(sum(kept(inside, True)))
    leave_first = left_parts(expand(up_ref[0], take_even))

    inverse = left_parts(inv_ref[0])
    later_inverse = left_parts(inv_ref[1])
    first = long_product(inverse, right_parts(jnp.concatenate([-from_first, source(0)], axis=1)))

    side = put_odd[:, :HALF]
    lane = lax.broadcasted_iota(jnp.int32, (BLOCK, HALF), 1)
    high, low = split(inv_ref[1])
    returned = -(dot(high, side) + dot(low, side))
    returned = jnp.where(lane < TRACE, returned, 0.0)
    returned_pair = right_parts(returned)
    keep_ref[1, :, 2 * HALF :] = returned

    inner = long_product(down, right_parts(first))
    earlier = -long_product(inverse, right_parts(long_product(up, returned_pair)))
    keep_ref[0, :, 2 * HALF :] = earlier

    base = jnp.concatenate([-from_second, source(1)], axis=1)
    second = long_product(later_inverse, right_parts(base - inner))
    keep_ref[1, :, : 2 * HALF] = second
    second_pair = right_parts(second)
    back = long_product(leave_second, returned_pair) + long_product(leave_first, right_parts(earlier))
    inner = long_product(up, second_pair)
    first = first - long_product(inverse, right_parts(inner))
    keep_ref[0, :, : 2 * HALF] = first
    mixed = long_product(leave_second, second_pair) + long_product(leave_first, right_parts(first))
    total_ref[...] = pack(last_plane(second), None, mixed, back)


def is_upper(level):
    return (lax.axis_index("stream") >> level) & 1


def merge(run1, run2):
    forward1, mixed1, back1 = run1
    forward2, mixed2, back2 = run2
    lane = lax.broadcasted_iota(jnp.int32, (TRACE, 2 * HALF), 1)
    columns = lane >= HALF
    forward1 = jnp.where(columns | (lane < TRACE), forward1, 0.0)
    forward_pair = split(forward1)
    cross = product(split(mixed2[:, :TRACE]), forward_pair) + jnp.where(columns, mixed2, 0.0)
    forward = product(split(forward2[:, :TRACE]), forward_pair)
    forward = forward + jnp.where(columns, forward2, 0.0)
    back_pair = split(back1)
    mixed = mixed1 + product(back_pair, split(cross))
    back = product(back_pair, split(back2))
    back2 = jnp.concatenate([back2, jnp.zeros((TRACE, HALF - TRACE), F32)], axis=1)
    return (forward, mixed, back), (forward1, cross, back2)


def track(upper, pieces, old_ref, state_ref):
    forward1, cross, back2 = pieces
    columns = lax.broadcasted_iota(jnp.int32, (TRACE, 2 * HALF), 1) >= HALF

    @pl.when(upper)
    def _():
        forward_pair = split(forward1)
        here = old_ref[:, : 2 * HALF]
        back = old_ref[:, 2 * HALF : 4 * HALF]
        state_ref[:, : 2 * HALF] = product(split(here[:, :TRACE]), forward_pair) + jnp.where(columns, here, 0.0)
        state_ref[:, 2 * HALF : 4 * HALF] = product(split(back[:, :TRACE]), forward_pair) + jnp.where(columns, back, 0.0)
        state_ref[:, 4 * HALF :] = old_ref[:, 4 * HALF :]

    @pl.when(jnp.logical_not(upper))
    def _():
        gain = split(old_ref[:, 4 * HALF : 4 * HALF + TRACE])
        state_ref[:, : 2 * HALF] = old_ref[:, : 2 * HALF]
        state_ref[:, 2 * HALF : 4 * HALF] = old_ref[:, 2 * HALF : 4 * HALF] + product(gain, split(cross))
        state_ref[:, 4 * HALF :] = product(gain, split(back2))


def first_kernel(pair_ref, total_ref, half_ref, state_ref):
    upper = is_upper(0) == 1
    total, (forward1, cross, back2) = merge(unpack(pair_ref[0]), unpack(pair_ref[1]))
    total = pack(total[0], None, total[1], total[2])
    total_ref[...] = total
    half_ref[...] = jnp.where(upper, total[TRACE // 2 :], total[: TRACE // 2])
    lane = lax.broadcasted_iota(jnp.int32, (TRACE, 2 * HALF), 1)
    row = lax.broadcasted_iota(jnp.int32, (TRACE, 2 * HALF), 0)
    eye = jnp.where(lane == row, 1.0, 0.0)
    state_ref[:, : 2 * HALF] = jnp.where(upper, forward1, eye)
    state_ref[:, 2 * HALF : 4 * HALF] = jnp.where(upper, 0.0, cross)
    state_ref[:, 4 * HALF :] = jnp.where(upper, eye[:, :HALF], back2)


def four_kernel(own_ref, others_ref, old_ref, half_ref, state_ref, middle_ref):
    odd, late = is_upper(1) == 1, is_upper(2) == 1
    own, near, far = own_ref[...], others_ref[0, :TRACE], others_ref[1, :TRACE]
    middle = jnp.concatenate([others_ref[0, TRACE:], others_ref[1, TRACE:]], axis=0)

    def ordered(swap, one, two):
        return unpack(jnp.where(swap, two, one)), unpack(jnp.where(swap, one, two))

    mine, pieces = merge(*ordered(odd, own, near))
    other, _ = merge(*ordered(odd, middle, far))
    track(odd, pieces, old_ref, middle_ref)
    earlier = [jnp.where(late, b, a) for a, b in zip(mine, other)]
    later = [jnp.where(late, a, b) for a, b in zip(mine, other)]
    total, pieces = merge(earlier, later)
    total = pack(total[0], None, total[1], total[2])
    half_ref[...] = jnp.where(is_upper(0) == 1, total[TRACE // 2 :], total[: TRACE // 2])
    track(late, pieces, middle_ref, state_ref)


def combine_kernel(level, sends, pair_ref, old_ref, half_ref, state_ref):
    total, pieces = merge(unpack(pair_ref[0]), unpack(pair_ref[1]))
    if sends == "top":
        total = jnp.where(is_upper(level + 1) == 1, total[1], total[0])
    else:
        total = pack(total[0], None, total[1], total[2])
    half_ref[...] = jnp.where(is_upper(0) == 1, total[TRACE // 2 :], total[: TRACE // 2])
    track(is_upper(level) == 1, pieces, old_ref, state_ref)


def last_kernel(level, pair_ref, old_ref, keep_ref, out_ref, ends_ref):
    ends_ref[:, TRACE:] = jnp.zeros((2, HALF - TRACE, COLUMNS), F32)

    @pl.when(is_upper(level) == 1)
    def _():
        inflow = split(pair_ref[0, :, HALF:])
        ends_ref[0, :TRACE] = old_ref[:, HALF : 2 * HALF] + product(split(old_ref[:, :TRACE]), inflow)
        ends_ref[1, :TRACE] = old_ref[:, 3 * HALF : 4 * HALF] + product(split(old_ref[:, 2 * HALF : 2 * HALF + TRACE]), inflow)

    @pl.when(is_upper(level) == 0)
    def _():
        outflow = split(pair_ref[0, :, HALF:])
        value = pair_ref[1, :, HALF:] + product(split(pair_ref[1, :, :TRACE]), outflow)
        gain = split(old_ref[:, 4 * HALF : 4 * HALF + TRACE])
        ends_ref[0, :TRACE] = old_ref[:, HALF : 2 * HALF]
        ends_ref[1, :TRACE] = old_ref[:, 3 * HALF : 4 * HALF] + product(gain, split(value))

    ends = split(ends_ref[...].reshape(2 * HALF, COLUMNS))
    for element in range(2):
        known = keep_ref[element]
        maps = jnp.concatenate([known[:, :HALF], known[:, 2 * HALF :]], axis=1)
        out_ref[element] = known[:, HALF : 2 * HALF] + product(split(maps), ends)


def call(kernel, shapes, operands, flops, specs=None, scratch=(), limit=8 * 1024):
    moved = 4 * sum(v.size for v in operands) + 4 * sum(s.size for s in shapes)
    single = len(shapes) == 1
    return pl.pallas_call(
        kernel,
        out_shape=shapes[0] if single else shapes,
        in_specs=specs or [VMEM] * len(operands),
        out_specs=VMEM if single else [VMEM] * len(shapes),
        scratch_shapes=list(scratch),
        compiler_params=pltpu.CompilerParams(vmem_limit_bytes=limit * 1024),
        cost_estimate=pl.CostEstimate(flops=flops, bytes_accessed=moved, transcendentals=0),
    )(*operands)


def shape(*dims):
    return jax.ShapeDtypeStruct(dims, F32)


def gather(value, masks):
    count = lax.axis_size("stream")
    masks = [(across * 8 + along) * 2 + core for across, along, core in masks]
    seen, groups = set(), []
    for device in range(count):
        if device in seen:
            continue
        group = {device}
        for mask in masks:
            group |= {member ^ mask for member in group}
        seen |= group
        groups.append(sorted(group))
    return lax.all_gather(value, "stream", axis_index_groups=groups)


def swap(value, along):
    count = lax.axis_size("stream")
    return lax.ppermute(value, "stream", [(k, k ^ (2 * along[k % 2])) for k in range(count)])


def shards(rhs, inverse, lower, upper, upwind, rows, target):
    groups = lax.axis_size("azi")
    local = rhs.shape[0]
    target = target.reshape(1, -1)
    rows, target, upwind = [pltpu.with_memory_space_constraint(v, pltpu.HBM) for v in (rows, target, upwind)]
    partial, crosses = call(
        wake_kernel,
        [shape(groups * local, BLOCK), shape(8, HALF)],
        [target, rows, upwind],
        10**10,
        specs=[HBM, HBM, HBM],
        scratch=[
            pltpu.VMEM(target.shape, jnp.int32),
            pltpu.VMEM(rows.shape, F32),
            pltpu.SMEM(upwind.shape, jnp.int32),
            pltpu.SemaphoreType.DMA((3,)),
        ],
    )
    parts = lax.all_to_all(partial.reshape(groups, local, BLOCK), "azi", 0, 0)
    parts = jnp.swapaxes(parts, 0, 1)
    total, keep = call(
        local_kernel,
        [shape(TRACE, 4 * HALF), shape(local, BLOCK, 3 * HALF)],
        [*face_rows(), crosses, parts, lower, upper, inverse, rhs],
        2 * 10**9,
        limit=24 * 1024,
    )
    full, half, state = shape(TRACE, 4 * HALF), shape(TRACE // 2, 4 * HALF), shape(TRACE, 5 * HALF)
    total, part, tracked = call(first_kernel, [full, half, state], [gather(total, [(0, 0, 1)])], 3 * 10**7)
    received = jnp.concatenate([swap(total, (1, 3)), swap(part, (2, 2))], axis=0)
    received = gather(received, [(0, 0, 1)])
    part, tracked = call(
        four_kernel,
        [half, state],
        [total, received, tracked],
        10**8,
        scratch=[pltpu.VMEM((TRACE, 5 * HALF), F32)],
    )
    pair = gather(part, [(0, 0, 1), (0, 6, 0)]).reshape(2, TRACE, 4 * HALF)
    part, tracked = call(functools.partial(combine_kernel, 3, "whole"), [half, state], [pair, tracked], 3 * 10**7)
    pair = gather(part, [(0, 0, 1), (1, 0, 0)]).reshape(2, TRACE, 4 * HALF)
    crossing = shape(TRACE // 2, 2 * HALF)
    part, tracked = call(functools.partial(combine_kernel, 4, "top"), [crossing, state], [pair, tracked], 3 * 10**7)
    pair = gather(part, [(0, 0, 1), (3, 0, 0)]).reshape(2, TRACE, 2 * HALF)
    return call(
        functools.partial(last_kernel, 5),
        [shape(local, BLOCK, COLUMNS)],
        [pair, tracked, keep],
        10**8,
        scratch=[pltpu.VMEM((2, HALF, COLUMNS), F32)],
    )


def solution(mesh):
    both = ("stream", "azi")
    return jax.shard_map(
        shards,
        mesh=mesh,
        in_specs=(
            P(both, None, None),
            P(both, None, None),
            P(both, None, None),
            P(both, None, None),
            P(both, None),
            P(both, None),
            P(both),
        ),
        out_specs=P(both, None, None),
        check_vma=False,
    )
```

```python
import functools

import jax
import jax.numpy as jnp
import numpy as np
from jax import lax
from jax.experimental import pallas as pl
from jax.experimental.pallas import tpu as pltpu
from jax.sharding import PartitionSpec as P

TRACE = 80
BLOCK = 320
COLUMNS = 128
PLANE = 16
CUBE = 64
HALF = 128
F32 = jnp.float32
BF16 = jnp.bfloat16
VMEM = pl.BlockSpec(memory_space=pltpu.VMEM)
SMEM = pl.BlockSpec(memory_space=pltpu.SMEM)
HBM = pl.BlockSpec(memory_space=pltpu.HBM)


def split(value):
    high = value.astype(BF16)
    return high, (value - high.astype(F32)).astype(BF16)


def dot(left, right):
    return jnp.dot(left, right, preferred_element_type=F32)


def product(left, right):
    return dot(left[0], right[0]) + (dot(left[0], right[1]) + dot(left[1], right[0]))


def select_rows(onehot, value):
    return dot(onehot, value[0]), dot(onehot, value[1])


def fetch(sources, buffers, sems):
    copies = [pltpu.make_async_copy(a, b, sems.at[i]) for i, (a, b) in enumerate(zip(sources, buffers))]
    for copy in copies:
        copy.start()
    return copies


def wake_kernel(target_hbm, rows_hbm, upwind_hbm, out_ref, crosses_ref, target_ref, rows_ref, upwind_ref, sems):
    for copy in fetch((target_hbm, rows_hbm, upwind_hbm), (target_ref, rows_ref, upwind_ref), sems):
        copy.wait()
    ids = lax.broadcasted_iota(jnp.int32, (out_ref.shape[0], target_ref.shape[1]), 0)
    onehot = jnp.where(ids == target_ref[...], 1.0, 0.0).astype(BF16)
    high, low = split(rows_ref[...])
    out_ref[...] = dot(onehot, high) + dot(onehot, low)
    face = lax.broadcasted_iota(jnp.int32, crosses_ref.shape, 0)
    crosses = jnp.zeros(crosses_ref.shape, F32)
    for at in range(3):
        crosses = jnp.where((face == at) & (upwind_ref[1, at] == 2), 1.0, crosses)
    crosses_ref[...] = crosses


def face_block(ref, element, face):
    return ref[element, :, face * TRACE : (face + 1) * TRACE]


def face_rows():
    trace = np.arange(TRACE)
    field, upper, lower = trace // PLANE, trace // 4 % 4, trace % 4
    take = np.zeros((2, 3 * TRACE, BLOCK), np.float32)
    for odd in range(2):
        side = 3 * odd
        places = (side * 16 + upper * 4 + lower, upper * 16 + side * 4 + lower, upper * 16 + lower * 4 + side)
        for face, place in enumerate(places):
            take[odd, face * TRACE + trace, field * CUBE + place] = 1.0
    return jnp.asarray(take, BF16), jnp.asarray(take.transpose(0, 2, 1), BF16)


WHOLE = 256


def left_parts(value):
    high, low = split(value)
    ends = [part[:, WHOLE:].astype(F32) for part in (high, low, high)]
    return high[:, :WHOLE], low[:, :WHOLE], jnp.concatenate(ends, axis=1).astype(BF16)


def right_parts(value):
    high, low = split(value)
    ends = [part[WHOLE:] for part in (high, high, low)]
    return high[:WHOLE], low[:WHOLE], jnp.concatenate(ends, axis=0)


def long_product(left, right):
    return (dot(left[0], right[0]) + dot(left[2], right[2])) + (dot(left[0], right[1]) + dot(left[1], right[0]))


def last_plane(value):
    return jnp.concatenate(
        [value[at + CUBE - PLANE : at + CUBE] for at in range(0, BLOCK, CUBE)], axis=0
    )


def pack(first, second, third, fourth):
    lead = TRACE
    spare = HALF - lead
    mid = third[:, :HALF]
    return jnp.concatenate(
        [
            first[:, :lead],
            mid[:, :spare],
            first[:, HALF:],
            fourth[:, :lead],
            mid[:, spare:lead],
            jnp.zeros((TRACE, 2 * spare - lead), F32),
            third[:, HALF:],
        ],
        axis=1,
    )


def unpack(value):
    lead = TRACE
    spare = HALF - lead
    zeros = jnp.zeros((TRACE, spare), F32)
    forward = value[:, : 2 * HALF]
    mixed = jnp.concatenate(
        [
            value[:, lead:HALF],
            value[:, 2 * HALF + lead : 2 * HALF + lead + (lead - spare)],
            zeros,
            value[:, 3 * HALF :],
        ],
        axis=1,
    )
    return forward, mixed, value[:, 2 * HALF : 2 * HALF + lead]


def expand(block, take):
    high, low = split(block)
    return dot(high, take) + dot(low, take)


def local_kernel(take_ref, put_ref, crosses_ref, wake_ref, low_ref, up_ref, inv_ref, rhs_ref, total_ref, keep_ref):
    put_even, put_odd = put_ref[0], put_ref[1]
    take_even, take_odd = take_ref[0], take_ref[1]
    ones = jnp.ones((wake_ref.shape[1], COLUMNS), BF16)
    spare = jnp.zeros((3 * TRACE, HALF - TRACE), F32)
    at = [slice(face * TRACE, (face + 1) * TRACE) for face in range(3)]

    def source(element):
        high, low = split(wake_ref[element])
        dims = (((0,), (0,)), ((), ()))
        wake = lax.dot_general(high, ones, dims, preferred_element_type=F32)
        wake += lax.dot_general(low, ones, dims, preferred_element_type=F32)
        return rhs_ref[element] + wake

    def put(onehot, rows):
        return sum(select_rows(onehot, split(rows)))

    crosses = [crosses_ref[face : face + 1, :1] > 0.5 for face in range(3)]

    def kept(values, crossing):
        return [jnp.where(cross == crossing, v, 0.0) for cross, v in zip(crosses, values)]

    def wide(values):
        return jnp.concatenate([jnp.concatenate(values, axis=0), spare], axis=1)

    from_first = put(put_even, wide([face_block(low_ref, 0, face) for face in range(3)]))
    blocks = [face_block(low_ref, 1, face) for face in range(3)]
    from_second = put(put_even, wide(kept(blocks, True)))
    inside = [expand(blocks[face], take_odd[at[face]]) for face in range(3)]
    down = left_parts(put(put_even, jnp.concatenate(kept(inside, False), axis=0)))
    inside = [expand(face_block(up_ref, 1, face), take_even[at[face]]) for face in range(3)]
    up = left_parts(put(put_odd, jnp.concatenate(kept(inside, False), axis=0)))
    leave_second = left_parts(sum(kept(inside, True)))
    leave_first = left_parts(expand(up_ref[0], take_even))

    inverse = left_parts(inv_ref[0])
    later_inverse = left_parts(inv_ref[1])
    first = long_product(inverse, right_parts(jnp.concatenate([-from_first, source(0)], axis=1)))

    side = put_odd[:, :HALF]
    lane = lax.broadcasted_iota(jnp.int32, (BLOCK, HALF), 1)
    high, low = split(inv_ref[1])
    returned = -(dot(high, side) + dot(low, side))
    returned = jnp.where(lane < TRACE, returned, 0.0)
    returned_pair = right_parts(returned)
    keep_ref[1, :, 2 * HALF :] = returned

    inner = long_product(down, right_parts(first))
    earlier = -long_product(inverse, right_parts(long_product(up, returned_pair)))
    keep_ref[0, :, 2 * HALF :] = earlier

    base = jnp.concatenate([-from_second, source(1)], axis=1)
    second = long_product(later_inverse, right_parts(base - inner))
    keep_ref[1, :, : 2 * HALF] = second
    second_pair = right_parts(second)
    back = long_product(leave_second, returned_pair) + long_product(leave_first, right_parts(earlier))
    inner = long_product(up, second_pair)
    first = first - long_product(inverse, right_parts(inner))
    keep_ref[0, :, : 2 * HALF] = first
    mixed = long_product(leave_second, second_pair) + long_product(leave_first, right_parts(first))
    total_ref[...] = pack(last_plane(second), None, mixed, back)


def is_upper(level):
    return (lax.axis_index("stream") >> level) & 1


def merge(run1, run2):
    forward1, mixed1, back1 = run1
    forward2, mixed2, back2 = run2
    lane = lax.broadcasted_iota(jnp.int32, (TRACE, 2 * HALF), 1)
    columns = lane >= HALF
    forward1 = jnp.where(columns | (lane < TRACE), forward1, 0.0)
    forward_pair = split(forward1)
    cross = product(split(mixed2[:, :TRACE]), forward_pair) + jnp.where(columns, mixed2, 0.0)
    forward = product(split(forward2[:, :TRACE]), forward_pair)
    forward = forward + jnp.where(columns, forward2, 0.0)
    back_pair = split(back1)
    mixed = mixed1 + product(back_pair, split(cross))
    back = product(back_pair, split(back2))
    back2 = jnp.concatenate([back2, jnp.zeros((TRACE, HALF - TRACE), F32)], axis=1)
    return (forward, mixed, back), (forward1, cross, back2)


def track(upper, pieces, old_ref, state_ref):
    forward1, cross, back2 = pieces
    columns = lax.broadcasted_iota(jnp.int32, (TRACE, 2 * HALF), 1) >= HALF

    @pl.when(upper)
    def _():
        forward_pair = split(forward1)
        here = old_ref[:, : 2 * HALF]
        back = old_ref[:, 2 * HALF : 4 * HALF]
        state_ref[:, : 2 * HALF] = product(split(here[:, :TRACE]), forward_pair) + jnp.where(columns, here, 0.0)
        state_ref[:, 2 * HALF : 4 * HALF] = product(split(back[:, :TRACE]), forward_pair) + jnp.where(columns, back, 0.0)
        state_ref[:, 4 * HALF :] = old_ref[:, 4 * HALF :]

    @pl.when(jnp.logical_not(upper))
    def _():
        gain = split(old_ref[:, 4 * HALF : 4 * HALF + TRACE])
        state_ref[:, : 2 * HALF] = old_ref[:, : 2 * HALF]
        state_ref[:, 2 * HALF : 4 * HALF] = old_ref[:, 2 * HALF : 4 * HALF] + product(gain, split(cross))
        state_ref[:, 4 * HALF :] = product(gain, split(back2))


def first_kernel(pair_ref, total_ref, half_ref, state_ref):
    upper = is_upper(0) == 1
    total, (forward1, cross, back2) = merge(unpack(pair_ref[0]), unpack(pair_ref[1]))
    total = pack(total[0], None, total[1], total[2])
    total_ref[...] = total
    half_ref[...] = jnp.where(upper, total[TRACE // 2 :], total[: TRACE // 2])
    lane = lax.broadcasted_iota(jnp.int32, (TRACE, 2 * HALF), 1)
    row = lax.broadcasted_iota(jnp.int32, (TRACE, 2 * HALF), 0)
    eye = jnp.where(lane == row, 1.0, 0.0)
    state_ref[:, : 2 * HALF] = jnp.where(upper, forward1, eye)
    state_ref[:, 2 * HALF : 4 * HALF] = jnp.where(upper, 0.0, cross)
    state_ref[:, 4 * HALF :] = jnp.where(upper, eye[:, :HALF], back2)


def four_kernel(own_ref, others_ref, old_ref, half_ref, state_ref, middle_ref):
    odd, late = is_upper(1) == 1, is_upper(2) == 1
    own, near, far = own_ref[...], others_ref[0, :TRACE], others_ref[1, :TRACE]
    middle = jnp.concatenate([others_ref[0, TRACE:], others_ref[1, TRACE:]], axis=0)

    def ordered(swap, one, two):
        return unpack(jnp.where(swap, two, one)), unpack(jnp.where(swap, one, two))

    mine, pieces = merge(*ordered(odd, own, near))
    other, _ = merge(*ordered(odd, middle, far))
    track(odd, pieces, old_ref, middle_ref)
    earlier = [jnp.where(late, b, a) for a, b in zip(mine, other)]
    later = [jnp.where(late, a, b) for a, b in zip(mine, other)]
    total, pieces = merge(earlier, later)
    total = pack(total[0], None, total[1], total[2])
    half_ref[...] = jnp.where(is_upper(0) == 1, total[TRACE // 2 :], total[: TRACE // 2])
    track(late, pieces, middle_ref, state_ref)


def combine_kernel(level, sends, pair_ref, old_ref, total_ref, state_ref):
    total, pieces = merge(unpack(pair_ref[0]), unpack(pair_ref[1]))
    if sends == "top":
        total = jnp.where(is_upper(level + 1) == 1, total[1], total[0])
    else:
        total = pack(total[0], None, total[1], total[2])
    if sends != "top":
        total = jnp.where(is_upper(0) == 1, total[TRACE // 2 :], total[: TRACE // 2])
    total_ref[...] = total
    track(is_upper(level) == 1, pieces, old_ref, state_ref)


def last_kernel(level, pair_ref, old_ref, keep_ref, out_ref, ends_ref):
    ends_ref[:, TRACE:] = jnp.zeros((2, HALF - TRACE, COLUMNS), F32)

    @pl.when(is_upper(level) == 1)
    def _():
        inflow = split(pair_ref[0, :, HALF:])
        ends_ref[0, :TRACE] = old_ref[:, HALF : 2 * HALF] + product(split(old_ref[:, :TRACE]), inflow)
        ends_ref[1, :TRACE] = old_ref[:, 3 * HALF : 4 * HALF] + product(split(old_ref[:, 2 * HALF : 2 * HALF + TRACE]), inflow)

    @pl.when(is_upper(level) == 0)
    def _():
        outflow = split(pair_ref[0, :, HALF:])
        value = pair_ref[1, :, HALF:] + product(split(pair_ref[1, :, :TRACE]), outflow)
        gain = split(old_ref[:, 4 * HALF : 4 * HALF + TRACE])
        ends_ref[0, :TRACE] = old_ref[:, HALF : 2 * HALF]
        ends_ref[1, :TRACE] = old_ref[:, 3 * HALF : 4 * HALF] + product(gain, split(value))

    ends = split(ends_ref[...].reshape(2 * HALF, COLUMNS))
    for element in range(2):
        known = keep_ref[element]
        maps = jnp.concatenate([known[:, :HALF], known[:, 2 * HALF :]], axis=1)
        out_ref[element] = known[:, HALF : 2 * HALF] + product(split(maps), ends)


def call(kernel, shapes, operands, flops, specs=None, scratch=(), limit=8 * 1024):
    moved = 4 * sum(v.size for v in operands) + 4 * sum(s.size for s in shapes)
    single = len(shapes) == 1
    return pl.pallas_call(
        kernel,
        out_shape=shapes[0] if single else shapes,
        in_specs=specs or [VMEM] * len(operands),
        out_specs=VMEM if single else [VMEM] * len(shapes),
        scratch_shapes=list(scratch),
        compiler_params=pltpu.CompilerParams(vmem_limit_bytes=limit * 1024),
        cost_estimate=pl.CostEstimate(flops=flops, bytes_accessed=moved, transcendentals=0),
    )(*operands)


def shape(*dims):
    return jax.ShapeDtypeStruct(dims, F32)


def gather(value, masks):
    count = lax.axis_size("stream")
    masks = [(across * 8 + along) * 2 + core for across, along, core in masks]
    seen, groups = set(), []
    for device in range(count):
        if device in seen:
            continue
        group = {device}
        for mask in masks:
            group |= {member ^ mask for member in group}
        seen |= group
        groups.append(sorted(group))
    return lax.all_gather(value, "stream", axis_index_groups=groups)


def swap(value, along):
    count = lax.axis_size("stream")
    return lax.ppermute(value, "stream", [(k, k ^ (2 * along[k % 2])) for k in range(count)])


def shards(rhs, inverse, lower, upper, upwind, rows, target):
    groups = lax.axis_size("azi")
    local = rhs.shape[0]
    target = target.reshape(1, -1)
    rows, target, upwind = [pltpu.with_memory_space_constraint(v, pltpu.HBM) for v in (rows, target, upwind)]
    partial, crosses = call(
        wake_kernel,
        [shape(groups * local, BLOCK), shape(8, HALF)],
        [target, rows, upwind],
        10**10,
        specs=[HBM, HBM, HBM],
        scratch=[
            pltpu.VMEM(target.shape, jnp.int32),
            pltpu.VMEM(rows.shape, F32),
            pltpu.SMEM(upwind.shape, jnp.int32),
            pltpu.SemaphoreType.DMA((3,)),
        ],
    )
    parts = lax.all_to_all(partial.reshape(groups, local, BLOCK), "azi", 0, 0)
    parts = jnp.swapaxes(parts, 0, 1)
    total, keep = call(
        local_kernel,
        [shape(TRACE, 4 * HALF), shape(local, BLOCK, 3 * HALF)],
        [*face_rows(), crosses, parts, lower, upper, inverse, rhs],
        2 * 10**9,
        limit=24 * 1024,
    )
    full, half, state = shape(TRACE, 4 * HALF), shape(TRACE // 2, 4 * HALF), shape(TRACE, 5 * HALF)
    total, part, tracked = call(first_kernel, [full, half, state], [gather(total, [(0, 0, 1)])], 3 * 10**7)
    part = swap(part, (2, 2))
    received = jnp.concatenate([swap(total, (1, 3)), part], axis=0)
    received = gather(received, [(0, 0, 1)])
    part, tracked = call(
        four_kernel,
        [half, state],
        [total, received, tracked],
        10**8,
        scratch=[pltpu.VMEM((TRACE, 5 * HALF), F32)],
    )
    pair = gather(part, [(0, 0, 1), (0, 6, 0)]).reshape(2, TRACE, 4 * HALF)
    part, tracked = call(functools.partial(combine_kernel, 3, "whole"), [half, state], [pair, tracked], 3 * 10**7)
    pair = gather(part, [(0, 0, 1), (1, 0, 0)]).reshape(2, TRACE, 4 * HALF)
    crossing = shape(TRACE, 2 * HALF)
    total, tracked = call(functools.partial(combine_kernel, 4, "top"), [crossing, state], [pair, tracked], 3 * 10**7)
    pair = gather(total, [(3, 0, 0)])
    return call(
        functools.partial(last_kernel, 5),
        [shape(local, BLOCK, COLUMNS)],
        [pair, tracked, keep],
        10**8,
        scratch=[pltpu.VMEM((2, HALF, COLUMNS), F32)],
    )


def solution(mesh):
    both = ("stream", "azi")
    return jax.shard_map(
        shards,
        mesh=mesh,
        in_specs=(
            P(both, None, None),
            P(both, None, None),
            P(both, None, None),
            P(both, None, None),
            P(both, None),
            P(both, None),
            P(both),
        ),
        out_specs=P(both, None, None),
        check_vma=False,
    )
```

```python
import functools

import jax
import jax.numpy as jnp
import numpy as np
from jax import lax
from jax.experimental import pallas as pl
from jax.experimental.pallas import tpu as pltpu
from jax.sharding import PartitionSpec as P

TRACE = 80
BLOCK = 320
COLUMNS = 128
PLANE = 16
CUBE = 64
HALF = 128
F32 = jnp.float32
BF16 = jnp.bfloat16
VMEM = pl.BlockSpec(memory_space=pltpu.VMEM)
SMEM = pl.BlockSpec(memory_space=pltpu.SMEM)
HBM = pl.BlockSpec(memory_space=pltpu.HBM)


def split(value):
    high = value.astype(BF16)
    return high, (value - high.astype(F32)).astype(BF16)


def dot(left, right):
    return jnp.dot(left, right, preferred_element_type=F32)


def product(left, right):
    return dot(left[0], right[0]) + (dot(left[0], right[1]) + dot(left[1], right[0]))


def select_rows(onehot, value):
    return dot(onehot, value[0]), dot(onehot, value[1])


def fetch(sources, buffers, sems):
    copies = [pltpu.make_async_copy(a, b, sems.at[i]) for i, (a, b) in enumerate(zip(sources, buffers))]
    for copy in copies:
        copy.start()
    return copies


def wake_kernel(target_hbm, rows_hbm, upwind_hbm, out_ref, crosses_ref, target_ref, rows_ref, upwind_ref, sems):
    for copy in fetch((target_hbm, rows_hbm, upwind_hbm), (target_ref, rows_ref, upwind_ref), sems):
        copy.wait()
    ids = lax.broadcasted_iota(jnp.int32, (out_ref.shape[0], target_ref.shape[1]), 0)
    onehot = jnp.where(ids == target_ref[...], 1.0, 0.0).astype(BF16)
    high, low = split(rows_ref[...])
    out_ref[...] = dot(onehot, high) + dot(onehot, low)
    face = lax.broadcasted_iota(jnp.int32, crosses_ref.shape, 0)
    crosses = jnp.zeros(crosses_ref.shape, F32)
    for at in range(3):
        crosses = jnp.where((face == at) & (upwind_ref[1, at] == 2), 1.0, crosses)
    crosses_ref[...] = crosses


def face_block(ref, element, face):
    return ref[element, :, face * TRACE : (face + 1) * TRACE]


def face_rows():
    trace = np.arange(TRACE)
    field, upper, lower = trace // PLANE, trace // 4 % 4, trace % 4
    take = np.zeros((2, 3 * TRACE, BLOCK), np.float32)
    for odd in range(2):
        side = 3 * odd
        places = (side * 16 + upper * 4 + lower, upper * 16 + side * 4 + lower, upper * 16 + lower * 4 + side)
        for face, place in enumerate(places):
            take[odd, face * TRACE + trace, field * CUBE + place] = 1.0
    return jnp.asarray(take, BF16), jnp.asarray(take.transpose(0, 2, 1), BF16)


WHOLE = 256


def left_parts(value):
    high, low = split(value)
    ends = [part[:, WHOLE:].astype(F32) for part in (high, low, high)]
    return high[:, :WHOLE], low[:, :WHOLE], jnp.concatenate(ends, axis=1).astype(BF16)


def right_parts(value):
    high, low = split(value)
    ends = [part[WHOLE:] for part in (high, high, low)]
    return high[:WHOLE], low[:WHOLE], jnp.concatenate(ends, axis=0)


def long_product(left, right):
    return (dot(left[0], right[0]) + dot(left[2], right[2])) + (dot(left[0], right[1]) + dot(left[1], right[0]))


def last_plane(value):
    return jnp.concatenate(
        [value[at + CUBE - PLANE : at + CUBE] for at in range(0, BLOCK, CUBE)], axis=0
    )


def pack(first, second, third, fourth):
    lead = TRACE
    spare = HALF - lead
    mid = third[:, :HALF]
    return jnp.concatenate(
        [
            first[:, :lead],
            mid[:, :spare],
            first[:, HALF:],
            fourth[:, :lead],
            mid[:, spare:lead],
            jnp.zeros((TRACE, 2 * spare - lead), F32),
            third[:, HALF:],
        ],
        axis=1,
    )


def unpack(value):
    lead = TRACE
    spare = HALF - lead
    zeros = jnp.zeros((TRACE, spare), F32)
    forward = value[:, : 2 * HALF]
    mixed = jnp.concatenate(
        [
            value[:, lead:HALF],
            value[:, 2 * HALF + lead : 2 * HALF + lead + (lead - spare)],
            zeros,
            value[:, 3 * HALF :],
        ],
        axis=1,
    )
    return forward, mixed, value[:, 2 * HALF : 2 * HALF + lead]


def expand(block, take):
    high, low = split(block)
    return dot(high, take) + dot(low, take)


def local_kernel(take_ref, put_ref, crosses_ref, wake_ref, low_ref, up_ref, inv_ref, rhs_ref, total_ref, keep_ref):
    put_even, put_odd = put_ref[0], put_ref[1]
    take_even, take_odd = take_ref[0], take_ref[1]
    ones = jnp.ones((wake_ref.shape[1], COLUMNS), BF16)
    spare = jnp.zeros((3 * TRACE, HALF - TRACE), F32)
    at = [slice(face * TRACE, (face + 1) * TRACE) for face in range(3)]

    def source(element):
        high, low = split(wake_ref[element])
        dims = (((0,), (0,)), ((), ()))
        wake = lax.dot_general(high, ones, dims, preferred_element_type=F32)
        wake += lax.dot_general(low, ones, dims, preferred_element_type=F32)
        return rhs_ref[element] + wake

    def put(onehot, rows):
        return sum(select_rows(onehot, split(rows)))

    crosses = [crosses_ref[face : face + 1, :1] > 0.5 for face in range(3)]

    def kept(values, crossing):
        return [jnp.where(cross == crossing, v, 0.0) for cross, v in zip(crosses, values)]

    def wide(values):
        return jnp.concatenate([jnp.concatenate(values, axis=0), spare], axis=1)

    from_first = put(put_even, wide([face_block(low_ref, 0, face) for face in range(3)]))
    blocks = [face_block(low_ref, 1, face) for face in range(3)]
    from_second = put(put_even, wide(kept(blocks, True)))
    inside = [expand(blocks[face], take_odd[at[face]]) for face in range(3)]
    down = left_parts(put(put_even, jnp.concatenate(kept(inside, False), axis=0)))
    inside = [expand(face_block(up_ref, 1, face), take_even[at[face]]) for face in range(3)]
    up = left_parts(put(put_odd, jnp.concatenate(kept(inside, False), axis=0)))
    leave_second = left_parts(sum(kept(inside, True)))
    leave_first = left_parts(expand(up_ref[0], take_even))

    inverse = left_parts(inv_ref[0])
    later_inverse = left_parts(inv_ref[1])
    first = long_product(inverse, right_parts(jnp.concatenate([-from_first, source(0)], axis=1)))

    side = put_odd[:, :HALF]
    lane = lax.broadcasted_iota(jnp.int32, (BLOCK, HALF), 1)
    high, low = split(inv_ref[1])
    returned = -(dot(high, side) + dot(low, side))
    returned = jnp.where(lane < TRACE, returned, 0.0)
    returned_pair = right_parts(returned)
    keep_ref[1, :, 2 * HALF :] = returned

    inner = long_product(down, right_parts(first))
    earlier = -long_product(inverse, right_parts(long_product(up, returned_pair)))
    keep_ref[0, :, 2 * HALF :] = earlier

    base = jnp.concatenate([-from_second, source(1)], axis=1)
    second = long_product(later_inverse, right_parts(base - inner))
    keep_ref[1, :, : 2 * HALF] = second
    second_pair = right_parts(second)
    back = long_product(leave_second, returned_pair) + long_product(leave_first, right_parts(earlier))
    inner = long_product(up, second_pair)
    first = first - long_product(inverse, right_parts(inner))
    keep_ref[0, :, : 2 * HALF] = first
    mixed = long_product(leave_second, second_pair) + long_product(leave_first, right_parts(first))
    total_ref[...] = pack(last_plane(second), None, mixed, back)


def is_upper(level):
    return (lax.axis_index("stream") >> level) & 1


def merge(run1, run2):
    forward1, mixed1, back1 = run1
    forward2, mixed2, back2 = run2
    lane = lax.broadcasted_iota(jnp.int32, (TRACE, 2 * HALF), 1)
    columns = lane >= HALF
    forward1 = jnp.where(columns | (lane < TRACE), forward1, 0.0)
    forward_pair = split(forward1)
    cross = product(split(mixed2[:, :TRACE]), forward_pair) + jnp.where(columns, mixed2, 0.0)
    forward = product(split(forward2[:, :TRACE]), forward_pair)
    forward = forward + jnp.where(columns, forward2, 0.0)
    back_pair = split(back1)
    mixed = mixed1 + product(back_pair, split(cross))
    back = product(back_pair, split(back2))
    back2 = jnp.concatenate([back2, jnp.zeros((TRACE, HALF - TRACE), F32)], axis=1)
    return (forward, mixed, back), (forward1, cross, back2)


def track(upper, pieces, old):
    forward1, cross, back2 = pieces
    here, back, gain = old
    columns = lax.broadcasted_iota(jnp.int32, (TRACE, 2 * HALF), 1) >= HALF
    through = product(split(here[:, :TRACE]), split(forward1)) + jnp.where(columns, here, 0.0)
    factor = jnp.where(upper, back[:, :TRACE], gain[:, :TRACE])
    added = jnp.where(columns | jnp.logical_not(upper), back, 0.0)
    back = product(split(factor), split(jnp.where(upper, forward1, cross))) + added
    gained = product(split(gain[:, :TRACE]), split(back2))
    return jnp.where(upper, through, here), back, jnp.where(upper, gain, gained)


def state_of(ref):
    return ref[:, : 2 * HALF], ref[:, 2 * HALF : 4 * HALF], ref[:, 4 * HALF :]


def first_kernel(pair_ref, total_ref, half_ref, state_ref):
    upper = is_upper(0) == 1
    total, (forward1, cross, back2) = merge(unpack(pair_ref[0]), unpack(pair_ref[1]))
    total = pack(total[0], None, total[1], total[2])
    total_ref[...] = total
    half_ref[...] = jnp.where(upper, total[TRACE // 2 :], total[: TRACE // 2])
    lane = lax.broadcasted_iota(jnp.int32, (TRACE, 2 * HALF), 1)
    row = lax.broadcasted_iota(jnp.int32, (TRACE, 2 * HALF), 0)
    eye = jnp.where(lane == row, 1.0, 0.0)
    state_ref[:, : 2 * HALF] = jnp.where(upper, forward1, eye)
    state_ref[:, 2 * HALF : 4 * HALF] = jnp.where(upper, 0.0, cross)
    state_ref[:, 4 * HALF :] = jnp.where(upper, eye[:, :HALF], back2)


def four_kernel(own_ref, others_ref, old_ref, half_ref, state_ref):
    odd, late = is_upper(1) == 1, is_upper(2) == 1
    own, near, far = own_ref[...], others_ref[0, :TRACE], others_ref[1, :TRACE]
    middle = jnp.concatenate([others_ref[0, TRACE:], others_ref[1, TRACE:]], axis=0)

    def ordered(swap, one, two):
        return unpack(jnp.where(swap, two, one)), unpack(jnp.where(swap, one, two))

    mine, pieces = merge(*ordered(odd, own, near))
    other, _ = merge(*ordered(odd, middle, far))
    state = track(odd, pieces, state_of(old_ref))
    earlier = [jnp.where(late, b, a) for a, b in zip(mine, other)]
    later = [jnp.where(late, a, b) for a, b in zip(mine, other)]
    total, pieces = merge(earlier, later)
    total = pack(total[0], None, total[1], total[2])
    half_ref[...] = jnp.where(is_upper(0) == 1, total[TRACE // 2 :], total[: TRACE // 2])
    state_ref[...] = jnp.concatenate(track(late, pieces, state), axis=1)


def combine_kernel(level, sends, pair_ref, old_ref, total_ref, state_ref):
    total, pieces = merge(unpack(pair_ref[0]), unpack(pair_ref[1]))
    if sends == "top":
        total = jnp.where(is_upper(level + 1) == 1, total[1], total[0])
    else:
        total = pack(total[0], None, total[1], total[2])
    if sends != "top":
        total = jnp.where(is_upper(0) == 1, total[TRACE // 2 :], total[: TRACE // 2])
    total_ref[...] = total
    state_ref[...] = jnp.concatenate(track(is_upper(level) == 1, pieces, state_of(old_ref)), axis=1)


def last_kernel(level, pair_ref, old_ref, keep_ref, out_ref, ends_ref):
    ends_ref[:, TRACE:] = jnp.zeros((2, HALF - TRACE, COLUMNS), F32)

    @pl.when(is_upper(level) == 1)
    def _():
        inflow = split(pair_ref[0, :, HALF:])
        ends_ref[0, :TRACE] = old_ref[:, HALF : 2 * HALF] + product(split(old_ref[:, :TRACE]), inflow)
        ends_ref[1, :TRACE] = old_ref[:, 3 * HALF : 4 * HALF] + product(split(old_ref[:, 2 * HALF : 2 * HALF + TRACE]), inflow)

    @pl.when(is_upper(level) == 0)
    def _():
        outflow = split(pair_ref[0, :, HALF:])
        value = pair_ref[1, :, HALF:] + product(split(pair_ref[1, :, :TRACE]), outflow)
        gain = split(old_ref[:, 4 * HALF : 4 * HALF + TRACE])
        ends_ref[0, :TRACE] = old_ref[:, HALF : 2 * HALF]
        ends_ref[1, :TRACE] = old_ref[:, 3 * HALF : 4 * HALF] + product(gain, split(value))

    ends = split(ends_ref[...].reshape(2 * HALF, COLUMNS))
    for element in range(2):
        known = keep_ref[element]
        maps = jnp.concatenate([known[:, :HALF], known[:, 2 * HALF :]], axis=1)
        out_ref[element] = known[:, HALF : 2 * HALF] + product(split(maps), ends)


def call(kernel, shapes, operands, flops, specs=None, scratch=(), limit=8 * 1024):
    moved = 4 * sum(v.size for v in operands) + 4 * sum(s.size for s in shapes)
    single = len(shapes) == 1
    return pl.pallas_call(
        kernel,
        out_shape=shapes[0] if single else shapes,
        in_specs=specs or [VMEM] * len(operands),
        out_specs=VMEM if single else [VMEM] * len(shapes),
        scratch_shapes=list(scratch),
        compiler_params=pltpu.CompilerParams(vmem_limit_bytes=limit * 1024),
        cost_estimate=pl.CostEstimate(flops=flops, bytes_accessed=moved, transcendentals=0),
    )(*operands)


def shape(*dims):
    return jax.ShapeDtypeStruct(dims, F32)


def gather(value, masks):
    count = lax.axis_size("stream")
    masks = [(across * 8 + along) * 2 + core for across, along, core in masks]
    seen, groups = set(), []
    for device in range(count):
        if device in seen:
            continue
        group = {device}
        for mask in masks:
            group |= {member ^ mask for member in group}
        seen |= group
        groups.append(sorted(group))
    return lax.all_gather(value, "stream", axis_index_groups=groups)


def swap(value, along):
    count = lax.axis_size("stream")
    return lax.ppermute(value, "stream", [(k, k ^ (2 * along[k % 2])) for k in range(count)])


def shards(rhs, inverse, lower, upper, upwind, rows, target):
    groups = lax.axis_size("azi")
    local = rhs.shape[0]
    target = target.reshape(1, -1)
    rows, target, upwind = [pltpu.with_memory_space_constraint(v, pltpu.HBM) for v in (rows, target, upwind)]
    partial, crosses = call(
        wake_kernel,
        [shape(groups * local, BLOCK), shape(8, HALF)],
        [target, rows, upwind],
        10**10,
        specs=[HBM, HBM, HBM],
        scratch=[
            pltpu.VMEM(target.shape, jnp.int32),
            pltpu.VMEM(rows.shape, F32),
            pltpu.SMEM(upwind.shape, jnp.int32),
            pltpu.SemaphoreType.DMA((3,)),
        ],
    )
    parts = lax.all_to_all(partial.reshape(groups, local, BLOCK), "azi", 0, 0)
    parts = jnp.swapaxes(parts, 0, 1)
    total, keep = call(
        local_kernel,
        [shape(TRACE, 4 * HALF), shape(local, BLOCK, 3 * HALF)],
        [*face_rows(), crosses, parts, lower, upper, inverse, rhs],
        2 * 10**9,
        limit=24 * 1024,
    )
    full, half, state = shape(TRACE, 4 * HALF), shape(TRACE // 2, 4 * HALF), shape(TRACE, 5 * HALF)
    total, part, tracked = call(first_kernel, [full, half, state], [gather(total, [(0, 0, 1)])], 3 * 10**7)
    part = swap(part, (2, 2))
    received = jnp.concatenate([swap(total, (1, 3)), part], axis=0)
    received = gather(received, [(0, 0, 1)])
    part, tracked = call(
        four_kernel,
        [half, state],
        [total, received, tracked],
        10**8,
    )
    pair = gather(part, [(0, 0, 1), (0, 6, 0)]).reshape(2, TRACE, 4 * HALF)
    part, tracked = call(functools.partial(combine_kernel, 3, "whole"), [half, state], [pair, tracked], 3 * 10**7)
    pair = gather(part, [(0, 0, 1), (1, 0, 0)]).reshape(2, TRACE, 4 * HALF)
    crossing = shape(TRACE, 2 * HALF)
    total, tracked = call(functools.partial(combine_kernel, 4, "top"), [crossing, state], [pair, tracked], 3 * 10**7)
    pair = gather(total, [(3, 0, 0)])
    return call(
        functools.partial(last_kernel, 5),
        [shape(local, BLOCK, COLUMNS)],
        [pair, tracked, keep],
        10**8,
        scratch=[pltpu.VMEM((2, HALF, COLUMNS), F32)],
    )


def solution(mesh):
    both = ("stream", "azi")
    return jax.shard_map(
        shards,
        mesh=mesh,
        in_specs=(
            P(both, None, None),
            P(both, None, None),
            P(both, None, None),
            P(both, None, None),
            P(both, None),
            P(both, None),
            P(both),
        ),
        out_specs=P(both, None, None),
        check_vma=False,
    )
```

```python
import functools

import jax
import jax.numpy as jnp
import numpy as np
from jax import lax
from jax.experimental import pallas as pl
from jax.experimental.pallas import tpu as pltpu
from jax.sharding import PartitionSpec as P

TRACE = 80
BLOCK = 320
COLUMNS = 128
PLANE = 16
CUBE = 64
HALF = 128
F32 = jnp.float32
BF16 = jnp.bfloat16
VMEM = pl.BlockSpec(memory_space=pltpu.VMEM)
SMEM = pl.BlockSpec(memory_space=pltpu.SMEM)
HBM = pl.BlockSpec(memory_space=pltpu.HBM)


def split(value):
    high = value.astype(BF16)
    return high, (value - high.astype(F32)).astype(BF16)


def dot(left, right):
    return jnp.dot(left, right, preferred_element_type=F32)


def product(left, right):
    return dot(left[0], right[0]) + (dot(left[0], right[1]) + dot(left[1], right[0]))


def select_rows(onehot, value):
    return dot(onehot, value[0]), dot(onehot, value[1])


def fetch(sources, buffers, sems):
    copies = [pltpu.make_async_copy(a, b, sems.at[i]) for i, (a, b) in enumerate(zip(sources, buffers))]
    for copy in copies:
        copy.start()
    return copies


def wake_kernel(target_hbm, rows_hbm, upwind_hbm, out_ref, crosses_ref, target_ref, rows_ref, upwind_ref, sems):
    for copy in fetch((target_hbm, rows_hbm, upwind_hbm), (target_ref, rows_ref, upwind_ref), sems):
        copy.wait()
    ids = lax.broadcasted_iota(jnp.int32, (out_ref.shape[0], target_ref.shape[1]), 0)
    onehot = jnp.where(ids == target_ref[...], 1.0, 0.0).astype(BF16)
    high, low = split(rows_ref[...])
    out_ref[...] = dot(onehot, high) + dot(onehot, low)
    face = lax.broadcasted_iota(jnp.int32, crosses_ref.shape, 0)
    crosses = jnp.zeros(crosses_ref.shape, F32)
    for at in range(3):
        crosses = jnp.where((face == at) & (upwind_ref[1, at] == 2), 1.0, crosses)
    crosses_ref[...] = crosses


def face_block(ref, element, face):
    return ref[element, :, face * TRACE : (face + 1) * TRACE]


def face_rows():
    trace = np.arange(TRACE)
    field, upper, lower = trace // PLANE, trace // 4 % 4, trace % 4
    take = np.zeros((2, 3 * TRACE, BLOCK), np.float32)
    for odd in range(2):
        side = 3 * odd
        places = (side * 16 + upper * 4 + lower, upper * 16 + side * 4 + lower, upper * 16 + lower * 4 + side)
        for face, place in enumerate(places):
            take[odd, face * TRACE + trace, field * CUBE + place] = 1.0
    return jnp.asarray(take, BF16), jnp.asarray(take.transpose(0, 2, 1), BF16)


WHOLE = 256


def left_parts(value):
    high, low = split(value)
    ends = [part[:, WHOLE:].astype(F32) for part in (high, low, high)]
    return high[:, :WHOLE], low[:, :WHOLE], jnp.concatenate(ends, axis=1).astype(BF16)


def right_parts(value):
    high, low = split(value)
    ends = [part[WHOLE:] for part in (high, high, low)]
    return high[:WHOLE], low[:WHOLE], jnp.concatenate(ends, axis=0)


def long_product(left, right):
    return (dot(left[0], right[0]) + dot(left[2], right[2])) + (dot(left[0], right[1]) + dot(left[1], right[0]))


def last_plane(value):
    return jnp.concatenate(
        [value[at + CUBE - PLANE : at + CUBE] for at in range(0, BLOCK, CUBE)], axis=0
    )


def pack(first, second, third, fourth):
    lead = TRACE
    spare = HALF - lead
    mid = third[:, :HALF]
    return jnp.concatenate(
        [
            first[:, :lead],
            mid[:, :spare],
            first[:, HALF:],
            fourth[:, :lead],
            mid[:, spare:lead],
            jnp.zeros((TRACE, 2 * spare - lead), F32),
            third[:, HALF:],
        ],
        axis=1,
    )


def unpack(value):
    lead = TRACE
    spare = HALF - lead
    zeros = jnp.zeros((TRACE, spare), F32)
    forward = value[:, : 2 * HALF]
    mixed = jnp.concatenate(
        [
            value[:, lead:HALF],
            value[:, 2 * HALF + lead : 2 * HALF + lead + (lead - spare)],
            zeros,
            value[:, 3 * HALF :],
        ],
        axis=1,
    )
    return forward, mixed, value[:, 2 * HALF : 2 * HALF + lead]


def expand(block, take):
    high, low = split(block)
    return dot(high, take) + dot(low, take)


def local_kernel(take_ref, put_ref, crosses_ref, wake_ref, low_ref, up_ref, inv_ref, rhs_ref, total_ref, keep_ref):
    put_even, put_odd = put_ref[0], put_ref[1]
    take_even, take_odd = take_ref[0], take_ref[1]
    ones = jnp.ones((wake_ref.shape[1], COLUMNS), BF16)
    spare = jnp.zeros((3 * TRACE, HALF - TRACE), F32)
    at = [slice(face * TRACE, (face + 1) * TRACE) for face in range(3)]

    def source(element):
        high, low = split(wake_ref[element])
        dims = (((0,), (0,)), ((), ()))
        wake = lax.dot_general(high, ones, dims, preferred_element_type=F32)
        wake += lax.dot_general(low, ones, dims, preferred_element_type=F32)
        return rhs_ref[element] + wake

    def put(onehot, rows):
        return sum(select_rows(onehot, split(rows)))

    crosses = [crosses_ref[face : face + 1, :1] > 0.5 for face in range(3)]

    def kept(values, crossing):
        return [jnp.where(cross == crossing, v, 0.0) for cross, v in zip(crosses, values)]

    def wide(values):
        return jnp.concatenate([jnp.concatenate(values, axis=0), spare], axis=1)

    from_first = put(put_even, wide([face_block(low_ref, 0, face) for face in range(3)]))
    blocks = [face_block(low_ref, 1, face) for face in range(3)]
    from_second = put(put_even, wide(kept(blocks, True)))
    inside = [expand(blocks[face], take_odd[at[face]]) for face in range(3)]
    down = left_parts(put(put_even, jnp.concatenate(kept(inside, False), axis=0)))
    inside = [expand(face_block(up_ref, 1, face), take_even[at[face]]) for face in range(3)]
    up = left_parts(put(put_odd, jnp.concatenate(kept(inside, False), axis=0)))
    leave_second = left_parts(sum(kept(inside, True)))
    leave_first = left_parts(expand(up_ref[0], take_even))

    inverse = left_parts(inv_ref[0])
    later_inverse = left_parts(inv_ref[1])
    first = long_product(inverse, right_parts(jnp.concatenate([-from_first, source(0)], axis=1)))

    side = put_odd[:, :HALF]
    lane = lax.broadcasted_iota(jnp.int32, (BLOCK, HALF), 1)
    high, low = split(inv_ref[1])
    returned = -(dot(high, side) + dot(low, side))
    returned = jnp.where(lane < TRACE, returned, 0.0)
    returned_pair = right_parts(returned)
    keep_ref[1, :, 2 * HALF :] = returned

    inner = long_product(down, right_parts(first))
    earlier = -long_product(inverse, right_parts(long_product(up, returned_pair)))
    keep_ref[0, :, 2 * HALF :] = earlier

    base = jnp.concatenate([-from_second, source(1)], axis=1)
    second = long_product(later_inverse, right_parts(base - inner))
    keep_ref[1, :, : 2 * HALF] = second
    second_pair = right_parts(second)
    back = long_product(leave_second, returned_pair) + long_product(leave_first, right_parts(earlier))
    inner = long_product(up, second_pair)
    first = first - long_product(inverse, right_parts(inner))
    keep_ref[0, :, : 2 * HALF] = first
    mixed = long_product(leave_second, second_pair) + long_product(leave_first, right_parts(first))
    total_ref[...] = pack(last_plane(second), None, mixed, back)


def is_upper(level):
    return (lax.axis_index("stream") >> level) & 1


def merge(run1, run2):
    forward1, mixed1, back1 = run1
    forward2, mixed2, back2 = run2
    lane = lax.broadcasted_iota(jnp.int32, (TRACE, 2 * HALF), 1)
    columns = lane >= HALF
    forward1 = jnp.where(columns | (lane < TRACE), forward1, 0.0)
    forward_pair = split(forward1)
    cross = product(split(mixed2[:, :TRACE]), forward_pair) + jnp.where(columns, mixed2, 0.0)
    forward = product(split(forward2[:, :TRACE]), forward_pair)
    forward = forward + jnp.where(columns, forward2, 0.0)
    back_pair = split(back1)
    mixed = mixed1 + product(back_pair, split(cross))
    back = product(back_pair, split(back2))
    back2 = jnp.concatenate([back2, jnp.zeros((TRACE, HALF - TRACE), F32)], axis=1)
    return (forward, mixed, back), (forward1, cross, back2)


def track(upper, pieces, old):
    forward1, cross, back2 = pieces
    here, back, gain = old
    columns = lax.broadcasted_iota(jnp.int32, (TRACE, 2 * HALF), 1) >= HALF
    through = product(split(here[:, :TRACE]), split(forward1)) + jnp.where(columns, here, 0.0)
    factor = jnp.where(upper, back[:, :TRACE], gain[:, :TRACE])
    added = jnp.where(columns | jnp.logical_not(upper), back, 0.0)
    back = product(split(factor), split(jnp.where(upper, forward1, cross))) + added
    gained = product(split(gain[:, :TRACE]), split(back2))
    return jnp.where(upper, through, here), back, jnp.where(upper, gain, gained)


def state_of(ref):
    return ref[:, : 2 * HALF], ref[:, 2 * HALF : 4 * HALF], ref[:, 4 * HALF :]


def first_kernel(pair_ref, total_ref, half_ref, state_ref):
    upper = is_upper(0) == 1
    total, (forward1, cross, back2) = merge(unpack(pair_ref[0]), unpack(pair_ref[1]))
    total = pack(total[0], None, total[1], total[2])
    total_ref[...] = total
    half_ref[...] = jnp.where(upper, total[TRACE // 2 :], total[: TRACE // 2])
    lane = lax.broadcasted_iota(jnp.int32, (TRACE, 2 * HALF), 1)
    row = lax.broadcasted_iota(jnp.int32, (TRACE, 2 * HALF), 0)
    eye = jnp.where(lane == row, 1.0, 0.0)
    state_ref[:, : 2 * HALF] = jnp.where(upper, forward1, eye)
    state_ref[:, 2 * HALF : 4 * HALF] = jnp.where(upper, 0.0, cross)
    state_ref[:, 4 * HALF :] = jnp.where(upper, eye[:, :HALF], back2)


def four_kernel(own_ref, others_ref, old_ref, half_ref, state_ref):
    odd, late = is_upper(1) == 1, is_upper(2) == 1
    own, near, far = own_ref[...], others_ref[0, :TRACE], others_ref[1, :TRACE]
    middle = jnp.concatenate([others_ref[0, TRACE:], others_ref[1, TRACE:]], axis=0)

    def ordered(swap, one, two):
        return unpack(jnp.where(swap, two, one)), unpack(jnp.where(swap, one, two))

    mine, pieces = merge(*ordered(odd, own, near))
    other, _ = merge(*ordered(odd, middle, far))
    state = track(odd, pieces, state_of(old_ref))
    earlier = [jnp.where(late, b, a) for a, b in zip(mine, other)]
    later = [jnp.where(late, a, b) for a, b in zip(mine, other)]
    total, pieces = merge(earlier, later)
    total = pack(total[0], None, total[1], total[2])
    half_ref[...] = jnp.where(is_upper(0) == 1, total[TRACE // 2 :], total[: TRACE // 2])
    state_ref[...] = jnp.concatenate(track(late, pieces, state), axis=1)


def combine_kernel(level, sends, pair_ref, old_ref, total_ref, state_ref):
    total, pieces = merge(unpack(pair_ref[0]), unpack(pair_ref[1]))
    if sends == "top":
        total = jnp.where(is_upper(level + 1) == 1, total[1], total[0])
    else:
        total = pack(total[0], None, total[1], total[2])
    if sends != "top":
        total = jnp.where(is_upper(0) == 1, total[TRACE // 2 :], total[: TRACE // 2])
    total_ref[...] = total
    state_ref[...] = jnp.concatenate(track(is_upper(level) == 1, pieces, state_of(old_ref)), axis=1)


def last_kernel(level, pair_ref, old_ref, keep_ref, out_ref):
    upper = is_upper(level) == 1
    here, back, gain = state_of(old_ref)
    inflow = pair_ref[0, :, HALF:]
    inflow_pair = split(inflow)
    value = pair_ref[1, :, HALF:] + product(split(pair_ref[1, :, :TRACE]), inflow_pair)
    factor = jnp.where(upper, back[:, :TRACE], gain[:, :TRACE])
    incoming = back[:, HALF:] + product(split(factor), split(jnp.where(upper, inflow, value)))
    through = product(split(here[:, :TRACE]), inflow_pair)
    inflow = here[:, HALF:] + jnp.where(upper, through, 0.0)
    spare = jnp.zeros((HALF - TRACE, COLUMNS), F32)
    ends = split(jnp.concatenate([inflow, spare, incoming, spare], axis=0))
    for element in range(2):
        known = keep_ref[element]
        maps = jnp.concatenate([known[:, :HALF], known[:, 2 * HALF :]], axis=1)
        out_ref[element] = known[:, HALF : 2 * HALF] + product(split(maps), ends)


def call(kernel, shapes, operands, flops, specs=None, scratch=(), limit=8 * 1024):
    moved = 4 * sum(v.size for v in operands) + 4 * sum(s.size for s in shapes)
    single = len(shapes) == 1
    return pl.pallas_call(
        kernel,
        out_shape=shapes[0] if single else shapes,
        in_specs=specs or [VMEM] * len(operands),
        out_specs=VMEM if single else [VMEM] * len(shapes),
        scratch_shapes=list(scratch),
        compiler_params=pltpu.CompilerParams(vmem_limit_bytes=limit * 1024),
        cost_estimate=pl.CostEstimate(flops=flops, bytes_accessed=moved, transcendentals=0),
    )(*operands)


def shape(*dims):
    return jax.ShapeDtypeStruct(dims, F32)


def gather(value, masks):
    count = lax.axis_size("stream")
    masks = [(across * 8 + along) * 2 + core for across, along, core in masks]
    seen, groups = set(), []
    for device in range(count):
        if device in seen:
            continue
        group = {device}
        for mask in masks:
            group |= {member ^ mask for member in group}
        seen |= group
        groups.append(sorted(group))
    return lax.all_gather(value, "stream", axis_index_groups=groups)


def swap(value, along):
    count = lax.axis_size("stream")
    return lax.ppermute(value, "stream", [(k, k ^ (2 * along[k % 2])) for k in range(count)])


def shards(rhs, inverse, lower, upper, upwind, rows, target):
    groups = lax.axis_size("azi")
    local = rhs.shape[0]
    target = target.reshape(1, -1)
    rows, target, upwind = [pltpu.with_memory_space_constraint(v, pltpu.HBM) for v in (rows, target, upwind)]
    partial, crosses = call(
        wake_kernel,
        [shape(groups * local, BLOCK), shape(8, HALF)],
        [target, rows, upwind],
        10**10,
        specs=[HBM, HBM, HBM],
        scratch=[
            pltpu.VMEM(target.shape, jnp.int32),
            pltpu.VMEM(rows.shape, F32),
            pltpu.SMEM(upwind.shape, jnp.int32),
            pltpu.SemaphoreType.DMA((3,)),
        ],
    )
    parts = lax.all_to_all(partial.reshape(groups, local, BLOCK), "azi", 0, 0)
    parts = jnp.swapaxes(parts, 0, 1)
    total, keep = call(
        local_kernel,
        [shape(TRACE, 4 * HALF), shape(local, BLOCK, 3 * HALF)],
        [*face_rows(), crosses, parts, lower, upper, inverse, rhs],
        2 * 10**9,
        limit=24 * 1024,
    )
    full, half, state = shape(TRACE, 4 * HALF), shape(TRACE // 2, 4 * HALF), shape(TRACE, 5 * HALF)
    total, part, tracked = call(first_kernel, [full, half, state], [gather(total, [(0, 0, 1)])], 3 * 10**7)
    part = swap(part, (2, 2))
    received = jnp.concatenate([swap(total, (1, 3)), part], axis=0)
    received = gather(received, [(0, 0, 1)])
    part, tracked = call(
        four_kernel,
        [half, state],
        [total, received, tracked],
        10**8,
    )
    pair = gather(part, [(0, 0, 1), (0, 6, 0)]).reshape(2, TRACE, 4 * HALF)
    part, tracked = call(functools.partial(combine_kernel, 3, "whole"), [half, state], [pair, tracked], 3 * 10**7)
    pair = gather(part, [(0, 0, 1), (1, 0, 0)]).reshape(2, TRACE, 4 * HALF)
    crossing = shape(TRACE, 2 * HALF)
    total, tracked = call(functools.partial(combine_kernel, 4, "top"), [crossing, state], [pair, tracked], 3 * 10**7)
    pair = gather(total, [(3, 0, 0)])
    return call(
        functools.partial(last_kernel, 5),
        [shape(local, BLOCK, COLUMNS)],
        [pair, tracked, keep],
        10**8,
    )


def solution(mesh):
    both = ("stream", "azi")
    return jax.shard_map(
        shards,
        mesh=mesh,
        in_specs=(
            P(both, None, None),
            P(both, None, None),
            P(both, None, None),
            P(both, None, None),
            P(both, None),
            P(both, None),
            P(both),
        ),
        out_specs=P(both, None, None),
        check_vma=False,
    )
```

```python
import functools

import jax
import jax.numpy as jnp
import numpy as np
from jax import lax
from jax.experimental import pallas as pl
from jax.experimental.pallas import tpu as pltpu
from jax.sharding import PartitionSpec as P

TRACE = 80
BLOCK = 320
COLUMNS = 128
PLANE = 16
CUBE = 64
HALF = 128
F32 = jnp.float32
BF16 = jnp.bfloat16
VMEM = pl.BlockSpec(memory_space=pltpu.VMEM)
SMEM = pl.BlockSpec(memory_space=pltpu.SMEM)
HBM = pl.BlockSpec(memory_space=pltpu.HBM)


def split(value):
    high = value.astype(BF16)
    return high, (value - high.astype(F32)).astype(BF16)


def dot(left, right):
    return jnp.dot(left, right, preferred_element_type=F32)


def product(left, right):
    return dot(left[0], right[0]) + (dot(left[0], right[1]) + dot(left[1], right[0]))


def select_rows(onehot, value):
    return dot(onehot, value[0]), dot(onehot, value[1])


def fetch(sources, buffers, sems):
    copies = [pltpu.make_async_copy(a, b, sems.at[i]) for i, (a, b) in enumerate(zip(sources, buffers))]
    for copy in copies:
        copy.start()
    return copies


def wake_kernel(target_hbm, rows_hbm, upwind_hbm, out_ref, crosses_ref, target_ref, rows_ref, upwind_ref, sems):
    for copy in fetch((target_hbm, rows_hbm, upwind_hbm), (target_ref, rows_ref, upwind_ref), sems):
        copy.wait()
    ids = lax.broadcasted_iota(jnp.int32, (out_ref.shape[0], target_ref.shape[1]), 0)
    onehot = jnp.where(ids == target_ref[...], 1.0, 0.0).astype(BF16)
    high, low = split(rows_ref[...])
    out_ref[...] = dot(onehot, high) + dot(onehot, low)
    face = lax.broadcasted_iota(jnp.int32, crosses_ref.shape, 0)
    crosses = jnp.zeros(crosses_ref.shape, F32)
    for at in range(3):
        crosses = jnp.where((face == at) & (upwind_ref[1, at] == 2), 1.0, crosses)
    crosses_ref[...] = crosses


def face_block(ref, element, face):
    return ref[element, :, face * TRACE : (face + 1) * TRACE]


def face_rows():
    trace = np.arange(TRACE)
    field, upper, lower = trace // PLANE, trace // 4 % 4, trace % 4
    take = np.zeros((2, 3 * TRACE, BLOCK), np.float32)
    for odd in range(2):
        side = 3 * odd
        places = (side * 16 + upper * 4 + lower, upper * 16 + side * 4 + lower, upper * 16 + lower * 4 + side)
        for face, place in enumerate(places):
            take[odd, face * TRACE + trace, field * CUBE + place] = 1.0
    return jnp.asarray(take, BF16), jnp.asarray(take.transpose(0, 2, 1), BF16)


WHOLE = 256


def left_parts(value):
    high, low = split(value)
    ends = [part[:, WHOLE:].astype(F32) for part in (high, low, high)]
    return high[:, :WHOLE], low[:, :WHOLE], jnp.concatenate(ends, axis=1).astype(BF16)


def right_parts(value):
    high, low = split(value)
    ends = [part[WHOLE:] for part in (high, high, low)]
    return high[:WHOLE], low[:WHOLE], jnp.concatenate(ends, axis=0)


def long_product(left, right):
    return (dot(left[0], right[0]) + dot(left[2], right[2])) + (dot(left[0], right[1]) + dot(left[1], right[0]))


def last_plane(value):
    return jnp.concatenate(
        [value[at + CUBE - PLANE : at + CUBE] for at in range(0, BLOCK, CUBE)], axis=0
    )


def pack(first, second, third, fourth):
    lead = TRACE
    spare = HALF - lead
    mid = third[:, :HALF]
    return jnp.concatenate(
        [
            first[:, :lead],
            mid[:, :spare],
            first[:, HALF:],
            fourth[:, :lead],
            mid[:, spare:lead],
            jnp.zeros((TRACE, 2 * spare - lead), F32),
            third[:, HALF:],
        ],
        axis=1,
    )


def unpack(value):
    lead = TRACE
    spare = HALF - lead
    zeros = jnp.zeros((TRACE, spare), F32)
    forward = value[:, : 2 * HALF]
    mixed = jnp.concatenate(
        [
            value[:, lead:HALF],
            value[:, 2 * HALF + lead : 2 * HALF + lead + (lead - spare)],
            zeros,
            value[:, 3 * HALF :],
        ],
        axis=1,
    )
    return forward, mixed, value[:, 2 * HALF : 2 * HALF + lead]


def expand(block, take):
    high, low = split(block)
    return dot(high, take) + dot(low, take)


def local_kernel(take_ref, put_ref, crosses_ref, wake_ref, low_ref, up_ref, inv_ref, rhs_ref, total_ref, keep_ref):
    put_even, put_odd = put_ref[0], put_ref[1]
    take_even, take_odd = take_ref[0], take_ref[1]
    ones = jnp.ones((wake_ref.shape[1], COLUMNS), BF16)
    spare = jnp.zeros((3 * TRACE, HALF - TRACE), F32)
    at = [slice(face * TRACE, (face + 1) * TRACE) for face in range(3)]

    def source(element):
        high, low = split(wake_ref[element])
        dims = (((0,), (0,)), ((), ()))
        wake = lax.dot_general(high, ones, dims, preferred_element_type=F32)
        wake += lax.dot_general(low, ones, dims, preferred_element_type=F32)
        return rhs_ref[element] + wake

    def put(onehot, rows):
        return sum(select_rows(onehot, split(rows)))

    crosses = [crosses_ref[face : face + 1, :1] > 0.5 for face in range(3)]

    def kept(values, crossing):
        return [jnp.where(cross == crossing, v, 0.0) for cross, v in zip(crosses, values)]

    def wide(values):
        return jnp.concatenate([jnp.concatenate(values, axis=0), spare], axis=1)

    from_first = put(put_even, wide([face_block(low_ref, 0, face) for face in range(3)]))
    blocks = [face_block(low_ref, 1, face) for face in range(3)]
    from_second = put(put_even, wide(kept(blocks, True)))
    inside = [expand(blocks[face], take_odd[at[face]]) for face in range(3)]
    down = left_parts(put(put_even, jnp.concatenate(kept(inside, False), axis=0)))
    inside = [expand(face_block(up_ref, 1, face), take_even[at[face]]) for face in range(3)]
    up = left_parts(put(put_odd, jnp.concatenate(kept(inside, False), axis=0)))
    leave_second = left_parts(sum(kept(inside, True)))
    leave_first = left_parts(expand(up_ref[0], take_even))

    inverse = left_parts(inv_ref[0])
    later_inverse = left_parts(inv_ref[1])
    first = long_product(inverse, right_parts(jnp.concatenate([-from_first, source(0)], axis=1)))

    side = put_odd[:, :HALF]
    lane = lax.broadcasted_iota(jnp.int32, (BLOCK, HALF), 1)
    high, low = split(inv_ref[1])
    returned = -(dot(high, side) + dot(low, side))
    returned = jnp.where(lane < TRACE, returned, 0.0)
    returned_pair = right_parts(returned)
    keep_ref[1, :, 2 * HALF :] = returned

    inner = long_product(down, right_parts(first))
    earlier = -long_product(inverse, right_parts(long_product(up, returned_pair)))
    keep_ref[0, :, 2 * HALF :] = earlier

    base = jnp.concatenate([-from_second, source(1)], axis=1)
    second = long_product(later_inverse, right_parts(base - inner))
    keep_ref[1, :, : 2 * HALF] = second
    second_pair = right_parts(second)
    back = long_product(leave_second, returned_pair) + long_product(leave_first, right_parts(earlier))
    inner = long_product(up, second_pair)
    first = first - long_product(inverse, right_parts(inner))
    keep_ref[0, :, : 2 * HALF] = first
    mixed = long_product(leave_second, second_pair) + long_product(leave_first, right_parts(first))
    total_ref[...] = pack(last_plane(second), None, mixed, back)


def is_upper(level):
    return (lax.axis_index("stream") >> level) & 1


def merge(run1, run2):
    forward1, mixed1, back1 = run1
    forward2, mixed2, back2 = run2
    lane = lax.broadcasted_iota(jnp.int32, (TRACE, 2 * HALF), 1)
    columns = lane >= HALF
    forward1 = jnp.where(columns | (lane < TRACE), forward1, 0.0)
    forward_pair = split(forward1)
    cross = product(split(mixed2[:, :TRACE]), forward_pair) + jnp.where(columns, mixed2, 0.0)
    forward = product(split(forward2[:, :TRACE]), forward_pair)
    forward = forward + jnp.where(columns, forward2, 0.0)
    back_pair = split(back1)
    mixed = mixed1 + product(back_pair, split(cross))
    back = product(back_pair, split(back2))
    back2 = jnp.concatenate([back2, jnp.zeros((TRACE, HALF - TRACE), F32)], axis=1)
    return (forward, mixed, back), (forward1, cross, back2)


def track(upper, pieces, old):
    forward1, cross, back2 = pieces
    here, back, gain = old
    columns = lax.broadcasted_iota(jnp.int32, (TRACE, 2 * HALF), 1) >= HALF
    through = product(split(here[:, :TRACE]), split(forward1)) + jnp.where(columns, here, 0.0)
    factor = jnp.where(upper, back[:, :TRACE], gain[:, :TRACE])
    added = jnp.where(columns | jnp.logical_not(upper), back, 0.0)
    back = product(split(factor), split(jnp.where(upper, forward1, cross))) + added
    gained = product(split(gain[:, :TRACE]), split(back2))
    return jnp.where(upper, through, here), back, jnp.where(upper, gain, gained)


def state_of(ref):
    return ref[:, : 2 * HALF], ref[:, 2 * HALF : 4 * HALF], ref[:, 4 * HALF :]


def first_kernel(pair_ref, total_ref, half_ref, state_ref):
    upper = is_upper(0) == 1
    total, (forward1, cross, back2) = merge(unpack(pair_ref[0]), unpack(pair_ref[1]))
    total = pack(total[0], None, total[1], total[2])
    total_ref[...] = total
    half_ref[...] = jnp.where(upper, total[TRACE // 2 :], total[: TRACE // 2])
    lane = lax.broadcasted_iota(jnp.int32, (TRACE, 2 * HALF), 1)
    row = lax.broadcasted_iota(jnp.int32, (TRACE, 2 * HALF), 0)
    eye = jnp.where(lane == row, 1.0, 0.0)
    state_ref[:, : 2 * HALF] = jnp.where(upper, forward1, eye)
    state_ref[:, 2 * HALF : 4 * HALF] = jnp.where(upper, 0.0, cross)
    state_ref[:, 4 * HALF :] = jnp.where(upper, eye[:, :HALF], back2)


def four_kernel(own_ref, others_ref, old_ref, half_ref, state_ref):
    odd, late = is_upper(1) == 1, is_upper(2) == 1
    own, near, middle = own_ref[...], others_ref[0, :TRACE], others_ref[1, :TRACE]
    far = jnp.concatenate([others_ref[0, TRACE:], others_ref[1, TRACE:]], axis=0)

    def ordered(swap, one, two):
        return unpack(jnp.where(swap, two, one)), unpack(jnp.where(swap, one, two))

    mine, pieces = merge(*ordered(odd, own, near))
    other, _ = merge(*ordered(odd, middle, far))
    state = track(odd, pieces, state_of(old_ref))
    earlier = [jnp.where(late, b, a) for a, b in zip(mine, other)]
    later = [jnp.where(late, a, b) for a, b in zip(mine, other)]
    total, pieces = merge(earlier, later)
    total = pack(total[0], None, total[1], total[2])
    half_ref[...] = jnp.where(is_upper(0) == 1, total[TRACE // 2 :], total[: TRACE // 2])
    state_ref[...] = jnp.concatenate(track(late, pieces, state), axis=1)


def combine_kernel(level, sends, pair_ref, old_ref, total_ref, state_ref):
    total, pieces = merge(unpack(pair_ref[0]), unpack(pair_ref[1]))
    if sends == "top":
        total = jnp.where(is_upper(level + 1) == 1, total[1], total[0])
    else:
        total = pack(total[0], None, total[1], total[2])
    if sends != "top":
        total = jnp.where(is_upper(0) == 1, total[TRACE // 2 :], total[: TRACE // 2])
    total_ref[...] = total
    state_ref[...] = jnp.concatenate(track(is_upper(level) == 1, pieces, state_of(old_ref)), axis=1)


def last_kernel(level, pair_ref, old_ref, keep_ref, out_ref, ends_ref):
    ends_ref[:, TRACE:] = jnp.zeros((2, HALF - TRACE, COLUMNS), F32)

    @pl.when(is_upper(level) == 1)
    def _():
        inflow = split(pair_ref[0, :, HALF:])
        ends_ref[0, :TRACE] = old_ref[:, HALF : 2 * HALF] + product(split(old_ref[:, :TRACE]), inflow)
        ends_ref[1, :TRACE] = old_ref[:, 3 * HALF : 4 * HALF] + product(split(old_ref[:, 2 * HALF : 2 * HALF + TRACE]), inflow)

    @pl.when(is_upper(level) == 0)
    def _():
        outflow = split(pair_ref[0, :, HALF:])
        value = pair_ref[1, :, HALF:] + product(split(pair_ref[1, :, :TRACE]), outflow)
        gain = split(old_ref[:, 4 * HALF : 4 * HALF + TRACE])
        ends_ref[0, :TRACE] = old_ref[:, HALF : 2 * HALF]
        ends_ref[1, :TRACE] = old_ref[:, 3 * HALF : 4 * HALF] + product(gain, split(value))

    ends = split(ends_ref[...].reshape(2 * HALF, COLUMNS))
    for element in range(2):
        known = keep_ref[element]
        maps = jnp.concatenate([known[:, :HALF], known[:, 2 * HALF :]], axis=1)
        out_ref[element] = known[:, HALF : 2 * HALF] + product(split(maps), ends)


def call(kernel, shapes, operands, flops, specs=None, scratch=(), limit=8 * 1024):
    moved = 4 * sum(v.size for v in operands) + 4 * sum(s.size for s in shapes)
    single = len(shapes) == 1
    return pl.pallas_call(
        kernel,
        out_shape=shapes[0] if single else shapes,
        in_specs=specs or [VMEM] * len(operands),
        out_specs=VMEM if single else [VMEM] * len(shapes),
        scratch_shapes=list(scratch),
        compiler_params=pltpu.CompilerParams(vmem_limit_bytes=limit * 1024),
        cost_estimate=pl.CostEstimate(flops=flops, bytes_accessed=moved, transcendentals=0),
    )(*operands)


def shape(*dims):
    return jax.ShapeDtypeStruct(dims, F32)


def gather(value, masks):
    count = lax.axis_size("stream")
    masks = [(across * 8 + along) * 2 + core for across, along, core in masks]
    seen, groups = set(), []
    for device in range(count):
        if device in seen:
            continue
        group = {device}
        for mask in masks:
            group |= {member ^ mask for member in group}
        seen |= group
        groups.append(sorted(group))
    return lax.all_gather(value, "stream", axis_index_groups=groups)


def swap(value, along):
    count = lax.axis_size("stream")
    return lax.ppermute(value, "stream", [(k, k ^ (2 * along[k % 2])) for k in range(count)])


def shards(rhs, inverse, lower, upper, upwind, rows, target):
    groups = lax.axis_size("azi")
    local = rhs.shape[0]
    target = target.reshape(1, -1)
    rows, target, upwind = [pltpu.with_memory_space_constraint(v, pltpu.HBM) for v in (rows, target, upwind)]
    partial, crosses = call(
        wake_kernel,
        [shape(groups * local, BLOCK), shape(8, HALF)],
        [target, rows, upwind],
        10**10,
        specs=[HBM, HBM, HBM],
        scratch=[
            pltpu.VMEM(target.shape, jnp.int32),
            pltpu.VMEM(rows.shape, F32),
            pltpu.SMEM(upwind.shape, jnp.int32),
            pltpu.SemaphoreType.DMA((3,)),
        ],
    )
    parts = lax.all_to_all(partial.reshape(groups, local, BLOCK), "azi", 0, 0)
    parts = jnp.swapaxes(parts, 0, 1)
    total, keep = call(
        local_kernel,
        [shape(TRACE, 4 * HALF), shape(local, BLOCK, 3 * HALF)],
        [*face_rows(), crosses, parts, lower, upper, inverse, rhs],
        2 * 10**9,
        limit=24 * 1024,
    )
    full, half, state = shape(TRACE, 4 * HALF), shape(TRACE // 2, 4 * HALF), shape(TRACE, 5 * HALF)
    total, part, tracked = call(first_kernel, [full, half, state], [gather(total, [(0, 0, 1)])], 3 * 10**7)
    part = swap(part, (3, 3))
    received = jnp.concatenate([swap(total, (1, 2)), part], axis=0)
    received = gather(received, [(0, 0, 1)])
    part, tracked = call(
        four_kernel,
        [half, state],
        [total, received, tracked],
        10**8,
    )
    pair = gather(part, [(0, 0, 1), (0, 6, 0)]).reshape(2, TRACE, 4 * HALF)
    part, tracked = call(functools.partial(combine_kernel, 3, "whole"), [half, state], [pair, tracked], 3 * 10**7)
    pair = gather(part, [(0, 0, 1), (1, 0, 0)]).reshape(2, TRACE, 4 * HALF)
    crossing = shape(TRACE, 2 * HALF)
    total, tracked = call(functools.partial(combine_kernel, 4, "top"), [crossing, state], [pair, tracked], 3 * 10**7)
    pair = gather(total, [(3, 0, 0)])
    return call(
        functools.partial(last_kernel, 5),
        [shape(local, BLOCK, COLUMNS)],
        [pair, tracked, keep],
        10**8,
        scratch=[pltpu.VMEM((2, HALF, COLUMNS), F32)],
    )


def solution(mesh):
    both = ("stream", "azi")
    return jax.shard_map(
        shards,
        mesh=mesh,
        in_specs=(
            P(both, None, None),
            P(both, None, None),
            P(both, None, None),
            P(both, None, None),
            P(both, None),
            P(both, None),
            P(both),
        ),
        out_specs=P(both, None, None),
        check_vma=False,
    )
```
